256 devices in a mesh: pair: 32 (over z, x_hi, core), edge: 8 (over x_lo, y).
Axes of the slice: x: 4 (x_hi: 2, x_lo: 2; x = x_hi * 2 + x_lo), y: 4, z: 8, core: 2. Of those that a mesh axis runs over, the one named last changes fastest.
Arguments:
- left_block: float32 [32768, 400], P(('pair', 'edge')), may hold values from -0.9 to 0.9
- left_state: float32 [32768], P(('pair', 'edge')), may hold values from 0.05 to 0.5
- right_block: float32 [32768, 400], P(('pair', 'edge')), may hold values from -0.9 to 0.9
- right_state: float32 [32768], P(('pair', 'edge')), may hold values from 0.05 to 0.5
- relations: float32 [256, 400], replicated, may hold values from -4 to 4
- relation_state: float32 [256, 400], replicated, may hold values from 0.02 to 0.2
- source_ids: int32 [2, 128000], P(None, ('pair', 'edge')), may hold values from 0 to 1023
- relation_ids: int32 [2, 128000], P(None, ('pair', 'edge')), may hold values from 0 to 255
- target_ids: int32 [2, 128000], P(None, ('pair', 'edge')), may hold values from 0 to 1023
- sample_ids: int32 [2, 32000], P(None, 'pair'), may hold values from 0 to 1023
- bucket_counts: int32 [2, 32], P(None, 'pair'), may hold values from 250 to 4000, as said below
Outputs:
- left_out: float32 [32768, 400], P(('pair', 'edge'))
- left_state_out: float32 [32768], P(('pair', 'edge'))
- right_out: float32 [32768, 400], P(('pair', 'edge'))
- right_state_out: float32 [32768], P(('pair', 'edge'))
- relations_out: float32 [256, 400], replicated
- relation_state_out: float32 [256, 400], replicated
The draws below stay inside these ranges and needn't reach their ends.
Inputs may be any that keep to these rules, and one draw needn't show every extreme that they name: `bucket_counts`: in every round at least one bucket has all of its slots live.
All inputs are finite; a program needn't handle non-finite values.
Results may differ from the reference program's by a relative error of at most 0.013.
Values may be sent and summed in bfloat16 or wider, within the bound.
A program may use at most 64 MiB of HBM per device.

```python
import math
import jax
import jax.numpy as jnp
from jax import lax

D = 400
ROWS = 1024
NREL = 256
E_DEV = 500
NEG = 1000
ROUNDS = 2
ALL_ROWS = 32768
EDGES = 128000
SAMPLES = 32000
N_PAIR = 32
N_EDGE = 8


def draw_bucket_counts(key, part):
    key = jax.random.fold_in(key, 11)
    first_key, second_key = jax.random.split(key)
    largest = N_EDGE * E_DEV
    counts = jax.random.randint(first_key, (ROUNDS, N_PAIR), E_DEV // 2, largest + 1)
    chosen = jax.random.randint(second_key, (ROUNDS, 1), 0, N_PAIR)
    filled = jnp.arange(N_PAIR)[None, :] == chosen
    return jnp.where(filled, largest, counts).astype(jnp.int32)


def draw_relation_ids(key, part):
    key = jax.random.fold_in(key, 23)
    pick_key, spread_key = jax.random.split(key)
    owner = jnp.arange(EDGES, dtype=jnp.int32) // E_DEV % NREL
    owner = jnp.broadcast_to(owner[None, :], (ROUNDS, EDGES))
    spread = jax.random.randint(spread_key, (ROUNDS, EDGES), 0, NREL)
    local = jax.random.randint(pick_key, (ROUNDS, EDGES), 0, 2) == 1
    return jnp.where(local, owner, spread).astype(jnp.int32)


def set_ends(result, key, least, high):
    place = [jax.random.randint(jax.random.fold_in(key, axis), (), 0, length) for axis, length in enumerate(result.shape)]
    main_axis = result.shape.index(max(result.shape))
    neighbour = place[:main_axis] + [(place[main_axis] + 1) % result.shape[main_axis]] + place[main_axis + 1:]
    return result.at[tuple(place)].set(least).at[tuple(neighbour)].set(high)


def levels(stream_key, dims, pieces, least, high):
    def one(dim, shards_of):
        steps = jax.random.uniform(jax.random.fold_in(jax.random.fold_in(stream_key, 6), dim), (shards_of,), jnp.float32, least / len(pieces), high / len(pieces))
        return jnp.repeat(jnp.exp(steps), dims[dim] // shards_of).reshape((-1,) + (1,) * (len(dims) - dim - 1))

    factor_of = one(*pieces[0])
    for cut in pieces[1:]:
        factor_of = factor_of * one(*cut)
    return factor_of


def noise(stream_key, dims, deviation, reach, cuts=(), kind=jnp.bfloat16):
    result = deviation * jax.random.normal(stream_key, dims, jnp.float32)
    if cuts:
        result = result * levels(stream_key, dims, cuts, -0.22, 0.18)
    return jnp.clip(result, -reach, reach).astype(kind)


def setup_inputs(seed: int = 0) -> dict:
    arg_keys = jax.random.split(jax.random.key(seed), 12)
    return {
        "left_block": noise(arg_keys[0], (ALL_ROWS, D), 0.15, 0.9, ((0, 256),), jnp.float32),
        "left_state": jnp.clip(jnp.exp(math.log(0.5) - 2.3025851 * jax.random.uniform(arg_keys[1], (ALL_ROWS,), jnp.float32) ** levels(arg_keys[1], (ALL_ROWS,), ((0, 256),), -0.2, 0.2)), 0.05, 0.5),
        "right_block": noise(arg_keys[2], (ALL_ROWS, D), 0.15, 0.9, ((0, 256),), jnp.float32),
        "right_state": jnp.clip(jnp.exp(math.log(0.5) - 2.3025851 * jax.random.uniform(arg_keys[3], (ALL_ROWS,), jnp.float32) ** levels(arg_keys[3], (ALL_ROWS,), ((0, 256),), -0.2, 0.2)), 0.05, 0.5),
        "relations": noise(arg_keys[4], (NREL, D), 1.0, 4.0, (), jnp.float32),
        "relation_state": jnp.clip(jnp.exp(jax.random.uniform(arg_keys[5], (NREL, D), jnp.float32, math.log(0.02), math.log(0.2))), 0.02, 0.2),
        "source_ids": set_ends(jax.random.randint(arg_keys[6], (ROUNDS, EDGES), 0, ROWS), jax.random.fold_in(arg_keys[6], 1), 0, ROWS - 1).astype(jnp.int32),
        "relation_ids": draw_relation_ids(jax.random.fold_in(arg_keys[11], 71), 0),
        "target_ids": set_ends(jax.random.randint(arg_keys[8], (ROUNDS, EDGES), 0, ROWS), jax.random.fold_in(arg_keys[8], 1), 0, ROWS - 1).astype(jnp.int32),
        "sample_ids": set_ends(jax.random.randint(arg_keys[9], (ROUNDS, SAMPLES), 0, ROWS), jax.random.fold_in(arg_keys[9], 1), 0, ROWS - 1).astype(jnp.int32),
        "bucket_counts": draw_bucket_counts(jax.random.fold_in(arg_keys[11], 71), 0),
    }


entity_rate = 0.3
relation_rate = 0.3

def complex_product(left_value, right_value):
    middle = left_value.shape[-1] // 2
    left_real, left_imag = (left_value[..., :middle], left_value[..., middle:])
    right_real, right_imag = (right_value[..., :middle], right_value[..., middle:])
    return jnp.concatenate([left_real * right_real - left_imag * right_imag, left_real * right_imag + left_imag * right_real], axis=-1)

def conjugate(value):
    middle = value.shape[-1] // 2
    return jnp.concatenate([value[..., :middle], -value[..., middle:]], axis=-1)

def bucket_terms(left_block, right_block, relations, source_ids, relation_ids, target_ids, sample_ids, active):
    row_count = left_block.shape[0]
    left_low = left_block.astype(jnp.bfloat16)
    right_low = right_block.astype(jnp.bfloat16)
    source = jnp.take(left_low, source_ids, axis=0).astype(jnp.float32)
    target = jnp.take(right_low, target_ids, axis=0).astype(jnp.float32)
    operator = jnp.take(relations, relation_ids, axis=0)
    query_low = complex_product(source, operator).astype(jnp.bfloat16)
    query = query_low.astype(jnp.float32)
    sampled = jnp.take(right_low, sample_ids, axis=0)
    positive = lax.optimization_barrier(jnp.sum(query * target, axis=-1))
    scores = lax.dot_general(query_low, sampled, (((1,), (1,)), ((), ())), preferred_element_type=jnp.float32)
    weight_pos = -active * jax.nn.sigmoid(-positive)
    weight_neg = (jax.nn.sigmoid(scores) * (active / sample_ids.shape[0])[:, None]).astype(jnp.bfloat16)
    grad_query = jnp.dot(weight_neg, sampled, preferred_element_type=jnp.float32) + weight_pos[:, None] * target
    grad_sampled = lax.dot_general(weight_neg, query_low, (((0,), (0,)), ((), ())), preferred_element_type=jnp.float32)
    grad_source = complex_product(grad_query, conjugate(operator))
    grad_operator = complex_product(grad_query, conjugate(source))
    left_grad = jax.ops.segment_sum(grad_source, source_ids, row_count)
    right_grad = jax.ops.segment_sum(weight_pos[:, None] * query, target_ids, row_count)
    right_grad = right_grad + jax.ops.segment_sum(grad_sampled, sample_ids, row_count)
    relation_grad = jax.ops.segment_sum(grad_operator, relation_ids, relations.shape[0])
    return (left_grad, right_grad, relation_grad)

def row_update(block, state, grad):
    new_state = state + lax.optimization_barrier(jnp.mean(grad * grad, axis=-1))
    return (block - entity_rate * grad / jnp.sqrt(new_state)[..., None], new_state)

def reference(left_block, left_state, right_block, right_state, relations, relation_state, source_ids, relation_ids, target_ids, sample_ids, bucket_counts):
    left = left_block.reshape(N_PAIR, ROWS, D)
    left_sums = left_state.reshape(N_PAIR, ROWS)
    right = right_block.reshape(N_PAIR, ROWS, D)
    right_sums = right_state.reshape(N_PAIR, ROWS)
    relation_total = jnp.zeros((NREL, D), jnp.float32)
    slot_base = jnp.arange(N_EDGE * E_DEV, dtype=jnp.int32).reshape(N_EDGE, E_DEV)
    for round_index in range(ROUNDS):

        def train_group(inputs):
            group_left, group_right, group_src, group_rel, group_tgt, group_samples, count = inputs

            def one_member(member_inputs):
                member_src, member_rel, member_tgt, member_slots = member_inputs
                active = (member_slots < count).astype(jnp.float32)
                left_grad, right_grad, relation_grad = bucket_terms(group_left, group_right, relations, member_src, member_rel, member_tgt, group_samples, active)
                return (left_grad.astype(jnp.bfloat16), right_grad.astype(jnp.bfloat16), relation_grad)
            left_parts, right_parts, relation_parts = lax.map(one_member, (group_src, group_rel, group_tgt, slot_base))
            left_parts, right_parts = lax.optimization_barrier((left_parts, right_parts))
            return (lax.optimization_barrier(jnp.sum(left_parts.astype(jnp.float32), 0)), lax.optimization_barrier(jnp.sum(right_parts.astype(jnp.float32), 0)), lax.optimization_barrier(jnp.sum(relation_parts, 0)))
        group_inputs = (left, right, source_ids[round_index].reshape(N_PAIR, N_EDGE, E_DEV), relation_ids[round_index].reshape(N_PAIR, N_EDGE, E_DEV), target_ids[round_index].reshape(N_PAIR, N_EDGE, E_DEV), sample_ids[round_index].reshape(N_PAIR, NEG), bucket_counts[round_index])
        left_sum, right_sum, relation_sum = lax.map(train_group, group_inputs)
        left, left_sums = row_update(left, left_sums, left_sum)
        right, right_sums = row_update(right, right_sums, right_sum)
        relation_total = relation_total + lax.optimization_barrier(jnp.sum(relation_sum, 0))
        if round_index + 1 < ROUNDS:
            left = jnp.roll(left, 1, axis=0)
            left_sums = jnp.roll(left_sums, 1, axis=0)
            right = jnp.roll(right, -1, axis=0)
            right_sums = jnp.roll(right_sums, -1, axis=0)
    new_relation_state = relation_state + relation_total * relation_total
    new_relations = relations - relation_rate * relation_total / jnp.sqrt(new_relation_state)
    return (left.reshape(ALL_ROWS, D), left_sums.reshape(ALL_ROWS), right.reshape(ALL_ROWS, D), right_sums.reshape(ALL_ROWS), new_relations, new_relation_state)
```

```python
import functools

import jax
import jax.numpy as jnp
from jax import lax
from jax.experimental import pallas as pl
from jax.experimental.pallas import tpu as pltpu
from jax.sharding import PartitionSpec as P

ENTITY_RATE = 0.3
RELATION_RATE = 0.3
D, H = 400, 200
SHARE = 128
MEMBERS = 8
GROUPS = 32
ROWS = SHARE * MEMBERS
NREL = 256
SLOTS = 500
LANES = 512
NEG = 1000
CHUNK = 256
MESH = pl.DeviceIdType.MESH
VMEM = pl.BlockSpec(memory_space=pltpu.VMEM)
SMEM = pl.BlockSpec(memory_space=pltpu.SMEM)
f32, bf16, i32 = jnp.float32, jnp.bfloat16, jnp.int32


def nt(a, b):
    return lax.dot_general(a, b, (((1,), (1,)), ((), ())), preferred_element_type=f32)


def nn(a, b):
    return jnp.dot(a, b, preferred_element_type=f32)


def flag(condition):
    return jnp.where(condition, 1.0, 0.0).astype(bf16)


def remote(src, dst, send, recv, pair, edge):
    return pltpu.make_async_remote_copy(
        src_ref=src, dst_ref=dst, send_sem=send, recv_sem=recv,
        device_id=(pair, edge), device_id_type=MESH,
    )


def greet(devices):
    barrier = pltpu.get_barrier_semaphore()
    for device in devices:
        pl.semaphore_signal(barrier, inc=1, device_id=device, device_id_type=MESH)
    pl.semaphore_wait(barrier, len(devices))


def members(pair, edge):
    return [(pair, lax.rem(edge + d, MEMBERS)) for d in range(1, MEMBERS)]


def gather_kernel(right, source, relation, target, rows, ids, wide, low, send, recv):
    pair, edge = lax.axis_index("pair"), lax.axis_index("edge")
    peers = members(pair, edge)
    wide[...] = jnp.full_like(wide, -1.0)
    for r in range(2):
        s, k, t = (x[r : r + 1, :] for x in (source, relation, target))
        for row, value in enumerate((s >> 7, (s & 127) + 1, k, t >> 7, t & 127)):
            wide[8 * r + row : 8 * r + row + 1, 0:SLOTS] = value.astype(f32)
    ids[edge] = wide[...].astype(bf16)
    rows[edge] = right[...].astype(bf16)
    greet(peers)
    copies = []
    for d, peer in enumerate(peers):
        for j, ref in enumerate((ids, rows)):
            copy = remote(ref.at[edge], ref.at[edge], send.at[j, d], recv.at[j, d], *peer)
            copy.start()
            copies.append(copy)
    for copy in copies:
        copy.wait()


def gather(right, source, relation, target):
    return pl.pallas_call(
        gather_kernel,
        out_shape=(
            jax.ShapeDtypeStruct((MEMBERS, D, SHARE), bf16),
            jax.ShapeDtypeStruct((MEMBERS, 16, LANES), bf16),
        ),
        in_specs=[VMEM] * 4,
        out_specs=(VMEM, VMEM),
        scratch_shapes=[
            pltpu.VMEM((16, LANES), f32),
            pltpu.VMEM((16, LANES), bf16),
            pltpu.SemaphoreType.DMA((2, MEMBERS - 1)),
            pltpu.SemaphoreType.DMA((2, MEMBERS - 1)),
        ],
        compiler_params=pltpu.CompilerParams(collective_id=1, has_side_effects=True),
        name="gather_right",
    )(right, source, relation, target)


def train_kernel(
    r, rows, ids, samples, counts, left, left_state, relations, relation_in,
    right_grad, left_out, left_state_out, relation_out,
    table, table_t, rank, often, both, right_sum, left_sum,
):
    edge = lax.axis_index("edge")
    left_low = left[...].astype(bf16)
    high = relations[...].astype(bf16)
    both[:, 0:NREL] = high
    both[:, NREL:] = (relations[...] - high.astype(f32)).astype(bf16)
    for m in range(MEMBERS):
        table_t[:, m * SHARE : (m + 1) * SHARE] = rows[m]
        table[m * SHARE : (m + 1) * SHARE, :] = rows[m].T
    picked = flag(lax.broadcasted_iota(i32, (ROWS, NEG), 0) == samples[r : r + 1, :])
    often[...] = nn(picked, jnp.full((NEG, SHARE), 1.0, bf16)) * (1.0 / NEG)

    owner = jnp.concatenate(
        [ids[m].astype(f32)[8 * r : 8 * r + 1, :] for m in range(MEMBERS)], axis=0
    )
    lane = lax.broadcasted_iota(i32, (MEMBERS, LANES), 1)
    slot = lax.broadcasted_iota(i32, (MEMBERS, LANES), 0) * SLOTS + lane
    mine = (owner == edge.astype(f32)) & (slot < counts[r, 0])
    mark = flag(mine)
    before = flag(
        lax.broadcasted_iota(i32, (LANES, LANES), 0) < lax.broadcasted_iota(i32, (LANES, LANES), 1)
    )
    found = jnp.sum(jnp.where(mine, 1.0, 0.0), axis=1, keepdims=True)
    starts = [jnp.zeros((1, 1), f32)]
    for m in range(MEMBERS):
        starts.append(starts[-1] + found[m : m + 1, :])
    place = nn(mark, before) + jnp.concatenate(starts[:MEMBERS], axis=0)
    rank[...] = jnp.where(mine, place, -1.0).astype(i32)
    total = jnp.sum(found).astype(i32)

    right_sum[...] = jnp.zeros_like(right_sum)
    left_sum[...] = jnp.zeros_like(left_sum)
    relation_out[...] = relation_in[...]

    def chunk(c, carry):
        want = lax.broadcasted_iota(i32, (CHUNK, LANES), 0) + c * CHUNK
        found = jnp.zeros((16, CHUNK), f32)
        for m in range(MEMBERS):
            found = found + nt(ids[m], flag(rank[m : m + 1, :] == want))
        found = found[8 * r : 8 * r + 8, :].astype(i32)
        s, k = found[1:2, :] - 1, found[2:3, :]
        t = found[3:4, :] * SHARE + found[4:5, :]
        source_hot = flag(lax.broadcasted_iota(i32, (SHARE, CHUNK), 0) == s)
        relation_hot = flag(lax.broadcasted_iota(i32, (NREL, CHUNK), 0) == k)
        source = nn(left_low, source_hot)
        operator = nn(both[...], jnp.concatenate([relation_hot, relation_hot], axis=0))
        sr, si, kr, ki = source[:H], source[H:], operator[:H], operator[H:]
        query = jnp.concatenate([sr * kr - si * ki, sr * ki + si * kr], axis=0).astype(bf16)
        scores = nn(table[...], query)
        chance = 0.5 * jnp.tanh(0.5 * scores) + 0.5
        hit = lax.broadcasted_iota(i32, (ROWS, CHUNK), 0) == t
        spread = jnp.concatenate([often[...]] * (CHUNK // SHARE), axis=1)
        weight = (spread * chance - jnp.where(hit, 1.0 - chance, 0.0)).astype(bf16)
        grad = nn(table_t[...], weight)
        right_sum[...] += nt(query, weight)
        gr, gi = grad[:H], grad[H:]
        grad_source = jnp.concatenate([gr * kr + gi * ki, gi * kr - gr * ki], axis=0)
        grad_operator = jnp.concatenate([gr * sr + gi * si, gi * sr - gr * si], axis=0)
        left_sum[...] += nt(grad_source.astype(bf16), source_hot)
        relation_out[...] += nt(grad_operator.astype(bf16), relation_hot)
        return carry

    lax.fori_loop(0, (total + (CHUNK - 1)) // CHUNK, chunk, 0)
    for m in range(MEMBERS):
        right_grad[m] = right_sum[:, m * SHARE : (m + 1) * SHARE].astype(bf16)
    block, state = row_update(left[...], left_state[...], left_sum[...])
    left_out[...] = block
    left_state_out[...] = state


def row_update(block, state, grad):
    state = state + jnp.sum(grad * grad, axis=0, keepdims=True) * (1.0 / D)
    return block - ENTITY_RATE * grad / jnp.sqrt(state), state


def train(r, rows, ids, samples, counts, left, left_state, relations, relation_in):
    return pl.pallas_call(
        functools.partial(train_kernel, r),
        out_shape=(
            jax.ShapeDtypeStruct((MEMBERS, D, SHARE), bf16),
            jax.ShapeDtypeStruct((D, SHARE), f32),
            jax.ShapeDtypeStruct((1, SHARE), f32),
            jax.ShapeDtypeStruct((D, NREL), f32),
        ),
        in_specs=[VMEM, VMEM, VMEM, SMEM, VMEM, VMEM, VMEM, VMEM],
        out_specs=(VMEM,) * 4,
        scratch_shapes=[
            pltpu.VMEM((ROWS, D), bf16),
            pltpu.VMEM((D, ROWS), bf16),
            pltpu.VMEM((MEMBERS, LANES), i32),
            pltpu.VMEM((ROWS, SHARE), f32),
            pltpu.VMEM((D, 2 * NREL), bf16),
            pltpu.VMEM((D, ROWS), f32),
            pltpu.VMEM((D, SHARE), f32),
        ],
        compiler_params=pltpu.CompilerParams(vmem_limit_bytes=48 * 2**20),
        name="train_round",
    )(rows, ids, samples, counts, left, left_state, relations, relation_in)


def send_parts(parts, landing, send, recv, edge, peers):
    copies = []
    for d, peer in enumerate(peers):
        copy = remote(parts.at[peer[1]], landing.at[edge], send.at[d], recv.at[d], *peer)
        copy.start()
        copies.append(copy)
    return copies


def total_of(parts, landing, copies, edge):
    total = parts[edge].astype(f32)
    for d, copy in enumerate(copies):
        copy.wait_recv()
        total = total + landing[lax.rem(edge + (MEMBERS - 1 - d), MEMBERS)].astype(f32)
    return total


def exchange_kernel(
    parts, right, right_state, left, left_state,
    rows, right_out, right_state_out, left_out, left_state_out,
    landing, out_left, out_right, in_left, in_right, out_states, in_states,
    part_send, part_recv, row_send, row_recv, move_send, move_recv,
):
    pair, edge = lax.axis_index("pair"), lax.axis_index("edge")
    peers = members(pair, edge)
    ahead = (lax.rem(pair + 1, GROUPS), edge)
    behind = (lax.rem(pair + GROUPS - 1, GROUPS), edge)
    out_left[...] = left[...].astype(bf16)
    out_states[0] = jnp.broadcast_to(left_state[...], (8, SHARE))
    greet(peers + [ahead, behind])
    copies = send_parts(parts, landing, part_send, part_recv, edge, peers)
    moves = [
        remote(out_left, in_left, move_send.at[0], move_recv.at[0], *ahead),
        remote(out_states.at[0], in_states.at[0], move_send.at[1], move_recv.at[1], *ahead),
        remote(out_right, in_right, move_send.at[2], move_recv.at[2], *behind),
        remote(out_states.at[1], in_states.at[1], move_send.at[3], move_recv.at[3], *behind),
    ]
    moves[0].start()
    moves[1].start()
    grad = total_of(parts, landing, copies, edge)
    block, state = row_update(right[...], right_state[...], grad)
    out_right[...] = block.astype(bf16)
    out_states[1] = jnp.broadcast_to(state, (8, SHARE))
    moves[2].start()
    moves[3].start()
    moves[2].wait_recv()
    rows[edge] = in_right[...]
    gathers = []
    for d, peer in enumerate(peers):
        copy = remote(in_right, rows.at[edge], row_send.at[d], row_recv.at[d], *peer)
        copy.start()
        gathers.append(copy)
    right_out[...] = in_right[...].astype(f32)
    moves[3].wait_recv()
    right_state_out[...] = in_states[1, 0:1, :]
    moves[0].wait_recv()
    left_out[...] = in_left[...].astype(f32)
    moves[1].wait_recv()
    left_state_out[...] = in_states[0, 0:1, :]
    for copy in gathers:
        copy.wait_recv()
    for copy in copies + moves + gathers:
        copy.wait_send()


def exchange(parts, right, right_state, left, left_state):
    block = jax.ShapeDtypeStruct((D, SHARE), f32)
    row = jax.ShapeDtypeStruct((1, SHARE), f32)
    low = pltpu.VMEM((D, SHARE), bf16)
    dma = pltpu.SemaphoreType.DMA
    return pl.pallas_call(
        exchange_kernel,
        out_shape=(jax.ShapeDtypeStruct((MEMBERS, D, SHARE), bf16), block, row, block, row),
        in_specs=[VMEM] * 5,
        out_specs=(VMEM,) * 5,
        scratch_shapes=[
            pltpu.VMEM((MEMBERS, D, SHARE), bf16),
            low, low, low, low,
            pltpu.VMEM((2, 8, SHARE), f32),
            pltpu.VMEM((2, 8, SHARE), f32),
            dma((MEMBERS - 1,)), dma((MEMBERS - 1,)),
            dma((MEMBERS - 1,)), dma((MEMBERS - 1,)),
            dma((4,)), dma((4,)),
        ],
        compiler_params=pltpu.CompilerParams(
            collective_id=2, has_side_effects=True, vmem_limit_bytes=32 * 2**20
        ),
        name="exchange_rows",
    )(parts, right, right_state, left, left_state)


def finish_kernel(
    parts, right, right_state, relation_grad, relations, relation_state,
    right_out, right_state_out, relations_out, relation_state_out,
    landing, share, share_in, tiles, tiles_in, quad, whole,
    part_send, part_recv, s1, r1, s2, r2, s3, r3, s4, r4, s5, r5,
):
    pair, edge = lax.axis_index("pair"), lax.axis_index("edge")
    z, q = pair // 4, lax.rem(pair, 4)
    peers = members(pair, edge)
    depth = [(lax.rem(z + d, 8) * 4 + q, edge) for d in range(1, 8)]
    flat = [(z * 4 + lax.rem(q + d, 4), edge) for d in range(1, 4)]
    share[...] = jnp.zeros_like(share)
    grads = relation_grad[...].astype(bf16)
    stacked = jnp.concatenate(
        [grads[:, 0:SHARE], grads[:, SHARE:], jnp.zeros((224, SHARE), bf16)], axis=0
    )
    for m in range(MEMBERS):
        share[m] = stacked[m * SHARE : (m + 1) * SHARE, :]
    greet(peers + depth + flat)
    first = send_parts(share, share_in, s1, r1, edge, peers)
    copies = send_parts(parts, landing, part_send, part_recv, edge, peers)
    done = first + copies
    sums = total_of(share, share_in, first, edge).astype(bf16)
    for k in range(8):
        tiles[k] = sums[16 * k : 16 * k + 16, :]
    second = []
    for d, peer in enumerate(depth):
        copy = remote(
            tiles.at[lax.rem(z + d + 1, 8)], tiles_in.at[z], s2.at[d], r2.at[d], *peer
        )
        copy.start()
        second.append(copy)
    total = tiles[z].astype(f32)
    for d, copy in enumerate(second):
        copy.wait_recv()
        total = total + tiles_in[lax.rem(z + 7 - d, 8)].astype(f32)
    quad[q] = total
    third = []
    for d, peer in enumerate(flat):
        copy = remote(quad.at[q], quad.at[q], s3.at[d], r3.at[d], *peer)
        copy.start()
        third.append(copy)
    for copy in third:
        copy.wait_recv()
    rows = pl.ds(pl.multiple_of(z * 16, 16), 16)
    whole[edge, rows, :] = (quad[0] + quad[1] + quad[2] + quad[3]).astype(bf16)
    fourth = []
    for d, peer in enumerate(depth):
        here = whole.at[edge, rows, :]
        copy = remote(here, here, s4.at[d], r4.at[d], *peer)
        copy.start()
        fourth.append(copy)

    grad = total_of(parts, landing, copies, edge)
    block, state = row_update(right[...], right_state[...], grad)
    right_out[...] = block
    right_state_out[...] = state

    for copy in fourth:
        copy.wait_recv()
    fifth = []
    for d, peer in enumerate(peers):
        copy = remote(whole.at[edge], whole.at[edge], s5.at[d], r5.at[d], *peer)
        copy.start()
        fifth.append(copy)
    for copy in fifth:
        copy.wait_recv()
    gathered = whole[...].reshape(MEMBERS * SHARE, SHARE)
    grad = jnp.concatenate([gathered[0:D], gathered[D : 2 * D]], axis=1).astype(f32)
    state = relation_state[...] + grad * grad
    relation_state_out[...] = state
    relations_out[...] = relations[...] - RELATION_RATE * grad / jnp.sqrt(state)
    for copy in done + second + third + fourth + fifth:
        copy.wait_send()


def finish(parts, right, right_state, relation_grad, relations, relation_state):
    dma = pltpu.SemaphoreType.DMA
    table = jax.ShapeDtypeStruct((D, NREL), f32)
    return pl.pallas_call(
        finish_kernel,
        out_shape=(
            jax.ShapeDtypeStruct((D, SHARE), f32), jax.ShapeDtypeStruct((1, SHARE), f32),
            table, table,
        ),
        in_specs=[VMEM] * 6,
        out_specs=(VMEM,) * 4,
        scratch_shapes=[
            pltpu.VMEM((MEMBERS, D, SHARE), bf16),
            pltpu.VMEM((MEMBERS, SHARE, SHARE), bf16),
            pltpu.VMEM((MEMBERS, SHARE, SHARE), bf16),
            pltpu.VMEM((8, 16, SHARE), bf16),
            pltpu.VMEM((8, 16, SHARE), bf16),
            pltpu.VMEM((4, 16, SHARE), f32),
            pltpu.VMEM((MEMBERS, SHARE, SHARE), bf16),
            dma((7,)), dma((7,)), dma((7,)), dma((7,)), dma((7,)), dma((7,)),
            dma((3,)), dma((3,)), dma((7,)), dma((7,)), dma((7,)), dma((7,)),
        ],
        compiler_params=pltpu.CompilerParams(
            collective_id=3, has_side_effects=True, vmem_limit_bytes=32 * 2**20
        ),
        name="finish_right_and_relations",
    )(parts, right, right_state, relation_grad, relations, relation_state)


def body(
    left_block, left_state, right_block, right_state, relations, relation_state,
    source_ids, relation_ids, target_ids, sample_ids, bucket_counts,
):
    left, right = left_block.T, right_block.T
    left_sums, right_sums = left_state.reshape(1, SHARE), right_state.reshape(1, SHARE)
    operators, operator_state = relations.T, relation_state.T
    rows, ids = gather(right, source_ids, relation_ids, target_ids)
    grad = jnp.zeros((D, NREL), f32)
    parts, left, left_sums, grad = train(
        0, rows, ids, sample_ids, bucket_counts, left, left_sums, operators, grad
    )
    rows, right, right_sums, left, left_sums = exchange(parts, right, right_sums, left, left_sums)
    parts, left, left_sums, grad = train(
        1, rows, ids, sample_ids, bucket_counts, left, left_sums, operators, grad
    )
    right, right_sums, operators, operator_state = finish(
        parts, right, right_sums, grad, operators, operator_state
    )
    return (
        left.T, left_sums.reshape(SHARE), right.T, right_sums.reshape(SHARE),
        operators.T, operator_state.T,
    )


def solution(mesh):
    block, row = P(("pair", "edge"), None), P(("pair", "edge"))
    ids, group = P(None, ("pair", "edge")), P(None, "pair")
    return jax.shard_map(
        body,
        mesh=mesh,
        in_specs=(block, row, block, row, P(), P(), ids, ids, ids, group, group),
        out_specs=(block, row, block, row, P(), P()),
        check_vma=False,
    )
```

```python
import functools

import jax
import jax.numpy as jnp
from jax import lax
from jax.experimental import pallas as pl
from jax.experimental.pallas import tpu as pltpu
from jax.sharding import PartitionSpec as P

ENTITY_RATE = 0.3
RELATION_RATE = 0.3
D, H = 400, 200
SHARE = 128
MEMBERS = 8
GROUPS = 32
ROWS = SHARE * MEMBERS
NREL = 256
SLOTS = 500
LANES = 512
NEG = 1000
ROOM = 640
MESH = pl.DeviceIdType.MESH
SMEM = pl.BlockSpec(memory_space=pltpu.SMEM)
CHUNK = 256
VMEM = pl.BlockSpec(memory_space=pltpu.VMEM)
DMA = pltpu.SemaphoreType.DMA
f32, bf16, i32 = jnp.float32, jnp.bfloat16, jnp.int32
NA, NB = 208, 192
A, B = pl.ds(0, NA), pl.ds(NA, NB)


def remote(src, dst, send, recv, pair, edge):
    return pltpu.make_async_remote_copy(
        src_ref=src, dst_ref=dst, send_sem=send, recv_sem=recv,
        device_id=(pair, edge), device_id_type=MESH,
    )


def greet(devices):
    barrier = pltpu.get_barrier_semaphore()
    for device in devices:
        pl.semaphore_signal(barrier, inc=1, device_id=device, device_id_type=MESH)
    pl.semaphore_wait(barrier, len(devices))


def members(pair, edge):
    return [(pair, lax.rem(edge + d, MEMBERS)) for d in range(1, MEMBERS)]


def gather_kernel(right, source, relation, target, rows, ids, wide, low, send, recv):
    pair, edge = lax.axis_index("pair"), lax.axis_index("edge")
    peers = members(pair, edge)
    wide[...] = jnp.full_like(wide, -1.0)
    for r in range(2):
        s, k, t = (x[r : r + 1, :] for x in (source, relation, target))
        for row, value in enumerate((s >> 7, (s & 127) + 1, k, t >> 7, t & 127)):
            wide[8 * r + row : 8 * r + row + 1, 0:SLOTS] = value.astype(f32)
    ids[edge] = wide[...].astype(bf16)
    rows[edge] = right[...].astype(bf16)
    greet(peers)
    copies = []
    for d, peer in enumerate(peers):
        for j, ref in enumerate((ids, rows)):
            copy = remote(ref.at[edge], ref.at[edge], send.at[j, d], recv.at[j, d], *peer)
            copy.start()
            copies.append(copy)
    for copy in copies:
        copy.wait()


def gather(right, source, relation, target):
    return pl.pallas_call(
        gather_kernel,
        out_shape=(
            jax.ShapeDtypeStruct((MEMBERS, D, SHARE), bf16),
            jax.ShapeDtypeStruct((MEMBERS, 16, LANES), bf16),
        ),
        in_specs=[VMEM] * 4,
        out_specs=(VMEM, VMEM),
        scratch_shapes=[
            pltpu.VMEM((16, LANES), f32),
            pltpu.VMEM((16, LANES), bf16),
            pltpu.SemaphoreType.DMA((2, MEMBERS - 1)),
            pltpu.SemaphoreType.DMA((2, MEMBERS - 1)),
        ],
        compiler_params=pltpu.CompilerParams(collective_id=2, has_side_effects=True),
        name="gather_right",
    )(right, source, relation, target)


def chunks_kernel(
    r, rows, ids, samples, counts, left, left_state, relations, relation_in,
    right_grad, left_out, left_state_out, relation_out,
    table, table_t, rank, often, both, right_sum, left_sum,
):
    edge = lax.axis_index("edge")
    left_low = left[...].astype(bf16)
    high = relations[...].astype(bf16)
    both[:, 0:NREL] = high
    both[:, NREL:] = (relations[...] - high.astype(f32)).astype(bf16)
    for m in range(MEMBERS):
        table_t[:, m * SHARE : (m + 1) * SHARE] = rows[m]
        table[m * SHARE : (m + 1) * SHARE, :] = rows[m].T
    picked = flag(lax.broadcasted_iota(i32, (ROWS, NEG), 0) == samples[r : r + 1, :])
    often[...] = nn(picked, jnp.full((NEG, SHARE), 1.0, bf16)) * (1.0 / NEG)

    owner = jnp.concatenate(
        [ids[m].astype(f32)[8 * r : 8 * r + 1, :] for m in range(MEMBERS)], axis=0
    )
    lane = lax.broadcasted_iota(i32, (MEMBERS, LANES), 1)
    slot = lax.broadcasted_iota(i32, (MEMBERS, LANES), 0) * SLOTS + lane
    mine = (owner == edge.astype(f32)) & (slot < counts[r, 0])
    mark = flag(mine)
    before = flag(
        lax.broadcasted_iota(i32, (LANES, LANES), 0) < lax.broadcasted_iota(i32, (LANES, LANES), 1)
    )
    found = jnp.sum(jnp.where(mine, 1.0, 0.0), axis=1, keepdims=True)
    starts = [jnp.zeros((1, 1), f32)]
    for m in range(MEMBERS):
        starts.append(starts[-1] + found[m : m + 1, :])
    place = nn(mark, before) + jnp.concatenate(starts[:MEMBERS], axis=0)
    rank[...] = jnp.where(mine, place, -1.0).astype(i32)
    total = jnp.sum(found).astype(i32)

    right_sum[...] = jnp.zeros_like(right_sum)
    left_sum[...] = jnp.zeros_like(left_sum)
    relation_out[...] = relation_in[...]

    def chunk(c, carry):
        want = lax.broadcasted_iota(i32, (CHUNK, LANES), 0) + c * CHUNK
        found = jnp.zeros((16, CHUNK), f32)
        for m in range(MEMBERS):
            found = found + nt(ids[m], flag(rank[m : m + 1, :] == want))
        found = found[8 * r : 8 * r + 8, :].astype(i32)
        s, k = found[1:2, :] - 1, found[2:3, :]
        t = found[3:4, :] * SHARE + found[4:5, :]
        source_hot = flag(lax.broadcasted_iota(i32, (SHARE, CHUNK), 0) == s)
        relation_hot = flag(lax.broadcasted_iota(i32, (NREL, CHUNK), 0) == k)
        source = nn(left_low, source_hot)
        operator = nn(both[...], jnp.concatenate([relation_hot, relation_hot], axis=0))
        sr, si, kr, ki = source[:H], source[H:], operator[:H], operator[H:]
        query = jnp.concatenate([sr * kr - si * ki, sr * ki + si * kr], axis=0).astype(bf16)
        scores = nn(table[...], query)
        chance = 0.5 * jnp.tanh(0.5 * scores) + 0.5
        hit = lax.broadcasted_iota(i32, (ROWS, CHUNK), 0) == t
        spread = jnp.concatenate([often[...]] * (CHUNK // SHARE), axis=1)
        weight = (spread * chance - jnp.where(hit, 1.0 - chance, 0.0)).astype(bf16)
        grad = nn(table_t[...], weight)
        right_sum[...] += nt(query, weight)
        gr, gi = grad[:H], grad[H:]
        grad_source = jnp.concatenate([gr * kr + gi * ki, gi * kr - gr * ki], axis=0)
        grad_operator = jnp.concatenate([gr * sr + gi * si, gi * sr - gr * si], axis=0)
        left_sum[...] += nt(grad_source.astype(bf16), source_hot)
        relation_out[...] += nt(grad_operator.astype(bf16), relation_hot)
        return carry

    lax.fori_loop(0, (total + (CHUNK - 1)) // CHUNK, chunk, 0)
    for m in range(MEMBERS):
        right_grad[m] = right_sum[:, m * SHARE : (m + 1) * SHARE].astype(bf16)
    block, state = update(left[...], left_state[...], left_sum[...])
    left_out[...] = block
    left_state_out[...] = state


def train_chunks(r, rows, ids, samples, counts, left, left_state, relations, relation_in):
    return pl.pallas_call(
        functools.partial(chunks_kernel, r),
        out_shape=(
            jax.ShapeDtypeStruct((MEMBERS, D, SHARE), bf16),
            jax.ShapeDtypeStruct((D, SHARE), f32),
            jax.ShapeDtypeStruct((1, SHARE), f32),
            jax.ShapeDtypeStruct((D, NREL), f32),
        ),
        in_specs=[VMEM, VMEM, VMEM, SMEM, VMEM, VMEM, VMEM, VMEM],
        out_specs=(VMEM,) * 4,
        scratch_shapes=[
            pltpu.VMEM((ROWS, D), bf16),
            pltpu.VMEM((D, ROWS), bf16),
            pltpu.VMEM((MEMBERS, LANES), i32),
            pltpu.VMEM((ROWS, SHARE), f32),
            pltpu.VMEM((D, 2 * NREL), bf16),
            pltpu.VMEM((D, ROWS), f32),
            pltpu.VMEM((D, SHARE), f32),
        ],
        compiler_params=pltpu.CompilerParams(vmem_limit_bytes=48 * 2**20),
        name="train_chunks",
    )(rows, ids, samples, counts, left, left_state, relations, relation_in)


def send_parts(parts, landing, send, recv, edge, peers):
    copies = []
    for d, peer in enumerate(peers):
        copy = remote(parts.at[peer[1]], landing.at[edge], send.at[d], recv.at[d], *peer)
        copy.start()
        copies.append(copy)
    return copies


def total_of(parts, landing, copies, edge):
    total = parts[edge].astype(f32)
    for d, copy in enumerate(copies):
        copy.wait_recv()
        total = total + landing[lax.rem(edge + (MEMBERS - 1 - d), MEMBERS)].astype(f32)
    return total


def exchange_kernel(
    parts, right, right_state, left, left_state,
    rows, right_out, right_state_out, left_out, left_state_out,
    landing, out_left, out_right, in_left, in_right, out_states, in_states,
    part_send, part_recv, row_send, row_recv, move_send, move_recv,
):
    pair, edge = lax.axis_index("pair"), lax.axis_index("edge")
    peers = members(pair, edge)
    ahead = (lax.rem(pair + 1, GROUPS), edge)
    behind = (lax.rem(pair + GROUPS - 1, GROUPS), edge)
    out_left[...] = left[...].astype(bf16)
    out_states[0] = jnp.broadcast_to(left_state[...], (8, SHARE))
    greet(peers + [ahead, behind])
    copies = send_parts(parts, landing, part_send, part_recv, edge, peers)
    moves = [
        remote(out_left, in_left, move_send.at[0], move_recv.at[0], *ahead),
        remote(out_states.at[0], in_states.at[0], move_send.at[1], move_recv.at[1], *ahead),
        remote(out_right, in_right, move_send.at[2], move_recv.at[2], *behind),
        remote(out_states.at[1], in_states.at[1], move_send.at[3], move_recv.at[3], *behind),
    ]
    moves[0].start()
    moves[1].start()
    grad = total_of(parts, landing, copies, edge)
    block, state = update(right[...], right_state[...], grad)
    out_right[...] = block.astype(bf16)
    out_states[1] = jnp.broadcast_to(state, (8, SHARE))
    moves[2].start()
    moves[3].start()
    moves[2].wait_recv()
    rows[edge] = in_right[...]
    gathers = []
    for d, peer in enumerate(peers):
        copy = remote(in_right, rows.at[edge], row_send.at[d], row_recv.at[d], *peer)
        copy.start()
        gathers.append(copy)
    right_out[...] = in_right[...].astype(f32)
    moves[3].wait_recv()
    right_state_out[...] = in_states[1, 0:1, :]
    moves[0].wait_recv()
    left_out[...] = in_left[...].astype(f32)
    moves[1].wait_recv()
    left_state_out[...] = in_states[0, 0:1, :]
    for copy in gathers:
        copy.wait_recv()
    for copy in copies + moves + gathers:
        copy.wait_send()


def exchange(parts, right, right_state, left, left_state):
    block = jax.ShapeDtypeStruct((D, SHARE), f32)
    row = jax.ShapeDtypeStruct((1, SHARE), f32)
    low = pltpu.VMEM((D, SHARE), bf16)
    dma = pltpu.SemaphoreType.DMA
    return pl.pallas_call(
        exchange_kernel,
        out_shape=(jax.ShapeDtypeStruct((MEMBERS, D, SHARE), bf16), block, row, block, row),
        in_specs=[VMEM] * 5,
        out_specs=(VMEM,) * 5,
        scratch_shapes=[
            pltpu.VMEM((MEMBERS, D, SHARE), bf16),
            low, low, low, low,
            pltpu.VMEM((2, 8, SHARE), f32),
            pltpu.VMEM((2, 8, SHARE), f32),
            dma((MEMBERS - 1,)), dma((MEMBERS - 1,)),
            dma((MEMBERS - 1,)), dma((MEMBERS - 1,)),
            dma((4,)), dma((4,)),
        ],
        compiler_params=pltpu.CompilerParams(
            collective_id=3, has_side_effects=True, vmem_limit_bytes=32 * 2**20
        ),
        name="exchange_rows",
    )(parts, right, right_state, left, left_state)


def finish_kernel(
    parts, right, right_state, relation_grad, relations, relation_state,
    right_out, right_state_out, relations_out, relation_state_out,
    landing, share, share_in, tiles, tiles_in, quad, whole,
    part_send, part_recv, s1, r1, s2, r2, s3, r3, s4, r4, s5, r5,
):
    pair, edge = lax.axis_index("pair"), lax.axis_index("edge")
    z, q = pair // 4, lax.rem(pair, 4)
    peers = members(pair, edge)
    depth = [(lax.rem(z + d, 8) * 4 + q, edge) for d in range(1, 8)]
    flat = [(z * 4 + lax.rem(q + d, 4), edge) for d in range(1, 4)]
    share[...] = jnp.zeros_like(share)
    grads = relation_grad[...].astype(bf16)
    stacked = jnp.concatenate(
        [grads[:, 0:SHARE], grads[:, SHARE:], jnp.zeros((224, SHARE), bf16)], axis=0
    )
    for m in range(MEMBERS):
        share[m] = stacked[m * SHARE : (m + 1) * SHARE, :]
    greet(peers + depth + flat)
    first = send_parts(share, share_in, s1, r1, edge, peers)
    copies = send_parts(parts, landing, part_send, part_recv, edge, peers)
    done = first + copies
    sums = total_of(share, share_in, first, edge).astype(bf16)
    for k in range(8):
        tiles[k] = sums[16 * k : 16 * k + 16, :]
    second = []
    for d, peer in enumerate(depth):
        copy = remote(
            tiles.at[lax.rem(z + d + 1, 8)], tiles_in.at[z], s2.at[d], r2.at[d], *peer
        )
        copy.start()
        second.append(copy)
    total = tiles[z].astype(f32)
    for d, copy in enumerate(second):
        copy.wait_recv()
        total = total + tiles_in[lax.rem(z + 7 - d, 8)].astype(f32)
    quad[q] = total
    third = []
    for d, peer in enumerate(flat):
        copy = remote(quad.at[q], quad.at[q], s3.at[d], r3.at[d], *peer)
        copy.start()
        third.append(copy)
    for copy in third:
        copy.wait_recv()
    rows = pl.ds(pl.multiple_of(z * 16, 16), 16)
    whole[edge, rows, :] = (quad[0] + quad[1] + quad[2] + quad[3]).astype(bf16)
    fourth = []
    for d, peer in enumerate(depth):
        here = whole.at[edge, rows, :]
        copy = remote(here, here, s4.at[d], r4.at[d], *peer)
        copy.start()
        fourth.append(copy)

    grad = total_of(parts, landing, copies, edge)
    block, state = update(right[...], right_state[...], grad)
    right_out[...] = block
    right_state_out[...] = state

    for copy in fourth:
        copy.wait_recv()
    fifth = []
    for d, peer in enumerate(peers):
        copy = remote(whole.at[edge], whole.at[edge], s5.at[d], r5.at[d], *peer)
        copy.start()
        fifth.append(copy)
    for copy in fifth:
        copy.wait_recv()
    gathered = whole[...].reshape(MEMBERS * SHARE, SHARE)
    grad = jnp.concatenate([gathered[0:D], gathered[D : 2 * D]], axis=1).astype(f32)
    state = relation_state[...] + grad * grad
    relation_state_out[...] = state
    relations_out[...] = relations[...] - RELATION_RATE * grad / jnp.sqrt(state)
    for copy in done + second + third + fourth + fifth:
        copy.wait_send()


def finish(parts, right, right_state, relation_grad, relations, relation_state):
    dma = pltpu.SemaphoreType.DMA
    table = jax.ShapeDtypeStruct((D, NREL), f32)
    return pl.pallas_call(
        finish_kernel,
        out_shape=(
            jax.ShapeDtypeStruct((D, SHARE), f32), jax.ShapeDtypeStruct((1, SHARE), f32),
            table, table,
        ),
        in_specs=[VMEM] * 6,
        out_specs=(VMEM,) * 4,
        scratch_shapes=[
            pltpu.VMEM((MEMBERS, D, SHARE), bf16),
            pltpu.VMEM((MEMBERS, SHARE, SHARE), bf16),
            pltpu.VMEM((MEMBERS, SHARE, SHARE), bf16),
            pltpu.VMEM((8, 16, SHARE), bf16),
            pltpu.VMEM((8, 16, SHARE), bf16),
            pltpu.VMEM((4, 16, SHARE), f32),
            pltpu.VMEM((MEMBERS, SHARE, SHARE), bf16),
            dma((7,)), dma((7,)), dma((7,)), dma((7,)), dma((7,)), dma((7,)),
            dma((3,)), dma((3,)), dma((7,)), dma((7,)), dma((7,)), dma((7,)),
        ],
        compiler_params=pltpu.CompilerParams(
            collective_id=4, has_side_effects=True, vmem_limit_bytes=32 * 2**20
        ),
        name="finish_right_and_relations",
    )(parts, right, right_state, relation_grad, relations, relation_state)


def any_spread(
    left_block, left_state, right_block, right_state, relations, relation_state,
    source_ids, relation_ids, target_ids, sample_ids, bucket_counts,
):
    left, right = left_block.T, right_block.T
    left_sums, right_sums = left_state.reshape(1, SHARE), right_state.reshape(1, SHARE)
    operators, operator_state = relations.T, relation_state.T
    rows, ids = gather(right, source_ids, relation_ids, target_ids)
    grad = jnp.zeros((D, NREL), f32)
    parts, left, left_sums, grad = train_chunks(
        0, rows, ids, sample_ids, bucket_counts, left, left_sums, operators, grad
    )
    rows, right, right_sums, left, left_sums = exchange(parts, right, right_sums, left, left_sums)
    parts, left, left_sums, grad = train_chunks(
        1, rows, ids, sample_ids, bucket_counts, left, left_sums, operators, grad
    )
    right, right_sums, operators, operator_state = finish(
        parts, right, right_sums, grad, operators, operator_state
    )
    return (
        left.T, left_sums.reshape(SHARE), right.T, right_sums.reshape(SHARE),
        operators.T, operator_state.T,
    )


def nt(a, b):
    return lax.dot_general(a, b, (((1,), (1,)), ((), ())), preferred_element_type=f32)


def nn(a, b):
    return jnp.dot(a, b, preferred_element_type=f32)


def flag(condition):
    return jnp.where(condition, 1.0, 0.0).astype(bf16)


def columns(member):
    return pl.ds(pl.multiple_of(member * SHARE, SHARE), SHARE)


class Mail:
    def __init__(self, send, recv):
        self.send, self.recv, self.sent = send, recv, {}

    def post(self, k, src, dst, device):
        copy = pltpu.make_async_remote_copy(
            src_ref=src, dst_ref=dst, send_sem=self.send.at[k], recv_sem=self.recv.at[k],
            device_id=device, device_id_type=MESH,
        )
        copy.start()
        self.sent[k] = copy

    def take(self, *keys):
        for k in keys:
            self.sent[k].wait_recv()

    def close(self):
        for copy in self.sent.values():
            copy.wait_send()


class Place:
    def __init__(self):
        pair, edge = lax.axis_index("pair"), lax.axis_index("edge")
        self.pair, self.edge = pair, edge
        self.x, self.y = edge // 4, lax.rem(edge, 4)
        self.z, self.core = pair // 4, lax.rem(pair, 2)
        self.chip = lax.rem(pair // 2, 2) * 8 + edge
        other = (1 - self.x) * 4
        up, far, down = (lax.rem(self.y + d, 4) for d in (1, 2, 3))
        self.up, self.down, self.far = self.x * 4 + up, self.x * 4 + down, self.x * 4 + far
        self.o, self.oup, self.odown, self.ofar = other + self.y, other + up, other + down, other + far
        self.twin = (pair + 1 - 2 * self.core, edge)
        self.plane = []
        for d in range(1, 16):
            c = lax.rem(self.chip + d, 16)
            self.plane.append((self.z * 4 + (c // 8) * 2 + self.core, lax.rem(c, 8)))
        self.depth = [(lax.rem(pair + 4 * d, GROUPS), edge) for d in range(1, 8)]
        self.peers = [(pair, lax.rem(edge + d, MEMBERS)) for d in range(1, MEMBERS)]

    def group(self, distance):
        return (lax.rem(self.pair + distance + GROUPS, GROUPS), self.edge)

    def met(self):
        return self.plane + self.depth + [self.twin] + [self.group(d) for d in (1, -1, 2, -2)]


def spread(here, rows, mail):
    up, down, far, o = here.up, here.down, here.far, here.o

    def go(k, slot, piece, member):
        ref = rows.at[piece, columns(slot)]
        mail.post(k, ref, ref, (here.pair, member))

    edge = here.edge
    go(0, edge, A, o)
    go(1, edge, B, far), go(2, edge, B, up), go(3, edge, B, down)
    go(4, edge, B, o)
    go(5, edge, A, far), go(6, edge, A, up), go(7, edge, A, down)
    yield
    mail.take(0)
    go(8, o, A, far), go(9, o, A, up), go(10, o, A, down)
    yield
    mail.take(2)
    go(11, down, B, o)
    mail.take(3)
    go(12, up, B, o)
    mail.take(1)
    go(13, far, B, o)
    yield
    mail.take(4, 5, 6, 7, 8, 9, 10, 11, 12, 13)
    mail.close()


def fold_scratch():
    low = lambda *s: pltpu.VMEM(s + (SHARE,), bf16)
    return [low(7, NA), low(7, NB), low(1, NA), low(3, NB), DMA((14,)), DMA((14,))]


def fold(here, parts, total, land_a, land_b, out_a, out_b, send, recv):
    mail = Mail(send, recv)
    up, down, far, o = here.up, here.down, here.far, here.o

    def go(k, src, dst, member):
        mail.post(k, src, dst, (here.pair, member))

    def part(slot, piece):
        return parts[slot, piece].astype(f32)

    for k, slot, member in ((3, here.oup, up), (4, here.odown, down), (5, here.ofar, far)):
        go(k, parts.at[slot, A], land_a.at[k], member)
    for k, slot in ((8, here.oup), (9, here.odown), (10, here.ofar)):
        go(k, parts.at[slot, B], land_b.at[k - 7], o)
    for k, slot in ((0, up), (1, down), (2, far)):
        go(k, parts.at[slot, A], land_a.at[k], slot)
    go(7, parts.at[o, B], land_b.at[0], o)
    yield
    mail.take(3, 4, 5)
    out_a[0] = (
        part(o, A) + land_a[3].astype(f32) + land_a[4].astype(f32) + land_a[5].astype(f32)
    ).astype(bf16)
    go(6, out_a.at[0], land_a.at[6], o)
    yield
    for i, member in enumerate((up, down, far)):
        mail.take(8 + i)
        out_b[i] = (part(member, B) + land_b[1 + i].astype(f32)).astype(bf16)
        go(11 + i, out_b.at[i], land_b.at[4 + i], member)
    yield
    mail.take(0, 1, 2, 6)
    total[A] = part(here.edge, A) + sum(land_a[i].astype(f32) for i in (0, 1, 2, 6))
    mail.take(7, 11, 12, 13)
    total[B] = part(here.edge, B) + sum(land_b[i].astype(f32) for i in (0, 4, 5, 6))
    mail.close()


def reduce_scratch():
    low = lambda *s: pltpu.VMEM(s + (SHARE,), bf16)
    return [
        low(2, 16, 32), low(16, 32), low(16, 32), low(16, 32), low(8, 32), low(2, 16, 32),
        DMA((2,)), DMA((2,)), DMA((15,)), DMA((15,)), DMA((7,)), DMA((7,)), DMA((15,)), DMA((15,)),
    ]


def reduce_all(here, share, from_twin, mine, from_plane, from_depth, whole, cs, cr, s1, r1, s2, r2, s3, r3):
    core, chip, z = here.core, here.chip, here.z
    twin, first, second, third = Mail(cs, cr), Mail(s1, r1), Mail(s2, r2), Mail(s3, r3)
    twin.post(0, share.at[1 - core], from_twin, here.twin)
    yield
    twin.take(0)
    mine[...] = (share[core].astype(f32) + from_twin[...].astype(f32)).astype(bf16)
    for d, device in enumerate(here.plane):
        first.post(d, mine.at[lax.rem(chip + d + 1, 16)], from_plane.at[chip], device)
    yield
    total = mine[chip].astype(f32)
    for d in range(15):
        first.take(d)
        total = total + from_plane[lax.rem(chip + 15 - d, 16)].astype(f32)
    from_depth[z] = total.astype(bf16)
    for d, device in enumerate(here.depth):
        second.post(d, from_depth.at[z], from_depth.at[z], device)
    yield
    second.take(*range(7))
    whole[core, chip] = sum(from_depth[k].astype(f32) for k in range(8)).astype(bf16)
    for d, device in enumerate(here.plane):
        third.post(d, whole.at[core, chip], whole.at[core, chip], device)
    yield
    third.take(*range(15))
    twin.post(1, whole.at[core], whole.at[core], here.twin)
    yield
    twin.take(1)
    for mail in (twin, first, second, third):
        mail.close()


def update(block, state, grad):
    state = state + jnp.sum(grad * grad, axis=0, keepdims=True) * (1.0 / D)
    return block - ENTITY_RATE * grad / jnp.sqrt(state), state


def draw_share(drawn):
    picked = flag(lax.broadcasted_iota(i32, (ROWS, ROWS), 0) == drawn)
    return nt(jnp.full((8, ROWS), 1.0, bf16), picked) * (1.0 / NEG)


def pick(edge, ids, r, source_hot, relation_hot, target):
    owner = jnp.concatenate(
        [ids[m].astype(f32)[8 * r : 8 * r + 1, :] for m in range(MEMBERS)], axis=0
    )
    mine = owner == edge.astype(f32)
    before = flag(
        lax.broadcasted_iota(i32, (LANES, LANES), 0) < lax.broadcasted_iota(i32, (LANES, LANES), 1)
    )
    found = jnp.sum(jnp.where(mine, 1.0, 0.0), axis=1, keepdims=True)
    starts = [jnp.zeros((1, 1), f32)]
    for m in range(MEMBERS):
        starts.append(starts[-1] + found[m : m + 1, :])
    place = nn(flag(mine), before) + jnp.concatenate(starts[:MEMBERS], axis=0)
    rank = jnp.where(mine, place, -1.0).astype(i32)
    want = lax.broadcasted_iota(i32, (ROOM, LANES), 0)
    as_row, as_column = jnp.zeros((16, ROOM), f32), jnp.zeros((ROOM, 16), f32)
    for m in range(MEMBERS):
        chosen = flag(rank[m : m + 1, :] == want)
        as_row = as_row + nt(ids[m], chosen)
        as_column = as_column + nt(chosen, ids[m])
    as_row = as_row[8 * r : 8 * r + 8, :].astype(i32)
    source_hot[...] = flag(lax.broadcasted_iota(i32, (SHARE, ROOM), 0) == as_row[1:2, :] - 1)
    relation_hot[...] = flag(lax.broadcasted_iota(i32, (NREL, ROOM), 0) == as_row[2:3, :])
    wanted = as_column[:, 8 * r + 3 : 8 * r + 4] * SHARE + as_column[:, 8 * r + 4 : 8 * r + 5]
    target[...] = jnp.broadcast_to(wanted.astype(i32), (ROOM, SHARE))
    return jnp.where(starts[MEMBERS] > ROOM, 1.0, 0.0)


def ask(left_low, both, source_hot, relation_hot, source, operator, query, query_t):
    source[...] = nn(left_low, source_hot[...])
    operator[...] = nn(both[...], jnp.concatenate([relation_hot[...], relation_hot[...]], axis=0))
    sr, si, kr, ki = source[:H], source[H:], operator[:H], operator[H:]
    asked = jnp.concatenate([sr * kr - si * ki, sr * ki + si * kr], axis=0).astype(bf16)
    query[...] = asked
    query_t[...] = asked.T


def weigh(b, rows, often, target, query_t, weight):
    wide = pl.ds(b * 2 * SHARE, 2 * SHARE)
    scores = nn(query_t[...], rows[:, wide])
    lane = lax.broadcasted_iota(i32, (ROOM, SHARE), 1)
    for j in range(2):
        block = pl.ds((2 * b + j) * SHARE, SHARE)
        chance = 0.5 * jnp.tanh(0.5 * scores[:, j * SHARE : (j + 1) * SHARE]) + 0.5
        hit = lane + (2 * b + j) * SHARE == target[...]
        value = often[0:1, block] * chance - jnp.where(hit, 1.0 - chance, 0.0)
        weight[:, block] = value.astype(bf16)


def right_parts(b, query, weight, parts):
    wide = nn(query[...], weight[:, pl.ds(b * 2 * SHARE, 2 * SHARE)]).astype(bf16)
    parts[2 * b], parts[2 * b + 1] = wide[:, :SHARE], wide[:, SHARE:]


def train_kernel(
    left, left_state, right, right_state, relations, relation_state,
    source_ids, relation_ids, target_ids, sample_ids, counts,
    left_out, left_state_out, right_out, right_state_out, relations_out, relation_state_out, missed,
    wide, ids1, ids2, drawn1, drawn2, both, rows1, rows2, often1, often2,
    source_hot1, relation_hot1, target1, source_hot2, relation_hot2, target2,
    source, operator, query, query_t, weight, parts1, parts2, total, relation_sum, left_two, left_two_state,
    out_left, in_left, out_right, in_right, out_rows, in_rows, out_states, in_states,
    id_send, id_recv, id2_send, id2_recv, move_send, move_recv,
    spread1_send, spread1_recv, spread2_send, spread2_recv,
    *folds,
):
    fold1, fold2, reduction = folds[:6], folds[6:12], folds[12:]
    here = Place()
    pair, edge = here.pair, here.edge
    barrier = pltpu.get_barrier_semaphore()
    met = here.met()
    for device in met:
        pl.semaphore_signal(barrier, inc=1, device_id=device, device_id_type=MESH)

    wide[...] = jnp.full_like(wide, -1.0)
    slot = edge * SLOTS + lax.broadcasted_iota(i32, (1, SLOTS), 1)
    for r in range(2):
        s, k, t = (x[r : r + 1, :] for x in (source_ids, relation_ids, target_ids))
        owner = jnp.where(slot < counts[0:1, r : r + 1], s >> 7, -1)
        for row, value in enumerate((owner, (s & 127) + 1, k, t >> 7, t & 127)):
            wide[8 * r + row : 8 * r + row + 1, 0:SLOTS] = value.astype(f32)
    ids1[edge] = wide[...].astype(bf16)
    drawn1[...] = jnp.full_like(drawn1, -1)
    drawn1[:, 0:NEG] = sample_ids[...]
    for j in range(8):
        drawn2[0, j : j + 1, :] = drawn1[1:2, j * SHARE : (j + 1) * SHARE]
    rows1[:, columns(edge)] = right[...].astype(bf16)
    often1[...] = draw_share(drawn1[0:1, :])
    pl.semaphore_wait(barrier, len(met))

    id_mail, id2_mail, moves = Mail(id_send, id_recv), Mail(id2_send, id2_recv), Mail(move_send, move_recv)
    ahead, behind = here.group(1), here.group(-1)
    for d, device in enumerate(here.peers):
        id_mail.post(d, ids1.at[edge], ids1.at[edge], device)
    moves.post(0, ids1.at[edge], ids2.at[edge], ahead)
    moves.post(1, drawn2.at[0], drawn2.at[1], ahead)
    gather = spread(here, rows1, Mail(spread1_send, spread1_recv))
    next(gather)
    high = relations[...].astype(bf16)
    both[:, 0:NREL] = high
    both[:, NREL:] = (relations[...] - high.astype(f32)).astype(bf16)
    id_mail.take(*range(7))
    next(gather)
    late1 = pick(edge, ids1, 0, source_hot1, relation_hot1, target1)
    next(gather)
    ask(left[...].astype(bf16), both, source_hot1, relation_hot1, source, operator, query, query_t)
    moves.take(0)
    for d, device in enumerate(here.peers):
        id2_mail.post(d, ids2.at[edge], ids2.at[edge], device)
    next(gather, None)

    for b in range(4):
        weigh(b, rows1, often1, target1, query_t, weight)
        right_parts(b, query, weight, parts1)
    folding = fold(here, parts1, total, *fold1)
    next(folding)
    grad = nt(rows1[...], weight[...])
    gr, gi, kr, ki = grad[:H], grad[H:], operator[:H], operator[H:]
    back = jnp.concatenate([gr * kr + gi * ki, gi * kr - gr * ki], axis=0).astype(bf16)
    left_sum = nt(back, source_hot1[...])
    block, state = update(left[...], left_state[...], left_sum)
    out_left[...] = block.astype(bf16)
    out_states[0] = jnp.broadcast_to(state, (8, SHARE))
    moves.post(2, out_left, in_left, here.group(2))
    moves.post(3, out_states.at[0], in_states.at[0], here.group(2))
    next(folding)
    sr, si = source[:H], source[H:]
    back = jnp.concatenate([gr * sr + gi * si, gi * sr - gr * si], axis=0).astype(bf16)
    relation_sum[...] = nt(back, relation_hot1[...])
    next(folding)
    id2_mail.take(*range(7))
    late2 = pick(edge, ids2, 1, source_hot2, relation_hot2, target2)
    moves.take(1)
    often2[...] = draw_share(
        jnp.concatenate([drawn2[1, j : j + 1, :] for j in range(8)], axis=1)
    )
    next(folding, None)
    right_two, right_two_state = update(right[...], right_state[...], total[...])
    rows2[:, columns(edge)] = right_two.astype(bf16)
    gather = spread(here, rows2, Mail(spread2_send, spread2_recv))
    next(gather)
    right_out[...] = right_two
    moves.take(2, 3)
    left_two[...] = in_left[...].astype(f32)
    left_two_state[...] = in_states[0, 0:1, :]
    next(gather)
    ask(in_left[...], both, source_hot2, relation_hot2, source, operator, query, query_t)
    next(gather)
    next(gather, None)

    for b in range(4):
        weigh(b, rows2, often2, target2, query_t, weight)
    grad = nt(rows2[...], weight[...])
    gr, gi, sr, si = grad[:H], grad[H:], source[:H], source[H:]
    back = jnp.concatenate([gr * sr + gi * si, gi * sr - gr * si], axis=0).astype(bf16)
    relation_grad = relation_sum[...] + nt(back, relation_hot2[...])
    last = jnp.broadcast_to(late1 + late2, (224, SHARE))
    share = reduction[0]
    share[...] = (
        jnp.concatenate([relation_grad[:, :SHARE], relation_grad[:, SHARE:], last], axis=0)
        .reshape(2, 16, 32, SHARE)
        .astype(bf16)
    )
    reducing = reduce_all(here, *reduction)
    next(reducing)
    for b in range(4):
        right_parts(b, query, weight, parts2)
    next(reducing)
    folding = fold(here, parts2, total, *fold2)
    next(folding)
    kr, ki = operator[:H], operator[H:]
    back = jnp.concatenate([gr * kr + gi * ki, gi * kr - gr * ki], axis=0).astype(bf16)
    left_sum = nt(back, source_hot2[...])
    block, state = update(left_two[...], left_two_state[...], left_sum)
    out_rows[0] = block.astype(bf16)
    out_states[1] = jnp.broadcast_to(state, (8, SHARE))
    moves.post(4, out_rows.at[0], in_rows.at[0], behind)
    moves.post(5, out_states.at[1], in_states.at[1], behind)
    next(folding)
    next(reducing)
    next(folding)
    next(folding, None)
    block, state = update(right_two, right_two_state, total[...])
    out_rows[1] = block.astype(bf16)
    out_states[2] = jnp.broadcast_to(state, (8, SHARE))
    moves.post(6, out_rows.at[1], in_rows.at[1], behind)
    moves.post(7, out_states.at[2], in_states.at[2], behind)
    next(reducing)
    moves.take(4, 5)
    left_out[...] = in_rows[0].astype(f32)
    left_state_out[...] = in_states[1, 0:1, :]
    next(reducing)
    moves.take(6, 7)
    right_out[...] = in_rows[1].astype(f32)
    right_state_out[...] = in_states[2, 0:1, :]
    next(reducing, None)
    whole = reduction[5]
    gathered = whole[...].reshape(ROWS, SHARE).astype(f32)
    grad = jnp.concatenate([gathered[0:D], gathered[D : 2 * D]], axis=1)
    state = relation_state[...] + grad * grad
    relation_state_out[...] = state
    relations_out[...] = relations[...] - RELATION_RATE * grad / jnp.sqrt(state)
    missed[...] = gathered[2 * D : 2 * D + 8]
    for mail in (id_mail, id2_mail, moves):
        mail.close()


def train(*args):
    table = jax.ShapeDtypeStruct((D, NREL), f32)
    block = jax.ShapeDtypeStruct((D, SHARE), f32)
    row = jax.ShapeDtypeStruct((1, SHARE), f32)
    vmem = pltpu.VMEM
    low = vmem((D, SHARE), bf16)
    hots = [vmem((SHARE, ROOM), bf16), vmem((NREL, ROOM), bf16), vmem((ROOM, SHARE), i32)]
    return pl.pallas_call(
        train_kernel,
        out_shape=(block, row, block, row, table, table, jax.ShapeDtypeStruct((8, SHARE), f32)),
        in_specs=[VMEM] * 11,
        out_specs=(VMEM,) * 7,
        scratch_shapes=[
            vmem((16, LANES), f32),
            vmem((MEMBERS, 16, LANES), bf16), vmem((MEMBERS, 16, LANES), bf16),
            vmem((2, ROWS), i32), vmem((2, 8, SHARE), i32),
            vmem((D, 2 * NREL), bf16),
            vmem((D, ROWS), bf16), vmem((D, ROWS), bf16),
            vmem((8, ROWS), f32), vmem((8, ROWS), f32),
            *hots, *hots,
            vmem((D, ROOM), f32), vmem((D, ROOM), f32),
            vmem((D, ROOM), bf16), vmem((ROOM, D), bf16), vmem((ROOM, ROWS), bf16),
            vmem((MEMBERS, D, SHARE), bf16), vmem((MEMBERS, D, SHARE), bf16),
            vmem((D, SHARE), f32), vmem((D, NREL), f32),
            vmem((D, SHARE), f32), vmem((1, SHARE), f32),
            low, low, low, low, vmem((2, D, SHARE), bf16), vmem((2, D, SHARE), bf16),
            vmem((3, 8, SHARE), f32), vmem((3, 8, SHARE), f32),
            DMA((7,)), DMA((7,)), DMA((7,)), DMA((7,)), DMA((8,)), DMA((8,)),
            DMA((14,)), DMA((14,)), DMA((14,)), DMA((14,)),
            *fold_scratch(), *fold_scratch(), *reduce_scratch(),
        ],
        compiler_params=pltpu.CompilerParams(
            collective_id=1, has_side_effects=True, vmem_limit_bytes=56 * 2**20
        ),
        name="train_two_rounds",
    )(*args)


def settle_kernel(*refs):
    for given, out in zip(refs[:6], refs[6:]):
        out[...] = given[...]


def settle(done):
    left, left_sums, right, right_sums, table, table_state = done
    flat = (left.T, left_sums.reshape(1, SHARE), right.T, right_sums.reshape(1, SHARE), table.T, table_state.T)
    left, left_sums, right, right_sums, table, table_state = pl.pallas_call(
        settle_kernel,
        out_shape=tuple(jax.ShapeDtypeStruct(x.shape, x.dtype) for x in flat),
        in_specs=[VMEM] * 6,
        out_specs=(VMEM,) * 6,
        name="settle",
    )(*flat)
    return (
        left.T, left_sums.reshape(SHARE), right.T, right_sums.reshape(SHARE), table.T, table_state.T,
    )


def body(
    left_block, left_state, right_block, right_state, relations, relation_state,
    source_ids, relation_ids, target_ids, sample_ids, bucket_counts,
):
    left, left_sums, right, right_sums, table, table_state, missed = train(
        left_block.T, left_state.reshape(1, SHARE), right_block.T, right_state.reshape(1, SHARE),
        relations.T, relation_state.T,
        source_ids, relation_ids, target_ids, sample_ids, bucket_counts.T,
    )
    fast = (
        left.T, left_sums.reshape(SHARE), right.T, right_sums.reshape(SHARE), table.T, table_state.T,
    )
    done = lax.cond(
        missed[0, 0] > 0.0,
        lambda *args: any_spread(*args[6:]),
        lambda *args: args[:6],
        *fast,
        left_block, left_state, right_block, right_state, relations, relation_state,
        source_ids, relation_ids, target_ids, sample_ids, bucket_counts,
    )
    return settle(done)


def solution(mesh):
    block, row = P(("pair", "edge"), None), P(("pair", "edge"))
    ids, group = P(None, ("pair", "edge")), P(None, "pair")
    return jax.shard_map(
        body,
        mesh=mesh,
        in_specs=(block, row, block, row, P(), P(), ids, ids, ids, group, group),
        out_specs=(block, row, block, row, P(), P()),
        check_vma=False,
    )
```

```python
import functools

import jax
import jax.numpy as jnp
from jax import lax
from jax.experimental import pallas as pl
from jax.experimental.pallas import tpu as pltpu
from jax.sharding import PartitionSpec as P

ENTITY_RATE = 0.3
RELATION_RATE = 0.3
D, H = 400, 200
SHARE = 128
MEMBERS = 8
GROUPS = 32
ROWS = SHARE * MEMBERS
NREL = 256
SLOTS = 500
LANES = 512
NEG = 1000
ROOM = 640
MESH = pl.DeviceIdType.MESH
SMEM = pl.BlockSpec(memory_space=pltpu.SMEM)
CHUNK = 256
VMEM = pl.BlockSpec(memory_space=pltpu.VMEM)
DMA = pltpu.SemaphoreType.DMA
f32, bf16, i32 = jnp.float32, jnp.bfloat16, jnp.int32
NA, NB = 208, 192
A, B = pl.ds(0, NA), pl.ds(NA, NB)


def remote(src, dst, send, recv, pair, edge):
    return pltpu.make_async_remote_copy(
        src_ref=src, dst_ref=dst, send_sem=send, recv_sem=recv,
        device_id=(pair, edge), device_id_type=MESH,
    )


def greet(devices):
    barrier = pltpu.get_barrier_semaphore()
    for device in devices:
        pl.semaphore_signal(barrier, inc=1, device_id=device, device_id_type=MESH)
    pl.semaphore_wait(barrier, len(devices))


def members(pair, edge):
    return [(pair, lax.rem(edge + d, MEMBERS)) for d in range(1, MEMBERS)]


def gather_kernel(right, source, relation, target, rows, ids, wide, low, send, recv):
    pair, edge = lax.axis_index("pair"), lax.axis_index("edge")
    peers = members(pair, edge)
    wide[...] = jnp.full_like(wide, -1.0)
    for r in range(2):
        s, k, t = (x[r : r + 1, :] for x in (source, relation, target))
        for row, value in enumerate((s >> 7, (s & 127) + 1, k, t >> 7, t & 127)):
            wide[8 * r + row : 8 * r + row + 1, 0:SLOTS] = value.astype(f32)
    ids[edge] = wide[...].astype(bf16)
    rows[edge] = right[...].astype(bf16)
    greet(peers)
    copies = []
    for d, peer in enumerate(peers):
        for j, ref in enumerate((ids, rows)):
            copy = remote(ref.at[edge], ref.at[edge], send.at[j, d], recv.at[j, d], *peer)
            copy.start()
            copies.append(copy)
    for copy in copies:
        copy.wait()


def gather(right, source, relation, target):
    return pl.pallas_call(
        gather_kernel,
        out_shape=(
            jax.ShapeDtypeStruct((MEMBERS, D, SHARE), bf16),
            jax.ShapeDtypeStruct((MEMBERS, 16, LANES), bf16),
        ),
        in_specs=[VMEM] * 4,
        out_specs=(VMEM, VMEM),
        scratch_shapes=[
            pltpu.VMEM((16, LANES), f32),
            pltpu.VMEM((16, LANES), bf16),
            pltpu.SemaphoreType.DMA((2, MEMBERS - 1)),
            pltpu.SemaphoreType.DMA((2, MEMBERS - 1)),
        ],
        compiler_params=pltpu.CompilerParams(collective_id=2, has_side_effects=True),
        name="gather_right",
    )(right, source, relation, target)


def chunks_kernel(
    r, rows, ids, samples, counts, left, left_state, relations, relation_in,
    right_grad, left_out, left_state_out, relation_out,
    table, table_t, rank, often, both, right_sum, left_sum,
):
    edge = lax.axis_index("edge")
    left_low = left[...].astype(bf16)
    high = relations[...].astype(bf16)
    both[:, 0:NREL] = high
    both[:, NREL:] = (relations[...] - high.astype(f32)).astype(bf16)
    for m in range(MEMBERS):
        table_t[:, m * SHARE : (m + 1) * SHARE] = rows[m]
        table[m * SHARE : (m + 1) * SHARE, :] = rows[m].T
    picked = flag(lax.broadcasted_iota(i32, (ROWS, NEG), 0) == samples[r : r + 1, :])
    often[...] = nn(picked, jnp.full((NEG, SHARE), 1.0, bf16)) * (1.0 / NEG)

    owner = jnp.concatenate(
        [ids[m].astype(f32)[8 * r : 8 * r + 1, :] for m in range(MEMBERS)], axis=0
    )
    lane = lax.broadcasted_iota(i32, (MEMBERS, LANES), 1)
    slot = lax.broadcasted_iota(i32, (MEMBERS, LANES), 0) * SLOTS + lane
    mine = (owner == edge.astype(f32)) & (slot < counts[r, 0])
    mark = flag(mine)
    before = flag(
        lax.broadcasted_iota(i32, (LANES, LANES), 0) < lax.broadcasted_iota(i32, (LANES, LANES), 1)
    )
    found = jnp.sum(jnp.where(mine, 1.0, 0.0), axis=1, keepdims=True)
    starts = [jnp.zeros((1, 1), f32)]
    for m in range(MEMBERS):
        starts.append(starts[-1] + found[m : m + 1, :])
    place = nn(mark, before) + jnp.concatenate(starts[:MEMBERS], axis=0)
    rank[...] = jnp.where(mine, place, -1.0).astype(i32)
    total = jnp.sum(found).astype(i32)

    right_sum[...] = jnp.zeros_like(right_sum)
    left_sum[...] = jnp.zeros_like(left_sum)
    relation_out[...] = relation_in[...]

    def chunk(c, carry):
        want = lax.broadcasted_iota(i32, (CHUNK, LANES), 0) + c * CHUNK
        found = jnp.zeros((16, CHUNK), f32)
        for m in range(MEMBERS):
            found = found + nt(ids[m], flag(rank[m : m + 1, :] == want))
        found = found[8 * r : 8 * r + 8, :].astype(i32)
        s, k = found[1:2, :] - 1, found[2:3, :]
        t = found[3:4, :] * SHARE + found[4:5, :]
        source_hot = flag(lax.broadcasted_iota(i32, (SHARE, CHUNK), 0) == s)
        relation_hot = flag(lax.broadcasted_iota(i32, (NREL, CHUNK), 0) == k)
        source = nn(left_low, source_hot)
        operator = nn(both[...], jnp.concatenate([relation_hot, relation_hot], axis=0))
        sr, si, kr, ki = source[:H], source[H:], operator[:H], operator[H:]
        query = jnp.concatenate([sr * kr - si * ki, sr * ki + si * kr], axis=0).astype(bf16)
        scores = nn(table[...], query)
        chance = 0.5 * jnp.tanh(0.5 * scores) + 0.5
        hit = lax.broadcasted_iota(i32, (ROWS, CHUNK), 0) == t
        spread = jnp.concatenate([often[...]] * (CHUNK // SHARE), axis=1)
        weight = (spread * chance - jnp.where(hit, 1.0 - chance, 0.0)).astype(bf16)
        grad = nn(table_t[...], weight)
        right_sum[...] += nt(query, weight)
        gr, gi = grad[:H], grad[H:]
        grad_source = jnp.concatenate([gr * kr + gi * ki, gi * kr - gr * ki], axis=0)
        grad_operator = jnp.concatenate([gr * sr + gi * si, gi * sr - gr * si], axis=0)
        left_sum[...] += nt(grad_source.astype(bf16), source_hot)
        relation_out[...] += nt(grad_operator.astype(bf16), relation_hot)
        return carry

    lax.fori_loop(0, (total + (CHUNK - 1)) // CHUNK, chunk, 0)
    for m in range(MEMBERS):
        right_grad[m] = right_sum[:, m * SHARE : (m + 1) * SHARE].astype(bf16)
    block, state = update(left[...], left_state[...], left_sum[...])
    left_out[...] = block
    left_state_out[...] = state


def train_chunks(r, rows, ids, samples, counts, left, left_state, relations, relation_in):
    return pl.pallas_call(
        functools.partial(chunks_kernel, r),
        out_shape=(
            jax.ShapeDtypeStruct((MEMBERS, D, SHARE), bf16),
            jax.ShapeDtypeStruct((D, SHARE), f32),
            jax.ShapeDtypeStruct((1, SHARE), f32),
            jax.ShapeDtypeStruct((D, NREL), f32),
        ),
        in_specs=[VMEM, VMEM, VMEM, SMEM, VMEM, VMEM, VMEM, VMEM],
        out_specs=(VMEM,) * 4,
        scratch_shapes=[
            pltpu.VMEM((ROWS, D), bf16),
            pltpu.VMEM((D, ROWS), bf16),
            pltpu.VMEM((MEMBERS, LANES), i32),
            pltpu.VMEM((ROWS, SHARE), f32),
            pltpu.VMEM((D, 2 * NREL), bf16),
            pltpu.VMEM((D, ROWS), f32),
            pltpu.VMEM((D, SHARE), f32),
        ],
        compiler_params=pltpu.CompilerParams(vmem_limit_bytes=48 * 2**20),
        name="train_chunks",
    )(rows, ids, samples, counts, left, left_state, relations, relation_in)


def send_parts(parts, landing, send, recv, edge, peers):
    copies = []
    for d, peer in enumerate(peers):
        copy = remote(parts.at[peer[1]], landing.at[edge], send.at[d], recv.at[d], *peer)
        copy.start()
        copies.append(copy)
    return copies


def total_of(parts, landing, copies, edge):
    total = parts[edge].astype(f32)
    for d, copy in enumerate(copies):
        copy.wait_recv()
        total = total + landing[lax.rem(edge + (MEMBERS - 1 - d), MEMBERS)].astype(f32)
    return total


def exchange_kernel(
    parts, right, right_state, left, left_state,
    rows, right_out, right_state_out, left_out, left_state_out,
    landing, out_left, out_right, in_left, in_right, out_states, in_states,
    part_send, part_recv, row_send, row_recv, move_send, move_recv,
):
    pair, edge = lax.axis_index("pair"), lax.axis_index("edge")
    peers = members(pair, edge)
    ahead = (lax.rem(pair + 1, GROUPS), edge)
    behind = (lax.rem(pair + GROUPS - 1, GROUPS), edge)
    out_left[...] = left[...].astype(bf16)
    out_states[0] = jnp.broadcast_to(left_state[...], (8, SHARE))
    greet(peers + [ahead, behind])
    copies = send_parts(parts, landing, part_send, part_recv, edge, peers)
    moves = [
        remote(out_left, in_left, move_send.at[0], move_recv.at[0], *ahead),
        remote(out_states.at[0], in_states.at[0], move_send.at[1], move_recv.at[1], *ahead),
        remote(out_right, in_right, move_send.at[2], move_recv.at[2], *behind),
        remote(out_states.at[1], in_states.at[1], move_send.at[3], move_recv.at[3], *behind),
    ]
    moves[0].start()
    moves[1].start()
    grad = total_of(parts, landing, copies, edge)
    block, state = update(right[...], right_state[...], grad)
    out_right[...] = block.astype(bf16)
    out_states[1] = jnp.broadcast_to(state, (8, SHARE))
    moves[2].start()
    moves[3].start()
    moves[2].wait_recv()
    rows[edge] = in_right[...]
    gathers = []
    for d, peer in enumerate(peers):
        copy = remote(in_right, rows.at[edge], row_send.at[d], row_recv.at[d], *peer)
        copy.start()
        gathers.append(copy)
    right_out[...] = in_right[...].astype(f32)
    moves[3].wait_recv()
    right_state_out[...] = in_states[1, 0:1, :]
    moves[0].wait_recv()
    left_out[...] = in_left[...].astype(f32)
    moves[1].wait_recv()
    left_state_out[...] = in_states[0, 0:1, :]
    for copy in gathers:
        copy.wait_recv()
    for copy in copies + moves + gathers:
        copy.wait_send()


def exchange(parts, right, right_state, left, left_state):
    block = jax.ShapeDtypeStruct((D, SHARE), f32)
    row = jax.ShapeDtypeStruct((1, SHARE), f32)
    low = pltpu.VMEM((D, SHARE), bf16)
    dma = pltpu.SemaphoreType.DMA
    return pl.pallas_call(
        exchange_kernel,
        out_shape=(jax.ShapeDtypeStruct((MEMBERS, D, SHARE), bf16), block, row, block, row),
        in_specs=[VMEM] * 5,
        out_specs=(VMEM,) * 5,
        scratch_shapes=[
            pltpu.VMEM((MEMBERS, D, SHARE), bf16),
            low, low, low, low,
            pltpu.VMEM((2, 8, SHARE), f32),
            pltpu.VMEM((2, 8, SHARE), f32),
            dma((MEMBERS - 1,)), dma((MEMBERS - 1,)),
            dma((MEMBERS - 1,)), dma((MEMBERS - 1,)),
            dma((4,)), dma((4,)),
        ],
        compiler_params=pltpu.CompilerParams(
            collective_id=3, has_side_effects=True, vmem_limit_bytes=32 * 2**20
        ),
        name="exchange_rows",
    )(parts, right, right_state, left, left_state)


def finish_kernel(
    parts, right, right_state, relation_grad, relations, relation_state,
    right_out, right_state_out, relations_out, relation_state_out,
    landing, share, share_in, tiles, tiles_in, quad, whole,
    part_send, part_recv, s1, r1, s2, r2, s3, r3, s4, r4, s5, r5,
):
    pair, edge = lax.axis_index("pair"), lax.axis_index("edge")
    z, q = pair // 4, lax.rem(pair, 4)
    peers = members(pair, edge)
    depth = [(lax.rem(z + d, 8) * 4 + q, edge) for d in range(1, 8)]
    flat = [(z * 4 + lax.rem(q + d, 4), edge) for d in range(1, 4)]
    share[...] = jnp.zeros_like(share)
    grads = relation_grad[...].astype(bf16)
    stacked = jnp.concatenate(
        [grads[:, 0:SHARE], grads[:, SHARE:], jnp.zeros((224, SHARE), bf16)], axis=0
    )
    for m in range(MEMBERS):
        share[m] = stacked[m * SHARE : (m + 1) * SHARE, :]
    greet(peers + depth + flat)
    first = send_parts(share, share_in, s1, r1, edge, peers)
    copies = send_parts(parts, landing, part_send, part_recv, edge, peers)
    done = first + copies
    sums = total_of(share, share_in, first, edge).astype(bf16)
    for k in range(8):
        tiles[k] = sums[16 * k : 16 * k + 16, :]
    second = []
    for d, peer in enumerate(depth):
        copy = remote(
            tiles.at[lax.rem(z + d + 1, 8)], tiles_in.at[z], s2.at[d], r2.at[d], *peer
        )
        copy.start()
        second.append(copy)
    total = tiles[z].astype(f32)
    for d, copy in enumerate(second):
        copy.wait_recv()
        total = total + tiles_in[lax.rem(z + 7 - d, 8)].astype(f32)
    quad[q] = total
    third = []
    for d, peer in enumerate(flat):
        copy = remote(quad.at[q], quad.at[q], s3.at[d], r3.at[d], *peer)
        copy.start()
        third.append(copy)
    for copy in third:
        copy.wait_recv()
    rows = pl.ds(pl.multiple_of(z * 16, 16), 16)
    whole[edge, rows, :] = (quad[0] + quad[1] + quad[2] + quad[3]).astype(bf16)
    fourth = []
    for d, peer in enumerate(depth):
        here = whole.at[edge, rows, :]
        copy = remote(here, here, s4.at[d], r4.at[d], *peer)
        copy.start()
        fourth.append(copy)

    grad = total_of(parts, landing, copies, edge)
    block, state = update(right[...], right_state[...], grad)
    right_out[...] = block
    right_state_out[...] = state

    for copy in fourth:
        copy.wait_recv()
    fifth = []
    for d, peer in enumerate(peers):
        copy = remote(whole.at[edge], whole.at[edge], s5.at[d], r5.at[d], *peer)
        copy.start()
        fifth.append(copy)
    for copy in fifth:
        copy.wait_recv()
    gathered = whole[...].reshape(MEMBERS * SHARE, SHARE)
    grad = jnp.concatenate([gathered[0:D], gathered[D : 2 * D]], axis=1).astype(f32)
    state = relation_state[...] + grad * grad
    relation_state_out[...] = state
    relations_out[...] = relations[...] - RELATION_RATE * grad / jnp.sqrt(state)
    for copy in done + second + third + fourth + fifth:
        copy.wait_send()


def finish(parts, right, right_state, relation_grad, relations, relation_state):
    dma = pltpu.SemaphoreType.DMA
    table = jax.ShapeDtypeStruct((D, NREL), f32)
    return pl.pallas_call(
        finish_kernel,
        out_shape=(
            jax.ShapeDtypeStruct((D, SHARE), f32), jax.ShapeDtypeStruct((1, SHARE), f32),
            table, table,
        ),
        in_specs=[VMEM] * 6,
        out_specs=(VMEM,) * 4,
        scratch_shapes=[
            pltpu.VMEM((MEMBERS, D, SHARE), bf16),
            pltpu.VMEM((MEMBERS, SHARE, SHARE), bf16),
            pltpu.VMEM((MEMBERS, SHARE, SHARE), bf16),
            pltpu.VMEM((8, 16, SHARE), bf16),
            pltpu.VMEM((8, 16, SHARE), bf16),
            pltpu.VMEM((4, 16, SHARE), f32),
            pltpu.VMEM((MEMBERS, SHARE, SHARE), bf16),
            dma((7,)), dma((7,)), dma((7,)), dma((7,)), dma((7,)), dma((7,)),
            dma((3,)), dma((3,)), dma((7,)), dma((7,)), dma((7,)), dma((7,)),
        ],
        compiler_params=pltpu.CompilerParams(
            collective_id=4, has_side_effects=True, vmem_limit_bytes=32 * 2**20
        ),
        name="finish_right_and_relations",
    )(parts, right, right_state, relation_grad, relations, relation_state)


def any_spread(
    left_block, left_state, right_block, right_state, relations, relation_state,
    source_ids, relation_ids, target_ids, sample_ids, bucket_counts,
):
    left, right = left_block.T, right_block.T
    left_sums, right_sums = left_state.reshape(1, SHARE), right_state.reshape(1, SHARE)
    operators, operator_state = relations.T, relation_state.T
    rows, ids = gather(right, source_ids, relation_ids, target_ids)
    grad = jnp.zeros((D, NREL), f32)
    parts, left, left_sums, grad = train_chunks(
        0, rows, ids, sample_ids, bucket_counts, left, left_sums, operators, grad
    )
    rows, right, right_sums, left, left_sums = exchange(parts, right, right_sums, left, left_sums)
    parts, left, left_sums, grad = train_chunks(
        1, rows, ids, sample_ids, bucket_counts, left, left_sums, operators, grad
    )
    right, right_sums, operators, operator_state = finish(
        parts, right, right_sums, grad, operators, operator_state
    )
    return (
        left.T, left_sums.reshape(SHARE), right.T, right_sums.reshape(SHARE),
        operators.T, operator_state.T,
    )


def nt(a, b):
    return lax.dot_general(a, b, (((1,), (1,)), ((), ())), preferred_element_type=f32)


def nn(a, b):
    return jnp.dot(a, b, preferred_element_type=f32)


def flag(condition):
    return jnp.where(condition, 1.0, 0.0).astype(bf16)


def columns(member):
    return pl.ds(pl.multiple_of(member * SHARE, SHARE), SHARE)


class Mail:
    def __init__(self, send, recv):
        self.send, self.recv, self.sent = send, recv, {}

    def post(self, k, src, dst, device):
        copy = pltpu.make_async_remote_copy(
            src_ref=src, dst_ref=dst, send_sem=self.send.at[k], recv_sem=self.recv.at[k],
            device_id=device, device_id_type=MESH,
        )
        copy.start()
        self.sent[k] = copy

    def take(self, *keys):
        for k in keys:
            self.sent[k].wait_recv()

    def close(self):
        for copy in self.sent.values():
            copy.wait_send()


class Place:
    def __init__(self):
        pair, edge = lax.axis_index("pair"), lax.axis_index("edge")
        self.pair, self.edge = pair, edge
        self.x, self.y = edge // 4, lax.rem(edge, 4)
        self.z, self.core = pair // 4, lax.rem(pair, 2)
        self.chip = lax.rem(pair // 2, 2) * 8 + edge
        self.up, self.far, self.down = (lax.rem(self.y + d, 4) for d in (1, 2, 3))
        self.o, self.oup, self.ofar, self.odown = (4 + v for v in (self.y, self.up, self.far, self.down))
        self.twin = (pair + 1 - 2 * self.core, edge)
        self.plane = []
        for d in range(1, 16):
            c = lax.rem(self.chip + d, 16)
            self.plane.append((self.z * 4 + (c // 8) * 2 + self.core, lax.rem(c, 8)))
        self.depth = [(lax.rem(pair + 4 * d, GROUPS), edge) for d in range(1, 8)]
        self.peers = [(pair, lax.rem(edge + d, MEMBERS)) for d in range(1, MEMBERS)]

    def group(self, distance):
        return (lax.rem(self.pair + distance + GROUPS, GROUPS), self.edge)

    def member(self, slot):
        return (self.pair, lax.rem(slot + 4 * self.x, MEMBERS))

    def met(self):
        return self.plane + self.depth + [self.twin] + [self.group(d) for d in (1, -1, 2, -2)]


def spread(here, rows, mail):
    up, down, far, o = here.up, here.down, here.far, here.o

    def go(k, slot, piece, to):
        there = lax.rem(slot + 4, MEMBERS) if to is o else slot
        mail.post(k, rows.at[piece, columns(slot)], rows.at[piece, columns(there)], here.member(to))

    me = here.y
    go(0, me, A, o)
    go(1, me, B, far), go(2, me, B, up), go(3, me, B, down)
    go(4, me, B, o)
    go(5, me, A, far), go(6, me, A, up), go(7, me, A, down)
    yield
    mail.take(0)
    go(8, o, A, far), go(9, o, A, up), go(10, o, A, down)
    yield
    mail.take(2)
    go(11, down, B, o)
    mail.take(3)
    go(12, up, B, o)
    yield
    mail.take(1)
    go(13, far, B, o)
    yield
    mail.take(5, 6, 7)
    yield
    mail.take(4, 8, 9, 10, 11, 12, 13)
    mail.close()


def fold_scratch():
    low = lambda *s: pltpu.VMEM(s + (SHARE,), bf16)
    return [low(7, NA), low(7, NB), low(1, NA), low(3, NB), DMA((14,)), DMA((14,))]


def fold(here, parts, total, land_a, land_b, out_a, out_b, send, recv):
    mail = Mail(send, recv)
    up, down, far, o = here.up, here.down, here.far, here.o

    def go(k, src, dst, to):
        mail.post(k, src, dst, here.member(to))

    def part(slot, piece):
        return parts[slot, piece].astype(f32)

    for k, slot in ((2, far), (0, up), (1, down)):
        go(k, parts.at[slot, A], land_a.at[k], slot)
    yield
    for k, slot, member in ((5, here.ofar, far), (3, here.oup, up), (4, here.odown, down)):
        go(k, parts.at[slot, A], land_a.at[k], member)
    for k, slot in ((10, here.ofar), (8, here.oup), (9, here.odown)):
        go(k, parts.at[slot, B], land_b.at[k - 7], o)
    go(7, parts.at[o, B], land_b.at[0], o)
    yield
    mail.take(3, 4, 5)
    out_a[0] = (
        part(o, A) + land_a[3].astype(f32) + land_a[4].astype(f32) + land_a[5].astype(f32)
    ).astype(bf16)
    go(6, out_a.at[0], land_a.at[6], o)
    yield
    for i, member in ((2, far), (0, up), (1, down)):
        mail.take(8 + i)
        out_b[i] = (part(member, B) + land_b[1 + i].astype(f32)).astype(bf16)
        go(11 + i, out_b.at[i], land_b.at[4 + i], member)
    yield
    mail.take(0, 1, 2, 6)
    total[A] = part(here.y, A) + sum(land_a[i].astype(f32) for i in (0, 1, 2, 6))
    mail.take(7, 11, 12, 13)
    total[B] = part(here.y, B) + sum(land_b[i].astype(f32) for i in (0, 4, 5, 6))
    mail.close()


def reduce_scratch():
    low = lambda *s: pltpu.VMEM(s + (SHARE,), bf16)
    return [
        low(2, 16, 32), low(16, 32), low(16, 32), low(16, 32), low(8, 32), low(2, 16, 32),
        DMA((17,)), DMA((17,)), DMA((15,)), DMA((15,)), DMA((7,)), DMA((7,)), DMA((15,)), DMA((15,)),
    ]


def reduce_all(here, share, from_twin, mine, from_plane, from_depth, whole, cs, cr, s1, r1, s2, r2, s3, r3):
    core, chip, z = here.core, here.chip, here.z
    twin, first, second, third = Mail(cs, cr), Mail(s1, r1), Mail(s2, r2), Mail(s3, r3)
    twin.post(0, share.at[1 - core], from_twin, here.twin)
    yield
    twin.take(0)
    mine[...] = (share[core].astype(f32) + from_twin[...].astype(f32)).astype(bf16)
    for d, device in enumerate(here.plane):
        first.post(d, mine.at[lax.rem(chip + d + 1, 16)], from_plane.at[chip], device)
    yield
    total = mine[chip].astype(f32)
    for d in range(15):
        first.take(d)
        total = total + from_plane[lax.rem(chip + 15 - d, 16)].astype(f32)
    from_depth[z] = total.astype(bf16)
    for d, device in enumerate(here.depth):
        second.post(d, from_depth.at[z], from_depth.at[z], device)
    yield
    second.take(*range(7))
    whole[core, chip] = sum(from_depth[k].astype(f32) for k in range(8)).astype(bf16)
    for d, device in enumerate(here.plane):
        third.post(d, whole.at[core, chip], whole.at[core, chip], device)
    twin.post(16, whole.at[core, chip], whole.at[core, chip], here.twin)
    yield
    for d in range(15):
        third.take(d)
        chunk = whole.at[core, lax.rem(chip + 15 - d, 16)]
        twin.post(1 + d, chunk, chunk, here.twin)
    yield
    twin.take(*range(1, 17))
    for mail in (twin, first, second, third):
        mail.close()


def update(block, state, grad):
    state = state + jnp.sum(grad * grad, axis=0, keepdims=True) * (1.0 / D)
    return block - ENTITY_RATE * grad / jnp.sqrt(state), state


def draw_share(x, drawn):
    drawn = jnp.where(drawn < 0, -1, (drawn + 4 * SHARE * x) & (ROWS - 1))
    picked = flag(lax.broadcasted_iota(i32, (ROWS, ROWS), 0) == drawn)
    return nt(jnp.full((8, ROWS), 1.0, bf16), picked) * (1.0 / NEG)


def line_up(edge, ids, r):
    owner = jnp.concatenate(
        [ids[m].astype(f32)[8 * r : 8 * r + 1, :] for m in range(MEMBERS)], axis=0
    )
    mine = owner == edge.astype(f32)
    before = flag(
        lax.broadcasted_iota(i32, (LANES, LANES), 0) < lax.broadcasted_iota(i32, (LANES, LANES), 1)
    )
    found = jnp.sum(jnp.where(mine, 1.0, 0.0), axis=1, keepdims=True)
    starts = [jnp.zeros((1, 1), f32)]
    for m in range(MEMBERS):
        starts.append(starts[-1] + found[m : m + 1, :])
    place = nn(flag(mine), before) + jnp.concatenate(starts[:MEMBERS], axis=0)
    rank = jnp.where(mine, place, -1.0).astype(i32)
    return rank, jnp.where(starts[MEMBERS] > ROOM, 1.0, 0.0)


def pick(x, rank, ids, r, source_hot, relation_hot, target):
    high, low = rank >> 7, rank & (SHARE - 1)
    as_row, as_column = jnp.zeros((32, SHARE), f32), jnp.zeros((SHARE, 32), f32)
    for m in range(MEMBERS):
        low_hot = flag(lax.broadcasted_iota(i32, (SHARE, LANES), 0) == low[m : m + 1, :])
        high_hot = lax.broadcasted_iota(i32, (8, LANES), 0) == high[m : m + 1, :]
        values = ids[m].astype(f32)[8 * r : 8 * r + 8]
        values = jnp.concatenate(
            [jnp.where(high_hot, values[f : f + 1, :], 0.0) for f in range(1, 5)], axis=0
        ).astype(bf16)
        as_row = as_row + nt(values, low_hot)
        as_column = as_column + nt(low_hot, values)
    blocks = range(ROOM // SHARE)
    s = jnp.concatenate([as_row[h : h + 1, :] for h in blocks], axis=1).astype(i32)
    k = jnp.concatenate([as_row[8 + h : 9 + h, :] for h in blocks], axis=1).astype(i32)
    source_hot[...] = flag(lax.broadcasted_iota(i32, (SHARE, ROOM), 0) == s - 1)
    relation_hot[...] = flag(lax.broadcasted_iota(i32, (NREL, ROOM), 0) == k)
    wanted = as_column.astype(i32)
    for h in blocks:
        t = ((wanted[:, 16 + h : 17 + h] + 4 * x) & 7) * SHARE + wanted[:, 24 + h : 25 + h]
        target[h * SHARE : (h + 1) * SHARE, :] = jnp.broadcast_to(t, (SHARE, SHARE))


def ask(left_low, both, source_hot, relation_hot, source, operator, query, query_t):
    source[...] = nn(left_low, source_hot[...])
    operator[...] = nn(both[...], jnp.concatenate([relation_hot[...], relation_hot[...]], axis=0))
    sr, si, kr, ki = source[:H], source[H:], operator[:H], operator[H:]
    asked = jnp.concatenate([sr * kr - si * ki, sr * ki + si * kr], axis=0).astype(bf16)
    query[...] = asked
    query_t[...] = asked.T


def weigh(half, rows, often, target, query_t, weight):
    lane = lax.broadcasted_iota(i32, (ROOM, SHARE), 1)
    for b in range(2):
        start = (4 * half + 2 * b) * SHARE
        scores = nn(query_t[...], rows[:, pl.ds(start, 2 * SHARE)])
        for j in range(2):
            block = pl.ds(start + j * SHARE, SHARE)
            chance = 0.5 * jnp.tanh(0.5 * scores[:, j * SHARE : (j + 1) * SHARE]) + 0.5
            hit = lane + (start + j * SHARE) == target[...]
            value = often[0:1, block] * chance - jnp.where(hit, 1.0 - chance, 0.0)
            weight[:, block] = value.astype(bf16)


def right_parts(half, query, weight, parts):
    for b in range(2):
        first = 4 * half + 2 * b
        wide = nn(query[...], weight[:, pl.ds(first * SHARE, 2 * SHARE)]).astype(bf16)
        parts[first], parts[first + 1] = wide[:, :SHARE], wide[:, SHARE:]


def train_kernel(
    *refs,
):
    fetched, loads = refs[18:29], refs[29]
    fetch = [
        pltpu.make_async_copy(given, taken, loads.at[i])
        for i, (given, taken) in enumerate(zip(refs[:11], fetched))
    ]
    train_rounds(fetch, *fetched, *refs[11:18], *refs[30:])


def train_rounds(
    fetch,
    left, left_state, right, right_state, relations, relation_state,
    source_ids, relation_ids, target_ids, sample_ids, counts,
    left_out, left_state_out, right_out, right_state_out, relations_out, relation_state_out, missed,
    wide, ids1, ids2, drawn1, drawn2, both, rows1, rows2, often1, often2,
    source_hot1, relation_hot1, target1, source_hot2, relation_hot2, target2,
    source, operator, query, query_t, weight, parts1, parts2, total, relation_sum, left_two, left_two_state,
    out_left, in_left, out_right, in_right, out_rows, in_rows, out_states, in_states,
    id_send, id_recv, id2_send, id2_recv, move_send, move_recv,
    spread1_send, spread1_recv, spread2_send, spread2_recv,
    *folds,
):
    fold1, fold2, reduction = folds[:6], folds[6:12], folds[12:]
    for i in (6, 7, 8, 10, 2, 9, 4, 0, 1, 3, 5):
        fetch[i].start()
    here = Place()
    pair, edge = here.pair, here.edge
    barrier = pltpu.get_barrier_semaphore()
    met = here.met()
    for device in met:
        pl.semaphore_signal(barrier, inc=1, device_id=device, device_id_type=MESH)

    wide[...] = jnp.full_like(wide, -1.0)
    for i in (6, 7, 8, 10):
        fetch[i].wait()
    slot = edge * SLOTS + lax.broadcasted_iota(i32, (1, SLOTS), 1)
    for r in range(2):
        s, k, t = (x[r : r + 1, :] for x in (source_ids, relation_ids, target_ids))
        owner = jnp.where(slot < counts[0:1, r : r + 1], s >> 7, -1)
        for row, value in enumerate((owner, (s & 127) + 1, k, t >> 7, t & 127)):
            wide[8 * r + row : 8 * r + row + 1, 0:SLOTS] = value.astype(f32)
    ids1[edge] = wide[...].astype(bf16)
    fetch[2].wait()
    rows1[:, columns(here.y)] = right[...].astype(bf16)
    pl.semaphore_wait(barrier, len(met))

    id_mail, id2_mail, moves = Mail(id_send, id_recv), Mail(id2_send, id2_recv), Mail(move_send, move_recv)
    ahead, behind = here.group(1), here.group(-1)
    for d, device in enumerate(here.peers):
        id_mail.post(d, ids1.at[edge], ids1.at[edge], device)
    gather = spread(here, rows1, Mail(spread1_send, spread1_recv))
    next(gather)
    moves.post(0, ids1.at[edge], ids2.at[edge], ahead)
    fetch[9].wait()
    drawn1[...] = jnp.full_like(drawn1, -1)
    drawn1[:, 0:NEG] = sample_ids[...]
    for j in range(8):
        drawn2[0, j : j + 1, :] = drawn1[1:2, j * SHARE : (j + 1) * SHARE]
    moves.post(1, drawn2.at[0], drawn2.at[1], ahead)
    often1[...] = draw_share(here.x, drawn1[0:1, :])
    fetch[4].wait()
    high = relations[...].astype(bf16)
    both[:, 0:NREL] = high
    both[:, NREL:] = (relations[...] - high.astype(f32)).astype(bf16)
    next(gather)
    id_mail.take(*range(7))
    rank, late1 = line_up(edge, ids1, 0)
    next(gather)
    next(gather)
    pick(here.x, rank, ids1, 0, source_hot1, relation_hot1, target1)
    fetch[0].wait()
    ask(left[...].astype(bf16), both, source_hot1, relation_hot1, source, operator, query, query_t)
    moves.take(0)
    for d, device in enumerate(here.peers):
        id2_mail.post(d, ids2.at[edge], ids2.at[edge], device)
    next(gather)

    weigh(0, rows1, often1, target1, query_t, weight)
    right_parts(0, query, weight, parts1)
    folding = fold(here, parts1, total, *fold1)
    next(folding)
    next(gather, None)
    weigh(1, rows1, often1, target1, query_t, weight)
    right_parts(1, query, weight, parts1)
    next(folding)
    for i in (1, 3, 5):
        fetch[i].wait()
    grad = nt(rows1[...], weight[...])
    gr, gi, kr, ki = grad[:H], grad[H:], operator[:H], operator[H:]
    back = jnp.concatenate([gr * kr + gi * ki, gi * kr - gr * ki], axis=0).astype(bf16)
    left_sum = nt(back, source_hot1[...])
    block, state = update(left[...], left_state[...], left_sum)
    out_left[...] = block.astype(bf16)
    out_states[0] = jnp.broadcast_to(state, (8, SHARE))
    moves.post(2, out_left, in_left, here.group(2))
    moves.post(3, out_states.at[0], in_states.at[0], here.group(2))
    next(folding)
    sr, si = source[:H], source[H:]
    back = jnp.concatenate([gr * sr + gi * si, gi * sr - gr * si], axis=0).astype(bf16)
    for c in range(2):
        relation_sum[c] = nt(back, relation_hot1[c * SHARE : (c + 1) * SHARE, :])
    next(folding)
    id2_mail.take(*range(7))
    rank, late2 = line_up(edge, ids2, 1)
    pick(here.x, rank, ids2, 1, source_hot2, relation_hot2, target2)
    moves.take(1)
    often2[...] = draw_share(
        here.x, jnp.concatenate([drawn2[1, j : j + 1, :] for j in range(8)], axis=1)
    )
    next(folding, None)
    right_two, right_two_state = update(right[...], right_state[...], total[...])
    rows2[:, columns(here.y)] = right_two.astype(bf16)
    gather = spread(here, rows2, Mail(spread2_send, spread2_recv))
    next(gather)
    moves.take(2, 3)
    left_two[...] = in_left[...].astype(f32)
    left_two_state[...] = in_states[0, 0:1, :]
    ask(in_left[...], both, source_hot2, relation_hot2, source, operator, query, query_t)
    for _ in range(4):
        next(gather)

    weigh(0, rows2, often2, target2, query_t, weight)
    right_parts(0, query, weight, parts2)
    folding = fold(here, parts2, total, *fold2)
    next(folding)
    next(gather, None)
    weigh(1, rows2, often2, target2, query_t, weight)
    grad = nt(rows2[...], weight[...])
    gr, gi, sr, si = grad[:H], grad[H:], source[:H], source[H:]
    back = jnp.concatenate([gr * sr + gi * si, gi * sr - gr * si], axis=0).astype(bf16)
    last = jnp.broadcast_to(late1 + late2, (512 - D, SHARE))
    share, whole = reduction[0], reduction[5]
    reducing = reduce_all(here, *reduction)
    for c in (1 - here.core, here.core):
        hot = relation_hot2[columns(c), :]
        full = jnp.concatenate([relation_sum[c] + nt(back, hot), last], axis=0)
        share[c] = full.reshape(16, 32, SHARE).astype(bf16)
        if c is not here.core:
            next(reducing)
    right_parts(1, query, weight, parts2)
    next(folding)
    next(reducing)
    kr, ki = operator[:H], operator[H:]
    back = jnp.concatenate([gr * kr + gi * ki, gi * kr - gr * ki], axis=0).astype(bf16)
    left_sum = nt(back, source_hot2[...])
    block, state = update(left_two[...], left_two_state[...], left_sum)
    out_rows[0] = block.astype(bf16)
    out_states[1] = jnp.broadcast_to(state, (8, SHARE))
    moves.post(4, out_rows.at[0], in_rows.at[0], behind)
    moves.post(5, out_states.at[1], in_states.at[1], behind)
    next(folding)
    next(reducing)
    next(folding)
    next(reducing)
    next(folding, None)
    block, state = update(right_two, right_two_state, total[...])
    out_rows[1] = block.astype(bf16)
    out_states[2] = jnp.broadcast_to(state, (8, SHARE))
    moves.post(6, out_rows.at[1], in_rows.at[1], behind)
    moves.post(7, out_states.at[2], in_states.at[2], behind)
    moves.take(4, 5)
    left_out[...] = in_rows[0].astype(f32)
    left_state_out[...] = in_states[1, 0:1, :]
    next(reducing)

    def relation_update(c):
        half = columns(c)
        grad = whole[c].reshape(512, SHARE)[:D].astype(f32)
        state = relation_state[:, half] + grad * grad
        relation_state_out[:, half] = state
        relations_out[:, half] = relations[:, half] - RELATION_RATE * grad / jnp.sqrt(state)

    relation_update(here.core)
    missed[...] = whole[here.core].reshape(512, SHARE)[D : D + 16].astype(f32)[0:1, 0:1].astype(i32)
    moves.take(6, 7)
    right_out[...] = in_rows[1].astype(f32)
    right_state_out[...] = in_states[2, 0:1, :]
    next(reducing, None)
    relation_update(1 - here.core)
    for mail in (id_mail, id2_mail, moves):
        mail.close()


def train(*args):
    table = jax.ShapeDtypeStruct((D, NREL), f32)
    block = jax.ShapeDtypeStruct((D, SHARE), f32)
    row = jax.ShapeDtypeStruct((1, SHARE), f32)
    vmem = pltpu.VMEM
    low = vmem((D, SHARE), bf16)
    hots = [vmem((SHARE, ROOM), bf16), vmem((NREL, ROOM), bf16), vmem((ROOM, SHARE), i32)]
    return pl.pallas_call(
        train_kernel,
        out_shape=(block, row, block, row, table, table, jax.ShapeDtypeStruct((1, 1), i32)),
        in_specs=[pl.BlockSpec(memory_space=pl.ANY)] * 11,
        out_specs=(VMEM,) * 7,
        scratch_shapes=[
            *(vmem(x.shape, x.dtype) for x in args), DMA((11,)),
            vmem((16, LANES), f32),
            vmem((MEMBERS, 16, LANES), bf16), vmem((MEMBERS, 16, LANES), bf16),
            vmem((2, ROWS), i32), vmem((2, 8, SHARE), i32),
            vmem((D, 2 * NREL), bf16),
            vmem((D, ROWS), bf16), vmem((D, ROWS), bf16),
            vmem((8, ROWS), f32), vmem((8, ROWS), f32),
            *hots, *hots,
            vmem((D, ROOM), f32), vmem((D, ROOM), f32),
            vmem((D, ROOM), bf16), vmem((ROOM, D), bf16), vmem((ROOM, ROWS), bf16),
            vmem((MEMBERS, D, SHARE), bf16), vmem((MEMBERS, D, SHARE), bf16),
            vmem((D, SHARE), f32), vmem((2, D, SHARE), f32),
            vmem((D, SHARE), f32), vmem((1, SHARE), f32),
            low, low, low, low, vmem((2, D, SHARE), bf16), vmem((2, D, SHARE), bf16),
            vmem((3, 8, SHARE), f32), vmem((3, 8, SHARE), f32),
            DMA((7,)), DMA((7,)), DMA((7,)), DMA((7,)), DMA((8,)), DMA((8,)),
            DMA((14,)), DMA((14,)), DMA((14,)), DMA((14,)),
            *fold_scratch(), *fold_scratch(), *reduce_scratch(),
        ],
        compiler_params=pltpu.CompilerParams(
            collective_id=1, has_side_effects=True, vmem_limit_bytes=56 * 2**20
        ),
        name="train_two_rounds",
    )(*args)


def settle_kernel(*refs):
    for given, out in zip(refs[:6], refs[6:]):
        out[...] = given[...]


def settle(done):
    left, left_sums, right, right_sums, table, table_state = done
    flat = (left.T, left_sums.reshape(1, SHARE), right.T, right_sums.reshape(1, SHARE), table.T, table_state.T)
    left, left_sums, right, right_sums, table, table_state = pl.pallas_call(
        settle_kernel,
        out_shape=tuple(jax.ShapeDtypeStruct(x.shape, x.dtype) for x in flat),
        in_specs=[VMEM] * 6,
        out_specs=(VMEM,) * 6,
        name="settle",
    )(*flat)
    return (
        left.T, left_sums.reshape(SHARE), right.T, right_sums.reshape(SHARE), table.T, table_state.T,
    )


def body(
    left_block, left_state, right_block, right_state, relations, relation_state,
    source_ids, relation_ids, target_ids, sample_ids, bucket_counts,
):
    left, left_sums, right, right_sums, table, table_state, missed = train(
        left_block.T, left_state.reshape(1, SHARE), right_block.T, right_state.reshape(1, SHARE),
        relations.T, relation_state.T,
        source_ids, relation_ids, target_ids, sample_ids, bucket_counts.T,
    )
    fast = (
        left.T, left_sums.reshape(SHARE), right.T, right_sums.reshape(SHARE), table.T, table_state.T,
    )
    done = lax.cond(
        missed[0, 0] > 0,
        lambda *args: any_spread(*args[6:]),
        lambda *args: args[:6],
        *fast,
        left_block, left_state, right_block, right_state, relations, relation_state,
        source_ids, relation_ids, target_ids, sample_ids, bucket_counts,
    )
    return settle(done)


def solution(mesh):
    block, row = P(("pair", "edge"), None), P(("pair", "edge"))
    ids, group = P(None, ("pair", "edge")), P(None, "pair")
    return jax.shard_map(
        body,
        mesh=mesh,
        in_specs=(block, row, block, row, P(), P(), ids, ids, ids, group, group),
        out_specs=(block, row, block, row, P(), P()),
        check_vma=False,
    )
```

```python
import functools

import jax
import jax.numpy as jnp
from jax import lax
from jax.experimental import pallas as pl
from jax.experimental.pallas import tpu as pltpu
from jax.sharding import PartitionSpec as P

ENTITY_RATE = 0.3
RELATION_RATE = 0.3
D, H = 400, 200
SHARE = 128
MEMBERS = 8
GROUPS = 32
ROWS = SHARE * MEMBERS
NREL = 256
SLOTS = 500
LANES = 512
NEG = 1000
ROOM = 640
MESH = pl.DeviceIdType.MESH
SMEM = pl.BlockSpec(memory_space=pltpu.SMEM)
CHUNK = 256
VMEM = pl.BlockSpec(memory_space=pltpu.VMEM)
DMA = pltpu.SemaphoreType.DMA
f32, bf16, i32 = jnp.float32, jnp.bfloat16, jnp.int32
NA, NB = 208, 192
A, B = pl.ds(0, NA), pl.ds(NA, NB)
PLANE = sorted(
    ((dx, dy) for dx in range(4) for dy in range(4) if dx or dy),
    key=lambda o: -min(o[0], 4 - o[0]) - min(o[1], 4 - o[1]),
)
DEPTH = (4, 3, 5, 2, 6, 1, 7)


def remote(src, dst, send, recv, pair, edge):
    return pltpu.make_async_remote_copy(
        src_ref=src, dst_ref=dst, send_sem=send, recv_sem=recv,
        device_id=(pair, edge), device_id_type=MESH,
    )


def greet(devices):
    barrier = pltpu.get_barrier_semaphore()
    for device in devices:
        pl.semaphore_signal(barrier, inc=1, device_id=device, device_id_type=MESH)
    pl.semaphore_wait(barrier, len(devices))


def members(pair, edge):
    return [(pair, lax.rem(edge + d, MEMBERS)) for d in range(1, MEMBERS)]


def gather_kernel(right, source, relation, target, rows, ids, wide, low, send, recv):
    pair, edge = lax.axis_index("pair"), lax.axis_index("edge")
    peers = members(pair, edge)
    wide[...] = jnp.full_like(wide, -1.0)
    for r in range(2):
        s, k, t = (x[r : r + 1, :] for x in (source, relation, target))
        for row, value in enumerate((s >> 7, (s & 127) + 1, k, t >> 7, t & 127)):
            wide[8 * r + row : 8 * r + row + 1, 0:SLOTS] = value.astype(f32)
    ids[edge] = wide[...].astype(bf16)
    rows[edge] = right[...].astype(bf16)
    greet(peers)
    copies = []
    for d, peer in enumerate(peers):
        for j, ref in enumerate((ids, rows)):
            copy = remote(ref.at[edge], ref.at[edge], send.at[j, d], recv.at[j, d], *peer)
            copy.start()
            copies.append(copy)
    for copy in copies:
        copy.wait()


def gather(right, source, relation, target):
    return pl.pallas_call(
        gather_kernel,
        out_shape=(
            jax.ShapeDtypeStruct((MEMBERS, D, SHARE), bf16),
            jax.ShapeDtypeStruct((MEMBERS, 16, LANES), bf16),
        ),
        in_specs=[VMEM] * 4,
        out_specs=(VMEM, VMEM),
        scratch_shapes=[
            pltpu.VMEM((16, LANES), f32),
            pltpu.VMEM((16, LANES), bf16),
            pltpu.SemaphoreType.DMA((2, MEMBERS - 1)),
            pltpu.SemaphoreType.DMA((2, MEMBERS - 1)),
        ],
        compiler_params=pltpu.CompilerParams(collective_id=2, has_side_effects=True),
        name="gather_right",
    )(right, source, relation, target)


def chunks_kernel(
    r, rows, ids, samples, counts, left, left_state, relations, relation_in,
    right_grad, left_out, left_state_out, relation_out,
    table, table_t, rank, often, both, right_sum, left_sum,
):
    edge = lax.axis_index("edge")
    left_low = left[...].astype(bf16)
    high = relations[...].astype(bf16)
    both[:, 0:NREL] = high
    both[:, NREL:] = (relations[...] - high.astype(f32)).astype(bf16)
    for m in range(MEMBERS):
        table_t[:, m * SHARE : (m + 1) * SHARE] = rows[m]
        table[m * SHARE : (m + 1) * SHARE, :] = rows[m].T
    picked = flag(lax.broadcasted_iota(i32, (ROWS, NEG), 0) == samples[r : r + 1, :])
    often[...] = nn(picked, jnp.full((NEG, SHARE), 1.0, bf16)) * (1.0 / NEG)

    owner = jnp.concatenate(
        [ids[m].astype(f32)[8 * r : 8 * r + 1, :] for m in range(MEMBERS)], axis=0
    )
    lane = lax.broadcasted_iota(i32, (MEMBERS, LANES), 1)
    slot = lax.broadcasted_iota(i32, (MEMBERS, LANES), 0) * SLOTS + lane
    mine = (owner == edge.astype(f32)) & (slot < counts[r, 0])
    mark = flag(mine)
    before = flag(
        lax.broadcasted_iota(i32, (LANES, LANES), 0) < lax.broadcasted_iota(i32, (LANES, LANES), 1)
    )
    found = jnp.sum(jnp.where(mine, 1.0, 0.0), axis=1, keepdims=True)
    starts = [jnp.zeros((1, 1), f32)]
    for m in range(MEMBERS):
        starts.append(starts[-1] + found[m : m + 1, :])
    place = nn(mark, before) + jnp.concatenate(starts[:MEMBERS], axis=0)
    rank[...] = jnp.where(mine, place, -1.0).astype(i32)
    total = jnp.sum(found).astype(i32)

    right_sum[...] = jnp.zeros_like(right_sum)
    left_sum[...] = jnp.zeros_like(left_sum)
    relation_out[...] = relation_in[...]

    def chunk(c, carry):
        want = lax.broadcasted_iota(i32, (CHUNK, LANES), 0) + c * CHUNK
        found = jnp.zeros((16, CHUNK), f32)
        for m in range(MEMBERS):
            found = found + nt(ids[m], flag(rank[m : m + 1, :] == want))
        found = found[8 * r : 8 * r + 8, :].astype(i32)
        s, k = found[1:2, :] - 1, found[2:3, :]
        t = found[3:4, :] * SHARE + found[4:5, :]
        source_hot = flag(lax.broadcasted_iota(i32, (SHARE, CHUNK), 0) == s)
        relation_hot = flag(lax.broadcasted_iota(i32, (NREL, CHUNK), 0) == k)
        source = nn(left_low, source_hot)
        operator = nn(both[...], jnp.concatenate([relation_hot, relation_hot], axis=0))
        sr, si, kr, ki = source[:H], source[H:], operator[:H], operator[H:]
        query = jnp.concatenate([sr * kr - si * ki, sr * ki + si * kr], axis=0).astype(bf16)
        scores = nn(table[...], query)
        chance = 0.5 * jnp.tanh(0.5 * scores) + 0.5
        hit = lax.broadcasted_iota(i32, (ROWS, CHUNK), 0) == t
        spread = jnp.concatenate([often[...]] * (CHUNK // SHARE), axis=1)
        weight = (spread * chance - jnp.where(hit, 1.0 - chance, 0.0)).astype(bf16)
        grad = nn(table_t[...], weight)
        right_sum[...] += nt(query, weight)
        gr, gi = grad[:H], grad[H:]
        grad_source = jnp.concatenate([gr * kr + gi * ki, gi * kr - gr * ki], axis=0)
        grad_operator = jnp.concatenate([gr * sr + gi * si, gi * sr - gr * si], axis=0)
        left_sum[...] += nt(grad_source.astype(bf16), source_hot)
        relation_out[...] += nt(grad_operator.astype(bf16), relation_hot)
        return carry

    lax.fori_loop(0, (total + (CHUNK - 1)) // CHUNK, chunk, 0)
    for m in range(MEMBERS):
        right_grad[m] = right_sum[:, m * SHARE : (m + 1) * SHARE].astype(bf16)
    block, state = update(left[...], left_state[...], left_sum[...])
    left_out[...] = block
    left_state_out[...] = state


def train_chunks(r, rows, ids, samples, counts, left, left_state, relations, relation_in):
    return pl.pallas_call(
        functools.partial(chunks_kernel, r),
        out_shape=(
            jax.ShapeDtypeStruct((MEMBERS, D, SHARE), bf16),
            jax.ShapeDtypeStruct((D, SHARE), f32),
            jax.ShapeDtypeStruct((1, SHARE), f32),
            jax.ShapeDtypeStruct((D, NREL), f32),
        ),
        in_specs=[VMEM, VMEM, VMEM, SMEM, VMEM, VMEM, VMEM, VMEM],
        out_specs=(VMEM,) * 4,
        scratch_shapes=[
            pltpu.VMEM((ROWS, D), bf16),
            pltpu.VMEM((D, ROWS), bf16),
            pltpu.VMEM((MEMBERS, LANES), i32),
            pltpu.VMEM((ROWS, SHARE), f32),
            pltpu.VMEM((D, 2 * NREL), bf16),
            pltpu.VMEM((D, ROWS), f32),
            pltpu.VMEM((D, SHARE), f32),
        ],
        compiler_params=pltpu.CompilerParams(vmem_limit_bytes=48 * 2**20),
        name="train_chunks",
    )(rows, ids, samples, counts, left, left_state, relations, relation_in)


def send_parts(parts, landing, send, recv, edge, peers):
    copies = []
    for d, peer in enumerate(peers):
        copy = remote(parts.at[peer[1]], landing.at[edge], send.at[d], recv.at[d], *peer)
        copy.start()
        copies.append(copy)
    return copies


def total_of(parts, landing, copies, edge):
    total = parts[edge].astype(f32)
    for d, copy in enumerate(copies):
        copy.wait_recv()
        total = total + landing[lax.rem(edge + (MEMBERS - 1 - d), MEMBERS)].astype(f32)
    return total


def exchange_kernel(
    parts, right, right_state, left, left_state,
    rows, right_out, right_state_out, left_out, left_state_out,
    landing, out_left, out_right, in_left, in_right, out_states, in_states,
    part_send, part_recv, row_send, row_recv, move_send, move_recv,
):
    pair, edge = lax.axis_index("pair"), lax.axis_index("edge")
    peers = members(pair, edge)
    ahead = (lax.rem(pair + 1, GROUPS), edge)
    behind = (lax.rem(pair + GROUPS - 1, GROUPS), edge)
    out_left[...] = left[...].astype(bf16)
    out_states[0] = jnp.broadcast_to(left_state[...], (8, SHARE))
    greet(peers + [ahead, behind])
    copies = send_parts(parts, landing, part_send, part_recv, edge, peers)
    moves = [
        remote(out_left, in_left, move_send.at[0], move_recv.at[0], *ahead),
        remote(out_states.at[0], in_states.at[0], move_send.at[1], move_recv.at[1], *ahead),
        remote(out_right, in_right, move_send.at[2], move_recv.at[2], *behind),
        remote(out_states.at[1], in_states.at[1], move_send.at[3], move_recv.at[3], *behind),
    ]
    moves[0].start()
    moves[1].start()
    grad = total_of(parts, landing, copies, edge)
    block, state = update(right[...], right_state[...], grad)
    out_right[...] = block.astype(bf16)
    out_states[1] = jnp.broadcast_to(state, (8, SHARE))
    moves[2].start()
    moves[3].start()
    moves[2].wait_recv()
    rows[edge] = in_right[...]
    gathers = []
    for d, peer in enumerate(peers):
        copy = remote(in_right, rows.at[edge], row_send.at[d], row_recv.at[d], *peer)
        copy.start()
        gathers.append(copy)
    right_out[...] = in_right[...].astype(f32)
    moves[3].wait_recv()
    right_state_out[...] = in_states[1, 0:1, :]
    moves[0].wait_recv()
    left_out[...] = in_left[...].astype(f32)
    moves[1].wait_recv()
    left_state_out[...] = in_states[0, 0:1, :]
    for copy in gathers:
        copy.wait_recv()
    for copy in copies + moves + gathers:
        copy.wait_send()


def exchange(parts, right, right_state, left, left_state):
    block = jax.ShapeDtypeStruct((D, SHARE), f32)
    row = jax.ShapeDtypeStruct((1, SHARE), f32)
    low = pltpu.VMEM((D, SHARE), bf16)
    dma = pltpu.SemaphoreType.DMA
    return pl.pallas_call(
        exchange_kernel,
        out_shape=(jax.ShapeDtypeStruct((MEMBERS, D, SHARE), bf16), block, row, block, row),
        in_specs=[VMEM] * 5,
        out_specs=(VMEM,) * 5,
        scratch_shapes=[
            pltpu.VMEM((MEMBERS, D, SHARE), bf16),
            low, low, low, low,
            pltpu.VMEM((2, 8, SHARE), f32),
            pltpu.VMEM((2, 8, SHARE), f32),
            dma((MEMBERS - 1,)), dma((MEMBERS - 1,)),
            dma((MEMBERS - 1,)), dma((MEMBERS - 1,)),
            dma((4,)), dma((4,)),
        ],
        compiler_params=pltpu.CompilerParams(
            collective_id=3, has_side_effects=True, vmem_limit_bytes=32 * 2**20
        ),
        name="exchange_rows",
    )(parts, right, right_state, left, left_state)


def finish_kernel(
    parts, right, right_state, relation_grad, relations, relation_state,
    right_out, right_state_out, relations_out, relation_state_out,
    landing, share, share_in, tiles, tiles_in, quad, whole,
    part_send, part_recv, s1, r1, s2, r2, s3, r3, s4, r4, s5, r5,
):
    pair, edge = lax.axis_index("pair"), lax.axis_index("edge")
    z, q = pair // 4, lax.rem(pair, 4)
    peers = members(pair, edge)
    depth = [(lax.rem(z + d, 8) * 4 + q, edge) for d in range(1, 8)]
    flat = [(z * 4 + lax.rem(q + d, 4), edge) for d in range(1, 4)]
    share[...] = jnp.zeros_like(share)
    grads = relation_grad[...].astype(bf16)
    stacked = jnp.concatenate(
        [grads[:, 0:SHARE], grads[:, SHARE:], jnp.zeros((224, SHARE), bf16)], axis=0
    )
    for m in range(MEMBERS):
        share[m] = stacked[m * SHARE : (m + 1) * SHARE, :]
    greet(peers + depth + flat)
    first = send_parts(share, share_in, s1, r1, edge, peers)
    copies = send_parts(parts, landing, part_send, part_recv, edge, peers)
    done = first + copies
    sums = total_of(share, share_in, first, edge).astype(bf16)
    for k in range(8):
        tiles[k] = sums[16 * k : 16 * k + 16, :]
    second = []
    for d, peer in enumerate(depth):
        copy = remote(
            tiles.at[lax.rem(z + d + 1, 8)], tiles_in.at[z], s2.at[d], r2.at[d], *peer
        )
        copy.start()
        second.append(copy)
    total = tiles[z].astype(f32)
    for d, copy in enumerate(second):
        copy.wait_recv()
        total = total + tiles_in[lax.rem(z + 7 - d, 8)].astype(f32)
    quad[q] = total
    third = []
    for d, peer in enumerate(flat):
        copy = remote(quad.at[q], quad.at[q], s3.at[d], r3.at[d], *peer)
        copy.start()
        third.append(copy)
    for copy in third:
        copy.wait_recv()
    rows = pl.ds(pl.multiple_of(z * 16, 16), 16)
    whole[edge, rows, :] = (quad[0] + quad[1] + quad[2] + quad[3]).astype(bf16)
    fourth = []
    for d, peer in enumerate(depth):
        here = whole.at[edge, rows, :]
        copy = remote(here, here, s4.at[d], r4.at[d], *peer)
        copy.start()
        fourth.append(copy)

    grad = total_of(parts, landing, copies, edge)
    block, state = update(right[...], right_state[...], grad)
    right_out[...] = block
    right_state_out[...] = state

    for copy in fourth:
        copy.wait_recv()
    fifth = []
    for d, peer in enumerate(peers):
        copy = remote(whole.at[edge], whole.at[edge], s5.at[d], r5.at[d], *peer)
        copy.start()
        fifth.append(copy)
    for copy in fifth:
        copy.wait_recv()
    gathered = whole[...].reshape(MEMBERS * SHARE, SHARE)
    grad = jnp.concatenate([gathered[0:D], gathered[D : 2 * D]], axis=1).astype(f32)
    state = relation_state[...] + grad * grad
    relation_state_out[...] = state
    relations_out[...] = relations[...] - RELATION_RATE * grad / jnp.sqrt(state)
    for copy in done + second + third + fourth + fifth:
        copy.wait_send()


def finish(parts, right, right_state, relation_grad, relations, relation_state):
    dma = pltpu.SemaphoreType.DMA
    table = jax.ShapeDtypeStruct((D, NREL), f32)
    return pl.pallas_call(
        finish_kernel,
        out_shape=(
            jax.ShapeDtypeStruct((D, SHARE), f32), jax.ShapeDtypeStruct((1, SHARE), f32),
            table, table,
        ),
        in_specs=[VMEM] * 6,
        out_specs=(VMEM,) * 4,
        scratch_shapes=[
            pltpu.VMEM((MEMBERS, D, SHARE), bf16),
            pltpu.VMEM((MEMBERS, SHARE, SHARE), bf16),
            pltpu.VMEM((MEMBERS, SHARE, SHARE), bf16),
            pltpu.VMEM((8, 16, SHARE), bf16),
            pltpu.VMEM((8, 16, SHARE), bf16),
            pltpu.VMEM((4, 16, SHARE), f32),
            pltpu.VMEM((MEMBERS, SHARE, SHARE), bf16),
            dma((7,)), dma((7,)), dma((7,)), dma((7,)), dma((7,)), dma((7,)),
            dma((3,)), dma((3,)), dma((7,)), dma((7,)), dma((7,)), dma((7,)),
        ],
        compiler_params=pltpu.CompilerParams(
            collective_id=4, has_side_effects=True, vmem_limit_bytes=32 * 2**20
        ),
        name="finish_right_and_relations",
    )(parts, right, right_state, relation_grad, relations, relation_state)


def any_spread(
    left_block, left_state, right_block, right_state, relations, relation_state,
    source_ids, relation_ids, target_ids, sample_ids, bucket_counts,
):
    left, right = left_block.T, right_block.T
    left_sums, right_sums = left_state.reshape(1, SHARE), right_state.reshape(1, SHARE)
    operators, operator_state = relations.T, relation_state.T
    rows, ids = gather(right, source_ids, relation_ids, target_ids)
    grad = jnp.zeros((D, NREL), f32)
    parts, left, left_sums, grad = train_chunks(
        0, rows, ids, sample_ids, bucket_counts, left, left_sums, operators, grad
    )
    rows, right, right_sums, left, left_sums = exchange(parts, right, right_sums, left, left_sums)
    parts, left, left_sums, grad = train_chunks(
        1, rows, ids, sample_ids, bucket_counts, left, left_sums, operators, grad
    )
    right, right_sums, operators, operator_state = finish(
        parts, right, right_sums, grad, operators, operator_state
    )
    return (
        left.T, left_sums.reshape(SHARE), right.T, right_sums.reshape(SHARE),
        operators.T, operator_state.T,
    )


def nt(a, b):
    return lax.dot_general(a, b, (((1,), (1,)), ((), ())), preferred_element_type=f32)


def nn(a, b):
    return jnp.dot(a, b, preferred_element_type=f32)


def flag(condition):
    return jnp.where(condition, 1.0, 0.0).astype(bf16)


def columns(member):
    return pl.ds(pl.multiple_of(member * SHARE, SHARE), SHARE)


class Mail:
    def __init__(self, send, recv):
        self.send, self.recv, self.sent = send, recv, {}

    def post(self, k, src, dst, device):
        copy = pltpu.make_async_remote_copy(
            src_ref=src, dst_ref=dst, send_sem=self.send.at[k], recv_sem=self.recv.at[k],
            device_id=device, device_id_type=MESH,
        )
        copy.start()
        self.sent[k] = copy

    def take(self, *keys):
        for k in keys:
            self.sent[k].wait_recv()

    def close(self):
        for copy in self.sent.values():
            copy.wait_send()


class Place:
    def __init__(self):
        pair, edge = lax.axis_index("pair"), lax.axis_index("edge")
        self.pair, self.edge = pair, edge
        self.x, self.y = edge // 4, lax.rem(edge, 4)
        self.z, self.core = pair // 4, lax.rem(pair, 2)
        self.chip = lax.rem(pair // 2, 2) * 8 + edge
        self.up, self.far, self.down = (lax.rem(self.y + d, 4) for d in (1, 2, 3))
        self.o, self.oup, self.ofar, self.odown = (4 + v for v in (self.y, self.up, self.far, self.down))
        self.twin = (pair + 1 - 2 * self.core, edge)
        self.plane = []
        for dx, dy in PLANE:
            c = self.chip_at(dx, dy)
            self.plane.append((self.z * 4 + (c // 8) * 2 + self.core, lax.rem(c, 8)))
        self.depth = [(lax.rem(pair + 4 * d, GROUPS), edge) for d in DEPTH]
        self.peers = [(pair, lax.rem(edge + d, MEMBERS)) for d in range(1, MEMBERS)]

    def group(self, distance):
        return (lax.rem(self.pair + distance + GROUPS, GROUPS), self.edge)

    def chip_at(self, dx, dy):
        return lax.rem(self.chip // 4 + dx, 4) * 4 + lax.rem(self.y + dy, 4)

    def member(self, slot):
        return (self.pair, lax.rem(slot + 4 * self.x, MEMBERS))

    def met(self):
        return self.depth + self.plane + [self.twin] + [self.group(d) for d in (1, -1, 2, -2)]


def spread(here, rows, mail):
    up, down, far, o = here.up, here.down, here.far, here.o

    def go(k, slot, piece, to):
        there = lax.rem(slot + 4, MEMBERS) if to is o else slot
        mail.post(k, rows.at[piece, columns(slot)], rows.at[piece, columns(there)], here.member(to))

    me = here.y
    go(0, me, A, o)
    go(1, me, B, far), go(2, me, B, up), go(3, me, B, down)
    yield
    go(4, me, B, o)
    go(5, me, A, far), go(6, me, A, up), go(7, me, A, down)
    yield
    mail.take(0)
    go(8, o, A, far), go(9, o, A, up), go(10, o, A, down)
    yield
    mail.take(2)
    go(11, down, B, o)
    mail.take(3)
    go(12, up, B, o)
    yield
    mail.take(1)
    go(13, far, B, o)
    yield
    mail.take(5, 6, 7)
    yield
    mail.take(4, 8, 9, 10, 11, 12, 13)
    mail.close()


def fold_scratch():
    low = lambda *s: pltpu.VMEM(s + (SHARE,), bf16)
    return [low(7, NA), low(7, NB), low(1, NA), low(3, NB), DMA((14,)), DMA((14,))]


def fold(here, parts, total, land_a, land_b, out_a, out_b, send, recv):
    mail = Mail(send, recv)
    up, down, far, o = here.up, here.down, here.far, here.o

    def go(k, src, dst, to):
        mail.post(k, src, dst, here.member(to))

    def part(slot, piece):
        return parts[slot, piece].astype(f32)

    for k, slot in ((2, far), (0, up), (1, down)):
        go(k, parts.at[slot, A], land_a.at[k], slot)
    yield
    for k, slot, member in ((5, here.ofar, far), (3, here.oup, up), (4, here.odown, down)):
        go(k, parts.at[slot, A], land_a.at[k], member)
    for k, slot in ((10, here.ofar), (8, here.oup), (9, here.odown)):
        go(k, parts.at[slot, B], land_b.at[k - 7], o)
    go(7, parts.at[o, B], land_b.at[0], o)
    yield
    mail.take(3, 4, 5)
    out_a[0] = (
        part(o, A) + land_a[3].astype(f32) + land_a[4].astype(f32) + land_a[5].astype(f32)
    ).astype(bf16)
    go(6, out_a.at[0], land_a.at[6], o)
    yield
    for i, member in ((2, far), (0, up), (1, down)):
        mail.take(8 + i)
        out_b[i] = (part(member, B) + land_b[1 + i].astype(f32)).astype(bf16)
        go(11 + i, out_b.at[i], land_b.at[4 + i], member)
    yield
    mail.take(0, 1, 2, 6)
    total[A] = part(here.y, A) + sum(land_a[i].astype(f32) for i in (0, 1, 2, 6))
    mail.take(7, 11, 12, 13)
    total[B] = part(here.y, B) + sum(land_b[i].astype(f32) for i in (0, 4, 5, 6))
    mail.close()


def reduce_scratch():
    low = lambda *s: pltpu.VMEM(s + (SHARE,), bf16)
    return [
        low(2, 16, 32), low(16, 32), low(16, 32), low(16, 32), low(8, 32), low(2, 16, 32),
        DMA((17,)), DMA((17,)), DMA((15,)), DMA((15,)), DMA((7,)), DMA((7,)), DMA((15,)), DMA((15,)),
    ]


def reduce_all(here, share, from_twin, mine, from_plane, from_depth, whole, cs, cr, s1, r1, s2, r2, s3, r3):
    core, chip, z = here.core, here.chip, here.z
    twin, first, second, third = Mail(cs, cr), Mail(s1, r1), Mail(s2, r2), Mail(s3, r3)
    twin.post(0, share.at[1 - core], from_twin, here.twin)
    yield
    twin.take(0)
    mine[...] = (share[core].astype(f32) + from_twin[...].astype(f32)).astype(bf16)
    for k, (dx, dy) in enumerate(PLANE):
        first.post(k, mine.at[here.chip_at(dx, dy)], from_plane.at[chip], here.plane[k])
    yield
    total = mine[chip].astype(f32)
    for k, (dx, dy) in reversed(list(enumerate(PLANE))):
        first.take(k)
        total = total + from_plane[here.chip_at(4 - dx, 4 - dy)].astype(f32)
    from_depth[z] = total.astype(bf16)
    for d, device in enumerate(here.depth):
        second.post(d, from_depth.at[z], from_depth.at[z], device)
    yield
    second.take(*range(7))
    whole[core, chip] = sum(from_depth[k].astype(f32) for k in range(8)).astype(bf16)
    for d, device in enumerate(here.plane):
        third.post(d, whole.at[core, chip], whole.at[core, chip], device)
    twin.post(16, whole.at[core, chip], whole.at[core, chip], here.twin)
    yield
    for k, (dx, dy) in reversed(list(enumerate(PLANE))):
        third.take(k)
        chunk = whole.at[core, here.chip_at(4 - dx, 4 - dy)]
        twin.post(1 + k, chunk, chunk, here.twin)
    yield
    twin.take(*range(1, 17))
    for mail in (twin, first, second, third):
        mail.close()


def update(block, state, grad):
    state = state + jnp.sum(grad * grad, axis=0, keepdims=True) * (1.0 / D)
    return block - ENTITY_RATE * grad / jnp.sqrt(state), state


def draw_share(x, drawn):
    drawn = jnp.where(drawn < 0, -1, (drawn + 4 * SHARE * x) & (ROWS - 1))
    picked = flag(lax.broadcasted_iota(i32, (ROWS, ROWS), 0) == drawn)
    return nt(jnp.full((8, ROWS), 1.0, bf16), picked) * (1.0 / NEG)


def line_up(edge, ids, r):
    owner = jnp.concatenate(
        [ids[m].astype(f32)[8 * r : 8 * r + 1, :] for m in range(MEMBERS)], axis=0
    )
    mine = owner == edge.astype(f32)
    before = flag(
        lax.broadcasted_iota(i32, (LANES, LANES), 0) < lax.broadcasted_iota(i32, (LANES, LANES), 1)
    )
    found = jnp.sum(jnp.where(mine, 1.0, 0.0), axis=1, keepdims=True)
    starts = [jnp.zeros((1, 1), f32)]
    for m in range(MEMBERS):
        starts.append(starts[-1] + found[m : m + 1, :])
    place = nn(flag(mine), before) + jnp.concatenate(starts[:MEMBERS], axis=0)
    rank = jnp.where(mine, place, -1.0).astype(i32)
    return rank, jnp.where(starts[MEMBERS] > ROOM, 1.0, 0.0)


def pick(x, rank, ids, r, source_hot, relation_hot, target):
    high, low = rank >> 7, rank & (SHARE - 1)
    as_row, as_column = jnp.zeros((32, SHARE), f32), jnp.zeros((SHARE, 32), f32)
    for m in range(MEMBERS):
        low_hot = flag(lax.broadcasted_iota(i32, (SHARE, LANES), 0) == low[m : m + 1, :])
        high_hot = lax.broadcasted_iota(i32, (8, LANES), 0) == high[m : m + 1, :]
        values = ids[m].astype(f32)[8 * r : 8 * r + 8]
        values = jnp.concatenate(
            [jnp.where(high_hot, values[f : f + 1, :], 0.0) for f in range(1, 5)], axis=0
        ).astype(bf16)
        as_row = as_row + nt(values, low_hot)
        as_column = as_column + nt(low_hot, values)
    blocks = range(ROOM // SHARE)
    s = jnp.concatenate([as_row[h : h + 1, :] for h in blocks], axis=1).astype(i32)
    k = jnp.concatenate([as_row[8 + h : 9 + h, :] for h in blocks], axis=1).astype(i32)
    source_hot[...] = flag(lax.broadcasted_iota(i32, (SHARE, ROOM), 0) == s - 1)
    relation_hot[...] = flag(lax.broadcasted_iota(i32, (NREL, ROOM), 0) == k)
    wanted = as_column.astype(i32)
    for h in blocks:
        t = ((wanted[:, 16 + h : 17 + h] + 4 * x) & 7) * SHARE + wanted[:, 24 + h : 25 + h]
        target[h * SHARE : (h + 1) * SHARE, :] = jnp.broadcast_to(t, (SHARE, SHARE))


def ask(left_low, both, source_hot, relation_hot, source, operator, query, query_t):
    source[...] = nn(left_low, source_hot[...])
    operator[...] = nn(both[...], jnp.concatenate([relation_hot[...], relation_hot[...]], axis=0))
    sr, si, kr, ki = source[:H], source[H:], operator[:H], operator[H:]
    asked = jnp.concatenate([sr * kr - si * ki, sr * ki + si * kr], axis=0).astype(bf16)
    query[...] = asked
    query_t[...] = asked.T


def weigh(half, rows, often, target, query_t, weight):
    lane = lax.broadcasted_iota(i32, (ROOM, SHARE), 1)
    for b in range(2):
        start = (4 * half + 2 * b) * SHARE
        scores = nn(query_t[...], rows[:, pl.ds(start, 2 * SHARE)])
        for j in range(2):
            block = pl.ds(start + j * SHARE, SHARE)
            chance = 0.5 * jnp.tanh(0.5 * scores[:, j * SHARE : (j + 1) * SHARE]) + 0.5
            hit = lane + (start + j * SHARE) == target[...]
            value = often[0:1, block] * chance - jnp.where(hit, 1.0 - chance, 0.0)
            weight[:, block] = value.astype(bf16)


def right_parts(half, query, weight, parts):
    for b in range(2):
        first = 4 * half + 2 * b
        wide = nn(query[...], weight[:, pl.ds(first * SHARE, 2 * SHARE)]).astype(bf16)
        parts[first], parts[first + 1] = wide[:, :SHARE], wide[:, SHARE:]


def train_kernel(
    *refs,
):
    fetched, loads = refs[18:29], refs[29]
    fetch = [
        pltpu.make_async_copy(given, taken, loads.at[i])
        for i, (given, taken) in enumerate(zip(refs[:11], fetched))
    ]
    train_rounds(fetch, *fetched, *refs[11:18], *refs[30:])


def train_rounds(
    fetch,
    left, left_state, right, right_state, relations, relation_state,
    source_ids, relation_ids, target_ids, sample_ids, counts,
    left_out, left_state_out, right_out, right_state_out, relations_out, relation_state_out, missed,
    wide, ids1, ids2, drawn1, drawn2, both, rows1, rows2, often1, often2,
    source_hot1, relation_hot1, target1, source_hot2, relation_hot2, target2,
    source, operator, query, query_t, weight, parts1, parts2, total, relation_sum, left_two, left_two_state,
    out_left, in_left, out_right, in_right, out_rows, in_rows, out_states, in_states,
    id_send, id_recv, id2_send, id2_recv, move_send, move_recv,
    spread1_send, spread1_recv, spread2_send, spread2_recv,
    *folds,
):
    fold1, fold2, reduction = folds[:6], folds[6:12], folds[12:]
    for i in (6, 7, 8, 10, 2, 9, 4, 0, 1, 3, 5):
        fetch[i].start()
    here = Place()
    pair, edge = here.pair, here.edge
    barrier = pltpu.get_barrier_semaphore()
    met = here.met()
    for device in met:
        pl.semaphore_signal(barrier, inc=1, device_id=device, device_id_type=MESH)

    wide[...] = jnp.full_like(wide, -1.0)
    for i in (6, 7, 8, 10):
        fetch[i].wait()
    slot = edge * SLOTS + lax.broadcasted_iota(i32, (1, SLOTS), 1)
    for r in range(2):
        s, k, t = (x[r : r + 1, :] for x in (source_ids, relation_ids, target_ids))
        owner = jnp.where(slot < counts[0:1, r : r + 1], s >> 7, -1)
        for row, value in enumerate((owner, (s & 127) + 1, k, t >> 7, t & 127)):
            wide[8 * r + row : 8 * r + row + 1, 0:SLOTS] = value.astype(f32)
    ids1[edge] = wide[...].astype(bf16)
    fetch[2].wait()
    rows1[:, columns(here.y)] = right[...].astype(bf16)
    pl.semaphore_wait(barrier, len(met))

    id_mail, id2_mail, moves = Mail(id_send, id_recv), Mail(id2_send, id2_recv), Mail(move_send, move_recv)
    ahead, behind = here.group(1), here.group(-1)
    gather = spread(here, rows1, Mail(spread1_send, spread1_recv))
    next(gather)
    for d, device in enumerate(here.peers):
        id_mail.post(d, ids1.at[edge], ids1.at[edge], device)
    next(gather)
    moves.post(0, ids1.at[edge], ids2.at[edge], ahead)
    fetch[9].wait()
    drawn1[...] = jnp.full_like(drawn1, -1)
    drawn1[:, 0:NEG] = sample_ids[...]
    for j in range(8):
        drawn2[0, j : j + 1, :] = drawn1[1:2, j * SHARE : (j + 1) * SHARE]
    moves.post(1, drawn2.at[0], drawn2.at[1], ahead)
    often1[...] = draw_share(here.x, drawn1[0:1, :])
    fetch[4].wait()
    high = relations[...].astype(bf16)
    both[:, 0:NREL] = high
    both[:, NREL:] = (relations[...] - high.astype(f32)).astype(bf16)
    next(gather)
    id_mail.take(*range(7))
    rank, late1 = line_up(edge, ids1, 0)
    next(gather)
    next(gather)
    pick(here.x, rank, ids1, 0, source_hot1, relation_hot1, target1)
    fetch[0].wait()
    ask(left[...].astype(bf16), both, source_hot1, relation_hot1, source, operator, query, query_t)
    moves.take(0)
    for d, device in enumerate(here.peers):
        id2_mail.post(d, ids2.at[edge], ids2.at[edge], device)
    next(gather)

    weigh(0, rows1, often1, target1, query_t, weight)
    right_parts(0, query, weight, parts1)
    folding = fold(here, parts1, total, *fold1)
    next(folding)
    next(gather, None)
    weigh(1, rows1, often1, target1, query_t, weight)
    right_parts(1, query, weight, parts1)
    next(folding)
    for i in (1, 3, 5):
        fetch[i].wait()
    grad = nt(rows1[...], weight[...])
    gr, gi, kr, ki = grad[:H], grad[H:], operator[:H], operator[H:]
    back = jnp.concatenate([gr * kr + gi * ki, gi * kr - gr * ki], axis=0).astype(bf16)
    left_sum = nt(back, source_hot1[...])
    block, state = update(left[...], left_state[...], left_sum)
    out_left[...] = block.astype(bf16)
    out_states[0] = jnp.broadcast_to(state, (8, SHARE))
    moves.post(2, out_left, in_left, here.group(2))
    moves.post(3, out_states.at[0], in_states.at[0], here.group(2))
    next(folding)
    sr, si = source[:H], source[H:]
    back = jnp.concatenate([gr * sr + gi * si, gi * sr - gr * si], axis=0).astype(bf16)
    for c in range(2):
        relation_sum[c] = nt(back, relation_hot1[c * SHARE : (c + 1) * SHARE, :])
    next(folding)
    id2_mail.take(*range(7))
    rank, late2 = line_up(edge, ids2, 1)
    pick(here.x, rank, ids2, 1, source_hot2, relation_hot2, target2)
    moves.take(1)
    often2[...] = draw_share(
        here.x, jnp.concatenate([drawn2[1, j : j + 1, :] for j in range(8)], axis=1)
    )
    next(folding, None)
    right_two, right_two_state = update(right[...], right_state[...], total[...])
    rows2[:, columns(here.y)] = right_two.astype(bf16)
    gather = spread(here, rows2, Mail(spread2_send, spread2_recv))
    next(gather)
    next(gather)
    moves.take(2, 3)
    left_two[...] = in_left[...].astype(f32)
    left_two_state[...] = in_states[0, 0:1, :]
    ask(in_left[...], both, source_hot2, relation_hot2, source, operator, query, query_t)
    for _ in range(4):
        next(gather)

    weigh(0, rows2, often2, target2, query_t, weight)
    right_parts(0, query, weight, parts2)
    folding = fold(here, parts2, total, *fold2)
    next(folding)
    half = 4 * SHARE
    grad = nt(rows2[:, :half], weight[:, :half])
    next(gather, None)
    weigh(1, rows2, often2, target2, query_t, weight)
    grad = grad + nt(rows2[:, half:], weight[:, half:])
    gr, gi, sr, si = grad[:H], grad[H:], source[:H], source[H:]
    back = jnp.concatenate([gr * sr + gi * si, gi * sr - gr * si], axis=0).astype(bf16)
    last = jnp.broadcast_to(late1 + late2, (512 - D, SHARE))
    share, whole = reduction[0], reduction[5]
    reducing = reduce_all(here, *reduction)
    for c in (1 - here.core, here.core):
        hot = relation_hot2[columns(c), :]
        full = jnp.concatenate([relation_sum[c] + nt(back, hot), last], axis=0)
        share[c] = full.reshape(16, 32, SHARE).astype(bf16)
        if c is not here.core:
            next(reducing)
    right_parts(1, query, weight, parts2)
    next(reducing)
    next(folding)
    kr, ki = operator[:H], operator[H:]
    back = jnp.concatenate([gr * kr + gi * ki, gi * kr - gr * ki], axis=0).astype(bf16)
    left_sum = nt(back, source_hot2[...])
    block, state = update(left_two[...], left_two_state[...], left_sum)
    out_rows[0] = block.astype(bf16)
    out_states[1] = jnp.broadcast_to(state, (8, SHARE))
    moves.post(4, out_rows.at[0], in_rows.at[0], behind)
    moves.post(5, out_states.at[1], in_states.at[1], behind)
    next(folding)
    next(reducing)
    next(folding)
    next(reducing)
    next(folding, None)
    block, state = update(right_two, right_two_state, total[...])
    out_rows[1] = block.astype(bf16)
    out_states[2] = jnp.broadcast_to(state, (8, SHARE))
    moves.post(6, out_rows.at[1], in_rows.at[1], behind)
    moves.post(7, out_states.at[2], in_states.at[2], behind)
    moves.take(4, 5)
    left_out[...] = in_rows[0].astype(f32)
    left_state_out[...] = in_states[1, 0:1, :]
    next(reducing)

    def relation_update(c):
        half = columns(c)
        grad = whole[c].reshape(512, SHARE)[:D].astype(f32)
        state = relation_state[:, half] + grad * grad
        relation_state_out[:, half] = state
        relations_out[:, half] = relations[:, half] - RELATION_RATE * grad / jnp.sqrt(state)

    relation_update(here.core)
    missed[...] = whole[here.core].reshape(512, SHARE)[D : D + 16].astype(f32)[0:1, 0:1].astype(i32)
    moves.take(6, 7)
    right_out[...] = in_rows[1].astype(f32)
    right_state_out[...] = in_states[2, 0:1, :]
    next(reducing, None)
    relation_update(1 - here.core)
    for mail in (id_mail, id2_mail, moves):
        mail.close()


def train(*args):
    table = jax.ShapeDtypeStruct((D, NREL), f32)
    block = jax.ShapeDtypeStruct((D, SHARE), f32)
    row = jax.ShapeDtypeStruct((1, SHARE), f32)
    vmem = pltpu.VMEM
    low = vmem((D, SHARE), bf16)
    hots = [vmem((SHARE, ROOM), bf16), vmem((NREL, ROOM), bf16), vmem((ROOM, SHARE), i32)]
    return pl.pallas_call(
        train_kernel,
        out_shape=(block, row, block, row, table, table, jax.ShapeDtypeStruct((1, 1), i32)),
        in_specs=[pl.BlockSpec(memory_space=pl.ANY)] * 11,
        out_specs=(VMEM,) * 7,
        scratch_shapes=[
            *(vmem(x.shape, x.dtype) for x in args), DMA((11,)),
            vmem((16, LANES), f32),
            vmem((MEMBERS, 16, LANES), bf16), vmem((MEMBERS, 16, LANES), bf16),
            vmem((2, ROWS), i32), vmem((2, 8, SHARE), i32),
            vmem((D, 2 * NREL), bf16),
            vmem((D, ROWS), bf16), vmem((D, ROWS), bf16),
            vmem((8, ROWS), f32), vmem((8, ROWS), f32),
            *hots, *hots,
            vmem((D, ROOM), f32), vmem((D, ROOM), f32),
            vmem((D, ROOM), bf16), vmem((ROOM, D), bf16), vmem((ROOM, ROWS), bf16),
            vmem((MEMBERS, D, SHARE), bf16), vmem((MEMBERS, D, SHARE), bf16),
            vmem((D, SHARE), f32), vmem((2, D, SHARE), f32),
            vmem((D, SHARE), f32), vmem((1, SHARE), f32),
            low, low, low, low, vmem((2, D, SHARE), bf16), vmem((2, D, SHARE), bf16),
            vmem((3, 8, SHARE), f32), vmem((3, 8, SHARE), f32),
            DMA((7,)), DMA((7,)), DMA((7,)), DMA((7,)), DMA((8,)), DMA((8,)),
            DMA((14,)), DMA((14,)), DMA((14,)), DMA((14,)),
            *fold_scratch(), *fold_scratch(), *reduce_scratch(),
        ],
        compiler_params=pltpu.CompilerParams(
            collective_id=1, has_side_effects=True, vmem_limit_bytes=56 * 2**20
        ),
        name="train_two_rounds",
    )(*args)


def settle_kernel(*refs):
    for given, out in zip(refs[:6], refs[6:]):
        out[...] = given[...]


def settle(done):
    left, left_sums, right, right_sums, table, table_state = done
    flat = (left.T, left_sums.reshape(1, SHARE), right.T, right_sums.reshape(1, SHARE), table.T, table_state.T)
    left, left_sums, right, right_sums, table, table_state = pl.pallas_call(
        settle_kernel,
        out_shape=tuple(jax.ShapeDtypeStruct(x.shape, x.dtype) for x in flat),
        in_specs=[VMEM] * 6,
        out_specs=(VMEM,) * 6,
        name="settle",
    )(*flat)
    return (
        left.T, left_sums.reshape(SHARE), right.T, right_sums.reshape(SHARE), table.T, table_state.T,
    )


def body(
    left_block, left_state, right_block, right_state, relations, relation_state,
    source_ids, relation_ids, target_ids, sample_ids, bucket_counts,
):
    left, left_sums, right, right_sums, table, table_state, missed = train(
        left_block.T, left_state.reshape(1, SHARE), right_block.T, right_state.reshape(1, SHARE),
        relations.T, relation_state.T,
        source_ids, relation_ids, target_ids, sample_ids, bucket_counts.T,
    )
    fast = (
        left.T, left_sums.reshape(SHARE), right.T, right_sums.reshape(SHARE), table.T, table_state.T,
    )
    done = lax.cond(
        missed[0, 0] > 0,
        lambda *args: any_spread(*args[6:]),
        lambda *args: args[:6],
        *fast,
        left_block, left_state, right_block, right_state, relations, relation_state,
        source_ids, relation_ids, target_ids, sample_ids, bucket_counts,
    )
    return settle(done)


def solution(mesh):
    block, row = P(("pair", "edge"), None), P(("pair", "edge"))
    ids, group = P(None, ("pair", "edge")), P(None, "pair")
    return jax.shard_map(
        body,
        mesh=mesh,
        in_specs=(block, row, block, row, P(), P(), ids, ids, ids, group, group),
        out_specs=(block, row, block, row, P(), P()),
        check_vma=False,
    )
```

```python
import functools

import jax
import jax.numpy as jnp
from jax import lax
from jax.experimental import pallas as pl
from jax.experimental.pallas import tpu as pltpu
from jax.sharding import PartitionSpec as P

ENTITY_RATE = 0.3
RELATION_RATE = 0.3
D, H = 400, 200
SHARE = 128
MEMBERS = 8
GROUPS = 32
ROWS = SHARE * MEMBERS
NREL = 256
SLOTS = 500
LANES = 512
NEG = 1000
ROOM = 640
MESH = pl.DeviceIdType.MESH
SMEM = pl.BlockSpec(memory_space=pltpu.SMEM)
CHUNK = 256
VMEM = pl.BlockSpec(memory_space=pltpu.VMEM)
DMA = pltpu.SemaphoreType.DMA
f32, bf16, i32 = jnp.float32, jnp.bfloat16, jnp.int32
NA, NB = 208, 192
A, B = pl.ds(0, NA), pl.ds(NA, NB)
PLANE = sorted(
    ((dx, dy) for dx in range(4) for dy in range(4) if dx or dy),
    key=lambda o: -min(o[0], 4 - o[0]) - min(o[1], 4 - o[1]),
)
DEPTH = (4, 3, 5, 2, 6, 1, 7)


def remote(src, dst, send, recv, pair, edge):
    return pltpu.make_async_remote_copy(
        src_ref=src, dst_ref=dst, send_sem=send, recv_sem=recv,
        device_id=(pair, edge), device_id_type=MESH,
    )


def greet(devices):
    barrier = pltpu.get_barrier_semaphore()
    for device in devices:
        pl.semaphore_signal(barrier, inc=1, device_id=device, device_id_type=MESH)
    pl.semaphore_wait(barrier, len(devices))


def members(pair, edge):
    return [(pair, lax.rem(edge + d, MEMBERS)) for d in range(1, MEMBERS)]


def gather_kernel(right, source, relation, target, rows, ids, wide, low, send, recv):
    pair, edge = lax.axis_index("pair"), lax.axis_index("edge")
    peers = members(pair, edge)
    wide[...] = jnp.full_like(wide, -1.0)
    for r in range(2):
        s, k, t = (x[r : r + 1, :] for x in (source, relation, target))
        for row, value in enumerate((s >> 7, (s & 127) + 1, k, t >> 7, t & 127)):
            wide[8 * r + row : 8 * r + row + 1, 0:SLOTS] = value.astype(f32)
    ids[edge] = wide[...].astype(bf16)
    rows[edge] = right[...].astype(bf16)
    greet(peers)
    copies = []
    for d, peer in enumerate(peers):
        for j, ref in enumerate((ids, rows)):
            copy = remote(ref.at[edge], ref.at[edge], send.at[j, d], recv.at[j, d], *peer)
            copy.start()
            copies.append(copy)
    for copy in copies:
        copy.wait()


def gather(right, source, relation, target):
    return pl.pallas_call(
        gather_kernel,
        out_shape=(
            jax.ShapeDtypeStruct((MEMBERS, D, SHARE), bf16),
            jax.ShapeDtypeStruct((MEMBERS, 16, LANES), bf16),
        ),
        in_specs=[VMEM] * 4,
        out_specs=(VMEM, VMEM),
        scratch_shapes=[
            pltpu.VMEM((16, LANES), f32),
            pltpu.VMEM((16, LANES), bf16),
            pltpu.SemaphoreType.DMA((2, MEMBERS - 1)),
            pltpu.SemaphoreType.DMA((2, MEMBERS - 1)),
        ],
        compiler_params=pltpu.CompilerParams(collective_id=2, has_side_effects=True),
        name="gather_right",
    )(right, source, relation, target)


def chunks_kernel(
    r, rows, ids, samples, counts, left, left_state, relations, relation_in,
    right_grad, left_out, left_state_out, relation_out,
    table, table_t, rank, often, both, right_sum, left_sum,
):
    edge = lax.axis_index("edge")
    left_low = left[...].astype(bf16)
    high = relations[...].astype(bf16)
    both[:, 0:NREL] = high
    both[:, NREL:] = (relations[...] - high.astype(f32)).astype(bf16)
    for m in range(MEMBERS):
        table_t[:, m * SHARE : (m + 1) * SHARE] = rows[m]
        table[m * SHARE : (m + 1) * SHARE, :] = rows[m].T
    picked = flag(lax.broadcasted_iota(i32, (ROWS, NEG), 0) == samples[r : r + 1, :])
    often[...] = nn(picked, jnp.full((NEG, SHARE), 1.0, bf16)) * (1.0 / NEG)

    owner = jnp.concatenate(
        [ids[m].astype(f32)[8 * r : 8 * r + 1, :] for m in range(MEMBERS)], axis=0
    )
    lane = lax.broadcasted_iota(i32, (MEMBERS, LANES), 1)
    slot = lax.broadcasted_iota(i32, (MEMBERS, LANES), 0) * SLOTS + lane
    mine = (owner == edge.astype(f32)) & (slot < counts[r, 0])
    mark = flag(mine)
    before = flag(
        lax.broadcasted_iota(i32, (LANES, LANES), 0) < lax.broadcasted_iota(i32, (LANES, LANES), 1)
    )
    found = jnp.sum(jnp.where(mine, 1.0, 0.0), axis=1, keepdims=True)
    starts = [jnp.zeros((1, 1), f32)]
    for m in range(MEMBERS):
        starts.append(starts[-1] + found[m : m + 1, :])
    place = nn(mark, before) + jnp.concatenate(starts[:MEMBERS], axis=0)
    rank[...] = jnp.where(mine, place, -1.0).astype(i32)
    total = jnp.sum(found).astype(i32)

    right_sum[...] = jnp.zeros_like(right_sum)
    left_sum[...] = jnp.zeros_like(left_sum)
    relation_out[...] = relation_in[...]

    def chunk(c, carry):
        want = lax.broadcasted_iota(i32, (CHUNK, LANES), 0) + c * CHUNK
        found = jnp.zeros((16, CHUNK), f32)
        for m in range(MEMBERS):
            found = found + nt(ids[m], flag(rank[m : m + 1, :] == want))
        found = found[8 * r : 8 * r + 8, :].astype(i32)
        s, k = found[1:2, :] - 1, found[2:3, :]
        t = found[3:4, :] * SHARE + found[4:5, :]
        source_hot = flag(lax.broadcasted_iota(i32, (SHARE, CHUNK), 0) == s)
        relation_hot = flag(lax.broadcasted_iota(i32, (NREL, CHUNK), 0) == k)
        source = nn(left_low, source_hot)
        operator = nn(both[...], jnp.concatenate([relation_hot, relation_hot], axis=0))
        sr, si, kr, ki = source[:H], source[H:], operator[:H], operator[H:]
        query = jnp.concatenate([sr * kr - si * ki, sr * ki + si * kr], axis=0).astype(bf16)
        scores = nn(table[...], query)
        chance = 0.5 * jnp.tanh(0.5 * scores) + 0.5
        hit = lax.broadcasted_iota(i32, (ROWS, CHUNK), 0) == t
        spread = jnp.concatenate([often[...]] * (CHUNK // SHARE), axis=1)
        weight = (spread * chance - jnp.where(hit, 1.0 - chance, 0.0)).astype(bf16)
        grad = nn(table_t[...], weight)
        right_sum[...] += nt(query, weight)
        gr, gi = grad[:H], grad[H:]
        grad_source = jnp.concatenate([gr * kr + gi * ki, gi * kr - gr * ki], axis=0)
        grad_operator = jnp.concatenate([gr * sr + gi * si, gi * sr - gr * si], axis=0)
        left_sum[...] += nt(grad_source.astype(bf16), source_hot)
        relation_out[...] += nt(grad_operator.astype(bf16), relation_hot)
        return carry

    lax.fori_loop(0, (total + (CHUNK - 1)) // CHUNK, chunk, 0)
    for m in range(MEMBERS):
        right_grad[m] = right_sum[:, m * SHARE : (m + 1) * SHARE].astype(bf16)
    block, state = update(left[...], left_state[...], left_sum[...])
    left_out[...] = block
    left_state_out[...] = state


def train_chunks(r, rows, ids, samples, counts, left, left_state, relations, relation_in):
    return pl.pallas_call(
        functools.partial(chunks_kernel, r),
        out_shape=(
            jax.ShapeDtypeStruct((MEMBERS, D, SHARE), bf16),
            jax.ShapeDtypeStruct((D, SHARE), f32),
            jax.ShapeDtypeStruct((1, SHARE), f32),
            jax.ShapeDtypeStruct((D, NREL), f32),
        ),
        in_specs=[VMEM, VMEM, VMEM, SMEM, VMEM, VMEM, VMEM, VMEM],
        out_specs=(VMEM,) * 4,
        scratch_shapes=[
            pltpu.VMEM((ROWS, D), bf16),
            pltpu.VMEM((D, ROWS), bf16),
            pltpu.VMEM((MEMBERS, LANES), i32),
            pltpu.VMEM((ROWS, SHARE), f32),
            pltpu.VMEM((D, 2 * NREL), bf16),
            pltpu.VMEM((D, ROWS), f32),
            pltpu.VMEM((D, SHARE), f32),
        ],
        compiler_params=pltpu.CompilerParams(vmem_limit_bytes=48 * 2**20),
        name="train_chunks",
    )(rows, ids, samples, counts, left, left_state, relations, relation_in)


def send_parts(parts, landing, send, recv, edge, peers):
    copies = []
    for d, peer in enumerate(peers):
        copy = remote(parts.at[peer[1]], landing.at[edge], send.at[d], recv.at[d], *peer)
        copy.start()
        copies.append(copy)
    return copies


def total_of(parts, landing, copies, edge):
    total = parts[edge].astype(f32)
    for d, copy in enumerate(copies):
        copy.wait_recv()
        total = total + landing[lax.rem(edge + (MEMBERS - 1 - d), MEMBERS)].astype(f32)
    return total


def exchange_kernel(
    parts, right, right_state, left, left_state,
    rows, right_out, right_state_out, left_out, left_state_out,
    landing, out_left, out_right, in_left, in_right, out_states, in_states,
    part_send, part_recv, row_send, row_recv, move_send, move_recv,
):
    pair, edge = lax.axis_index("pair"), lax.axis_index("edge")
    peers = members(pair, edge)
    ahead = (lax.rem(pair + 1, GROUPS), edge)
    behind = (lax.rem(pair + GROUPS - 1, GROUPS), edge)
    out_left[...] = left[...].astype(bf16)
    out_states[0] = jnp.broadcast_to(left_state[...], (8, SHARE))
    greet(peers + [ahead, behind])
    copies = send_parts(parts, landing, part_send, part_recv, edge, peers)
    moves = [
        remote(out_left, in_left, move_send.at[0], move_recv.at[0], *ahead),
        remote(out_states.at[0], in_states.at[0], move_send.at[1], move_recv.at[1], *ahead),
        remote(out_right, in_right, move_send.at[2], move_recv.at[2], *behind),
        remote(out_states.at[1], in_states.at[1], move_send.at[3], move_recv.at[3], *behind),
    ]
    moves[0].start()
    moves[1].start()
    grad = total_of(parts, landing, copies, edge)
    block, state = update(right[...], right_state[...], grad)
    out_right[...] = block.astype(bf16)
    out_states[1] = jnp.broadcast_to(state, (8, SHARE))
    moves[2].start()
    moves[3].start()
    moves[2].wait_recv()
    rows[edge] = in_right[...]
    gathers = []
    for d, peer in enumerate(peers):
        copy = remote(in_right, rows.at[edge], row_send.at[d], row_recv.at[d], *peer)
        copy.start()
        gathers.append(copy)
    right_out[...] = in_right[...].astype(f32)
    moves[3].wait_recv()
    right_state_out[...] = in_states[1, 0:1, :]
    moves[0].wait_recv()
    left_out[...] = in_left[...].astype(f32)
    moves[1].wait_recv()
    left_state_out[...] = in_states[0, 0:1, :]
    for copy in gathers:
        copy.wait_recv()
    for copy in copies + moves + gathers:
        copy.wait_send()


def exchange(parts, right, right_state, left, left_state):
    block = jax.ShapeDtypeStruct((D, SHARE), f32)
    row = jax.ShapeDtypeStruct((1, SHARE), f32)
    low = pltpu.VMEM((D, SHARE), bf16)
    dma = pltpu.SemaphoreType.DMA
    return pl.pallas_call(
        exchange_kernel,
        out_shape=(jax.ShapeDtypeStruct((MEMBERS, D, SHARE), bf16), block, row, block, row),
        in_specs=[VMEM] * 5,
        out_specs=(VMEM,) * 5,
        scratch_shapes=[
            pltpu.VMEM((MEMBERS, D, SHARE), bf16),
            low, low, low, low,
            pltpu.VMEM((2, 8, SHARE), f32),
            pltpu.VMEM((2, 8, SHARE), f32),
            dma((MEMBERS - 1,)), dma((MEMBERS - 1,)),
            dma((MEMBERS - 1,)), dma((MEMBERS - 1,)),
            dma((4,)), dma((4,)),
        ],
        compiler_params=pltpu.CompilerParams(
            collective_id=3, has_side_effects=True, vmem_limit_bytes=32 * 2**20
        ),
        name="exchange_rows",
    )(parts, right, right_state, left, left_state)


def finish_kernel(
    parts, right, right_state, relation_grad, relations, relation_state,
    right_out, right_state_out, relations_out, relation_state_out,
    landing, share, share_in, tiles, tiles_in, quad, whole,
    part_send, part_recv, s1, r1, s2, r2, s3, r3, s4, r4, s5, r5,
):
    pair, edge = lax.axis_index("pair"), lax.axis_index("edge")
    z, q = pair // 4, lax.rem(pair, 4)
    peers = members(pair, edge)
    depth = [(lax.rem(z + d, 8) * 4 + q, edge) for d in range(1, 8)]
    flat = [(z * 4 + lax.rem(q + d, 4), edge) for d in range(1, 4)]
    share[...] = jnp.zeros_like(share)
    grads = relation_grad[...].astype(bf16)
    stacked = jnp.concatenate(
        [grads[:, 0:SHARE], grads[:, SHARE:], jnp.zeros((224, SHARE), bf16)], axis=0
    )
    for m in range(MEMBERS):
        share[m] = stacked[m * SHARE : (m + 1) * SHARE, :]
    greet(peers + depth + flat)
    first = send_parts(share, share_in, s1, r1, edge, peers)
    copies = send_parts(parts, landing, part_send, part_recv, edge, peers)
    done = first + copies
    sums = total_of(share, share_in, first, edge).astype(bf16)
    for k in range(8):
        tiles[k] = sums[16 * k : 16 * k + 16, :]
    second = []
    for d, peer in enumerate(depth):
        copy = remote(
            tiles.at[lax.rem(z + d + 1, 8)], tiles_in.at[z], s2.at[d], r2.at[d], *peer
        )
        copy.start()
        second.append(copy)
    total = tiles[z].astype(f32)
    for d, copy in enumerate(second):
        copy.wait_recv()
        total = total + tiles_in[lax.rem(z + 7 - d, 8)].astype(f32)
    quad[q] = total
    third = []
    for d, peer in enumerate(flat):
        copy = remote(quad.at[q], quad.at[q], s3.at[d], r3.at[d], *peer)
        copy.start()
        third.append(copy)
    for copy in third:
        copy.wait_recv()
    rows = pl.ds(pl.multiple_of(z * 16, 16), 16)
    whole[edge, rows, :] = (quad[0] + quad[1] + quad[2] + quad[3]).astype(bf16)
    fourth = []
    for d, peer in enumerate(depth):
        here = whole.at[edge, rows, :]
        copy = remote(here, here, s4.at[d], r4.at[d], *peer)
        copy.start()
        fourth.append(copy)

    grad = total_of(parts, landing, copies, edge)
    block, state = update(right[...], right_state[...], grad)
    right_out[...] = block
    right_state_out[...] = state

    for copy in fourth:
        copy.wait_recv()
    fifth = []
    for d, peer in enumerate(peers):
        copy = remote(whole.at[edge], whole.at[edge], s5.at[d], r5.at[d], *peer)
        copy.start()
        fifth.append(copy)
    for copy in fifth:
        copy.wait_recv()
    gathered = whole[...].reshape(MEMBERS * SHARE, SHARE)
    grad = jnp.concatenate([gathered[0:D], gathered[D : 2 * D]], axis=1).astype(f32)
    state = relation_state[...] + grad * grad
    relation_state_out[...] = state
    relations_out[...] = relations[...] - RELATION_RATE * grad / jnp.sqrt(state)
    for copy in done + second + third + fourth + fifth:
        copy.wait_send()


def finish(parts, right, right_state, relation_grad, relations, relation_state):
    dma = pltpu.SemaphoreType.DMA
    table = jax.ShapeDtypeStruct((D, NREL), f32)
    return pl.pallas_call(
        finish_kernel,
        out_shape=(
            jax.ShapeDtypeStruct((D, SHARE), f32), jax.ShapeDtypeStruct((1, SHARE), f32),
            table, table,
        ),
        in_specs=[VMEM] * 6,
        out_specs=(VMEM,) * 4,
        scratch_shapes=[
            pltpu.VMEM((MEMBERS, D, SHARE), bf16),
            pltpu.VMEM((MEMBERS, SHARE, SHARE), bf16),
            pltpu.VMEM((MEMBERS, SHARE, SHARE), bf16),
            pltpu.VMEM((8, 16, SHARE), bf16),
            pltpu.VMEM((8, 16, SHARE), bf16),
            pltpu.VMEM((4, 16, SHARE), f32),
            pltpu.VMEM((MEMBERS, SHARE, SHARE), bf16),
            dma((7,)), dma((7,)), dma((7,)), dma((7,)), dma((7,)), dma((7,)),
            dma((3,)), dma((3,)), dma((7,)), dma((7,)), dma((7,)), dma((7,)),
        ],
        compiler_params=pltpu.CompilerParams(
            collective_id=4, has_side_effects=True, vmem_limit_bytes=32 * 2**20
        ),
        name="finish_right_and_relations",
    )(parts, right, right_state, relation_grad, relations, relation_state)


def any_spread(
    left_block, left_state, right_block, right_state, relations, relation_state,
    source_ids, relation_ids, target_ids, sample_ids, bucket_counts,
):
    left, right = left_block.T, right_block.T
    left_sums, right_sums = left_state.reshape(1, SHARE), right_state.reshape(1, SHARE)
    operators, operator_state = relations.T, relation_state.T
    rows, ids = gather(right, source_ids, relation_ids, target_ids)
    grad = jnp.zeros((D, NREL), f32)
    parts, left, left_sums, grad = train_chunks(
        0, rows, ids, sample_ids, bucket_counts, left, left_sums, operators, grad
    )
    rows, right, right_sums, left, left_sums = exchange(parts, right, right_sums, left, left_sums)
    parts, left, left_sums, grad = train_chunks(
        1, rows, ids, sample_ids, bucket_counts, left, left_sums, operators, grad
    )
    right, right_sums, operators, operator_state = finish(
        parts, right, right_sums, grad, operators, operator_state
    )
    return (
        left.T, left_sums.reshape(SHARE), right.T, right_sums.reshape(SHARE),
        operators.T, operator_state.T,
    )


def nt(a, b):
    return lax.dot_general(a, b, (((1,), (1,)), ((), ())), preferred_element_type=f32)


def nn(a, b):
    return jnp.dot(a, b, preferred_element_type=f32)


def flag(condition):
    return jnp.where(condition, 1.0, 0.0).astype(bf16)


def columns(member):
    return pl.ds(pl.multiple_of(member * SHARE, SHARE), SHARE)


class Mail:
    def __init__(self, send, recv):
        self.send, self.recv, self.sent = send, recv, {}

    def post(self, k, src, dst, device):
        copy = pltpu.make_async_remote_copy(
            src_ref=src, dst_ref=dst, send_sem=self.send.at[k], recv_sem=self.recv.at[k],
            device_id=device, device_id_type=MESH,
        )
        copy.start()
        self.sent[k] = copy

    def take(self, *keys):
        for k in keys:
            self.sent[k].wait_recv()

    def close(self):
        for copy in self.sent.values():
            copy.wait_send()


class Place:
    def __init__(self):
        pair, edge = lax.axis_index("pair"), lax.axis_index("edge")
        self.pair, self.edge = pair, edge
        self.x, self.y = edge // 4, lax.rem(edge, 4)
        self.z, self.core = pair // 4, lax.rem(pair, 2)
        self.chip = lax.rem(pair // 2, 2) * 8 + edge
        self.up, self.far, self.down = (lax.rem(self.y + d, 4) for d in (1, 2, 3))
        self.o, self.oup, self.ofar, self.odown = (4 + v for v in (self.y, self.up, self.far, self.down))
        self.twin = (pair + 1 - 2 * self.core, edge)
        self.plane = []
        for dx, dy in PLANE:
            c = self.chip_at(dx, dy)
            self.plane.append((self.z * 4 + (c // 8) * 2 + self.core, lax.rem(c, 8)))
        self.depth = [(lax.rem(pair + 4 * d, GROUPS), edge) for d in DEPTH]
        self.peers = [(pair, lax.rem(edge + d, MEMBERS)) for d in range(1, MEMBERS)]

    def group(self, distance):
        return (lax.rem(self.pair + distance + GROUPS, GROUPS), self.edge)

    def chip_at(self, dx, dy):
        return lax.rem(self.chip // 4 + dx, 4) * 4 + lax.rem(self.y + dy, 4)

    def member(self, slot):
        return (self.pair, lax.rem(slot + 4 * self.x, MEMBERS))

    def met(self):
        return self.depth + self.plane + [self.twin] + [self.group(d) for d in (1, -1, 2, -2)]


def spread(here, rows, mail):
    up, down, far, o = here.up, here.down, here.far, here.o

    def go(k, slot, piece, to):
        there = lax.rem(slot + 4, MEMBERS) if to is o else slot
        mail.post(k, rows.at[piece, columns(slot)], rows.at[piece, columns(there)], here.member(to))

    me = here.y
    go(0, me, A, o)
    go(1, me, B, far), go(2, me, B, up), go(3, me, B, down)
    yield
    go(4, me, B, o)
    go(5, me, A, far), go(6, me, A, up), go(7, me, A, down)
    yield
    mail.take(0)
    go(8, o, A, far), go(9, o, A, up), go(10, o, A, down)
    yield
    mail.take(2)
    go(11, down, B, o)
    mail.take(3)
    go(12, up, B, o)
    yield
    mail.take(1)
    go(13, far, B, o)
    yield
    mail.take(5, 6, 7)
    yield
    mail.take(4, 8, 9, 10, 11, 12, 13)
    mail.close()


def fold_scratch():
    low = lambda *s: pltpu.VMEM(s + (SHARE,), bf16)
    return [low(7, NA), low(7, NB), low(1, NA), low(3, NB), DMA((14,)), DMA((14,))]


def fold(here, parts, total, land_a, land_b, out_a, out_b, send, recv):
    mail = Mail(send, recv)
    up, down, far, o = here.up, here.down, here.far, here.o

    def go(k, src, dst, to):
        mail.post(k, src, dst, here.member(to))

    def part(slot, piece):
        return parts[slot, piece].astype(f32)

    for k, slot in ((2, far), (0, up), (1, down)):
        go(k, parts.at[slot, A], land_a.at[k], slot)
    yield
    for k, slot, member in ((5, here.ofar, far), (3, here.oup, up), (4, here.odown, down)):
        go(k, parts.at[slot, A], land_a.at[k], member)
    for k, slot in ((10, here.ofar), (8, here.oup), (9, here.odown)):
        go(k, parts.at[slot, B], land_b.at[k - 7], o)
    go(7, parts.at[o, B], land_b.at[0], o)
    yield
    mail.take(3, 4, 5)
    out_a[0] = (
        part(o, A) + land_a[3].astype(f32) + land_a[4].astype(f32) + land_a[5].astype(f32)
    ).astype(bf16)
    go(6, out_a.at[0], land_a.at[6], o)
    yield
    for i, member in ((2, far), (0, up), (1, down)):
        mail.take(8 + i)
        out_b[i] = (part(member, B) + land_b[1 + i].astype(f32)).astype(bf16)
        go(11 + i, out_b.at[i], land_b.at[4 + i], member)
    yield
    mail.take(0, 1, 2, 6)
    total[A] = part(here.y, A) + sum(land_a[i].astype(f32) for i in (0, 1, 2, 6))
    mail.take(7, 11, 12, 13)
    total[B] = part(here.y, B) + sum(land_b[i].astype(f32) for i in (0, 4, 5, 6))
    mail.close()


def reduce_scratch():
    low = lambda *s: pltpu.VMEM(s + (SHARE,), bf16)
    return [
        low(2, 16, 32), low(16, 32), low(16, 32), low(16, 32), low(8, 32), low(2, 16, 32),
        DMA((17,)), DMA((17,)), DMA((15,)), DMA((15,)), DMA((7,)), DMA((7,)), DMA((15,)), DMA((15,)),
    ]


def reduce_all(here, share, from_twin, mine, from_plane, from_depth, whole, cs, cr, s1, r1, s2, r2, s3, r3):
    core, chip, z = here.core, here.chip, here.z
    twin, first, second, third = Mail(cs, cr), Mail(s1, r1), Mail(s2, r2), Mail(s3, r3)
    twin.post(0, share.at[1 - core], from_twin, here.twin)
    yield
    twin.take(0)
    mine[...] = (share[core].astype(f32) + from_twin[...].astype(f32)).astype(bf16)
    for k, (dx, dy) in enumerate(PLANE):
        first.post(k, mine.at[here.chip_at(dx, dy)], from_plane.at[chip], here.plane[k])
    yield
    total = mine[chip].astype(f32)
    for k, (dx, dy) in reversed(list(enumerate(PLANE))):
        first.take(k)
        total = total + from_plane[here.chip_at(4 - dx, 4 - dy)].astype(f32)
    from_depth[z] = total.astype(bf16)
    for d, device in enumerate(here.depth):
        second.post(d, from_depth.at[z], from_depth.at[z], device)
    yield
    second.take(*range(7))
    whole[core, chip] = sum(from_depth[k].astype(f32) for k in range(8)).astype(bf16)
    for d, device in enumerate(here.plane):
        third.post(d, whole.at[core, chip], whole.at[core, chip], device)
    twin.post(16, whole.at[core, chip], whole.at[core, chip], here.twin)
    yield
    for k, (dx, dy) in reversed(list(enumerate(PLANE))):
        third.take(k)
        chunk = whole.at[core, here.chip_at(4 - dx, 4 - dy)]
        twin.post(1 + k, chunk, chunk, here.twin)
    yield
    twin.take(*range(1, 17))
    for mail in (twin, first, second, third):
        mail.close()


def update(block, state, grad):
    state = state + jnp.sum(grad * grad, axis=0, keepdims=True) * (1.0 / D)
    return block - ENTITY_RATE * grad / jnp.sqrt(state), state


def draw_share(x, drawn):
    drawn = jnp.where(drawn < 0, -1, (drawn + 4 * SHARE * x) & (ROWS - 1))
    picked = flag(lax.broadcasted_iota(i32, (ROWS, ROWS), 0) == drawn)
    return nt(jnp.full((8, ROWS), 1.0, bf16), picked) * (1.0 / NEG)


def line_up(edge, ids, r):
    owner = jnp.concatenate(
        [ids[m].astype(f32)[8 * r : 8 * r + 1, :] for m in range(MEMBERS)], axis=0
    )
    mine = owner == edge.astype(f32)
    before = flag(
        lax.broadcasted_iota(i32, (LANES, LANES), 0) < lax.broadcasted_iota(i32, (LANES, LANES), 1)
    )
    found = jnp.sum(jnp.where(mine, 1.0, 0.0), axis=1, keepdims=True)
    starts = [jnp.zeros((1, 1), f32)]
    for m in range(MEMBERS):
        starts.append(starts[-1] + found[m : m + 1, :])
    place = nn(flag(mine), before) + jnp.concatenate(starts[:MEMBERS], axis=0)
    rank = jnp.where(mine, place, -1.0).astype(i32)
    return rank, jnp.where(starts[MEMBERS] > ROOM, 1.0, 0.0)


def pick(x, rank, ids, r, source_hot, relation_hot, target):
    high, low = rank >> 7, rank & (SHARE - 1)
    as_row, as_column = jnp.zeros((32, SHARE), f32), jnp.zeros((SHARE, 32), f32)
    for m in range(MEMBERS):
        low_hot = flag(lax.broadcasted_iota(i32, (SHARE, LANES), 0) == low[m : m + 1, :])
        high_hot = lax.broadcasted_iota(i32, (8, LANES), 0) == high[m : m + 1, :]
        values = ids[m].astype(f32)[8 * r : 8 * r + 8]
        values = jnp.concatenate(
            [jnp.where(high_hot, values[f : f + 1, :], 0.0) for f in range(1, 5)], axis=0
        ).astype(bf16)
        as_row = as_row + nt(values, low_hot)
        as_column = as_column + nt(low_hot, values)
    blocks = range(ROOM // SHARE)
    s = jnp.concatenate([as_row[h : h + 1, :] for h in blocks], axis=1).astype(i32)
    k = jnp.concatenate([as_row[8 + h : 9 + h, :] for h in blocks], axis=1).astype(i32)
    source_hot[...] = flag(lax.broadcasted_iota(i32, (SHARE, ROOM), 0) == s - 1)
    relation_hot[...] = flag(lax.broadcasted_iota(i32, (NREL, ROOM), 0) == k)
    wanted = as_column.astype(i32)
    for h in blocks:
        t = ((wanted[:, 16 + h : 17 + h] + 4 * x) & 7) * SHARE + wanted[:, 24 + h : 25 + h]
        target[h * SHARE : (h + 1) * SHARE, :] = jnp.broadcast_to(t, (SHARE, SHARE))


def ask(left_low, both, source_hot, relation_hot, source, operator, query, query_t):
    source[...] = nn(left_low, source_hot[...])
    operator[...] = nn(both[...], jnp.concatenate([relation_hot[...], relation_hot[...]], axis=0))
    sr, si, kr, ki = source[:H], source[H:], operator[:H], operator[H:]
    asked = jnp.concatenate([sr * kr - si * ki, sr * ki + si * kr], axis=0).astype(bf16)
    query[...] = asked
    query_t[...] = asked.T


def weigh(half, rows, often, target, query_t, weight):
    lane = lax.broadcasted_iota(i32, (ROOM, SHARE), 1)
    for b in range(2):
        start = (4 * half + 2 * b) * SHARE
        scores = nn(query_t[...], rows[:, pl.ds(start, 2 * SHARE)])
        for j in range(2):
            block = pl.ds(start + j * SHARE, SHARE)
            chance = 0.5 * jnp.tanh(0.5 * scores[:, j * SHARE : (j + 1) * SHARE]) + 0.5
            hit = lane + (start + j * SHARE) == target[...]
            value = often[0:1, block] * chance - jnp.where(hit, 1.0 - chance, 0.0)
            weight[:, block] = value.astype(bf16)


def right_parts(half, query, weight, parts):
    for b in range(2):
        first = 4 * half + 2 * b
        wide = nn(query[...], weight[:, pl.ds(first * SHARE, 2 * SHARE)]).astype(bf16)
        parts[first], parts[first + 1] = wide[:, :SHARE], wide[:, SHARE:]


def train_kernel(
    *refs,
):
    fetched, loads = refs[18:29], refs[29]
    fetch = [
        pltpu.make_async_copy(given, taken, loads.at[i])
        for i, (given, taken) in enumerate(zip(refs[:11], fetched))
    ]
    train_rounds(fetch, *fetched, *refs[11:18], *refs[30:])


def train_rounds(
    fetch,
    left, left_state, right, right_state, relations, relation_state,
    source_ids, relation_ids, target_ids, sample_ids, counts,
    left_out, left_state_out, right_out, right_state_out, relations_out, relation_state_out, missed,
    wide, ids1, ids2, drawn1, drawn2, both, rows1, rows2, often1, often2,
    source_hot1, relation_hot1, target1, source_hot2, relation_hot2, target2,
    source, operator, query, query_t, weight, parts1, parts2, total, relation_sum, left_two, left_two_state,
    out_left, in_left, out_right, in_right, out_rows, in_rows, out_states, in_states,
    id_send, id_recv, id2_send, id2_recv, move_send, move_recv,
    spread1_send, spread1_recv, spread2_send, spread2_recv,
    *folds,
):
    fold1, fold2, reduction = folds[:6], folds[6:12], folds[12:]
    for i in (6, 7, 8, 10, 2, 9, 4, 0, 1, 3, 5):
        fetch[i].start()
    here = Place()
    pair, edge = here.pair, here.edge
    barrier = pltpu.get_barrier_semaphore()
    met = here.met()
    for device in met:
        pl.semaphore_signal(barrier, inc=1, device_id=device, device_id_type=MESH)

    wide[...] = jnp.full_like(wide, -1.0)
    for i in (6, 7, 8, 10):
        fetch[i].wait()
    slot = edge * SLOTS + lax.broadcasted_iota(i32, (1, SLOTS), 1)
    for r in range(2):
        s, k, t = (x[r : r + 1, :] for x in (source_ids, relation_ids, target_ids))
        owner = jnp.where(slot < counts[0:1, r : r + 1], s >> 7, -1)
        for row, value in enumerate((owner, (s & 127) + 1, k, t >> 7, t & 127)):
            wide[8 * r + row : 8 * r + row + 1, 0:SLOTS] = value.astype(f32)
    ids1[edge] = wide[...].astype(bf16)
    fetch[2].wait()
    rows1[:, columns(here.y)] = right[...].astype(bf16)
    pl.semaphore_wait(barrier, len(met))

    id_mail, id2_mail, moves = Mail(id_send, id_recv), Mail(id2_send, id2_recv), Mail(move_send, move_recv)
    ahead, behind = here.group(1), here.group(-1)
    gather = spread(here, rows1, Mail(spread1_send, spread1_recv))
    next(gather)
    for d, device in enumerate(here.peers):
        id_mail.post(d, ids1.at[edge], ids1.at[edge], device)
    next(gather)
    moves.post(0, ids1.at[edge], ids2.at[edge], ahead)
    fetch[9].wait()
    drawn1[...] = jnp.full_like(drawn1, -1)
    drawn1[:, 0:NEG] = sample_ids[...]
    for j in range(8):
        drawn2[0, j : j + 1, :] = drawn1[1:2, j * SHARE : (j + 1) * SHARE]
    moves.post(1, drawn2.at[0], drawn2.at[1], ahead)
    often1[...] = draw_share(here.x, drawn1[0:1, :])
    fetch[4].wait()
    high = relations[...].astype(bf16)
    both[:, 0:NREL] = high
    both[:, NREL:] = (relations[...] - high.astype(f32)).astype(bf16)
    next(gather)
    id_mail.take(*range(7))
    rank, late1 = line_up(edge, ids1, 0)
    next(gather)
    next(gather)
    pick(here.x, rank, ids1, 0, source_hot1, relation_hot1, target1)
    fetch[0].wait()
    ask(left[...].astype(bf16), both, source_hot1, relation_hot1, source, operator, query, query_t)
    moves.take(0)
    for d, device in enumerate(here.peers):
        id2_mail.post(d, ids2.at[edge], ids2.at[edge], device)
    next(gather)

    weigh(0, rows1, often1, target1, query_t, weight)
    right_parts(0, query, weight, parts1)
    folding = fold(here, parts1, total, *fold1)
    next(folding)
    next(gather, None)
    weigh(1, rows1, often1, target1, query_t, weight)
    right_parts(1, query, weight, parts1)
    next(folding)
    for i in (1, 3, 5):
        fetch[i].wait()
    grad = nt(rows1[...], weight[...])
    gr, gi, kr, ki = grad[:H], grad[H:], operator[:H], operator[H:]
    back = jnp.concatenate([gr * kr + gi * ki, gi * kr - gr * ki], axis=0).astype(bf16)
    left_sum = nt(back, source_hot1[...])
    block, state = update(left[...], left_state[...], left_sum)
    out_left[...] = block.astype(bf16)
    out_states[0] = jnp.broadcast_to(state, (8, SHARE))
    moves.post(2, out_left, in_left, here.group(2))
    moves.post(3, out_states.at[0], in_states.at[0], here.group(2))
    next(folding)
    sr, si = source[:H], source[H:]
    back = jnp.concatenate([gr * sr + gi * si, gi * sr - gr * si], axis=0).astype(bf16)
    for c in range(2):
        relation_sum[c] = nt(back, relation_hot1[c * SHARE : (c + 1) * SHARE, :])
    next(folding)
    id2_mail.take(*range(7))
    rank, late2 = line_up(edge, ids2, 1)
    pick(here.x, rank, ids2, 1, source_hot2, relation_hot2, target2)
    moves.take(1)
    often2[...] = draw_share(
        here.x, jnp.concatenate([drawn2[1, j : j + 1, :] for j in range(8)], axis=1)
    )
    next(folding, None)
    right_two, right_two_state = update(right[...], right_state[...], total[...])
    rows2[:, columns(here.y)] = right_two.astype(bf16)
    gather = spread(here, rows2, Mail(spread2_send, spread2_recv))
    next(gather)
    next(gather)
    moves.take(2, 3)
    left_two[...] = in_left[...].astype(f32)
    left_two_state[...] = in_states[0, 0:1, :]
    ask(in_left[...], both, source_hot2, relation_hot2, source, operator, query, query_t)
    for _ in range(4):
        next(gather)

    weigh(0, rows2, often2, target2, query_t, weight)
    right_parts(0, query, weight, parts2)
    folding = fold(here, parts2, total, *fold2)
    next(folding)
    half = 4 * SHARE
    grad = nt(rows2[:, :half], weight[:, :half])
    next(gather, None)
    weigh(1, rows2, often2, target2, query_t, weight)
    grad = grad + nt(rows2[:, half:], weight[:, half:])
    gr, gi, sr, si = grad[:H], grad[H:], source[:H], source[H:]
    back = jnp.concatenate([gr * sr + gi * si, gi * sr - gr * si], axis=0).astype(bf16)
    last = jnp.broadcast_to(late1 + late2, (512 - D, SHARE))
    share, whole = reduction[0], reduction[5]
    reducing = reduce_all(here, *reduction)
    for c in (1 - here.core, here.core):
        hot = relation_hot2[columns(c), :]
        full = jnp.concatenate([relation_sum[c] + nt(back, hot), last], axis=0)
        share[c] = full.reshape(16, 32, SHARE).astype(bf16)
        if c is not here.core:
            next(reducing)
    right_parts(1, query, weight, parts2)
    next(reducing)
    next(folding)
    kr, ki = operator[:H], operator[H:]
    back = jnp.concatenate([gr * kr + gi * ki, gi * kr - gr * ki], axis=0).astype(bf16)
    left_sum = nt(back, source_hot2[...])
    block, state = update(left_two[...], left_two_state[...], left_sum)
    out_rows[0] = block.astype(bf16)
    out_states[1] = jnp.broadcast_to(state, (8, SHARE))
    next(folding)
    next(reducing)
    moves.post(4, out_rows.at[0], in_rows.at[0], behind)
    moves.post(5, out_states.at[1], in_states.at[1], behind)
    next(folding)
    next(reducing)
    next(folding, None)
    block, state = update(right_two, right_two_state, total[...])
    out_rows[1] = block.astype(bf16)
    out_states[2] = jnp.broadcast_to(state, (8, SHARE))
    moves.post(6, out_rows.at[1], in_rows.at[1], behind)
    moves.post(7, out_states.at[2], in_states.at[2], behind)
    moves.take(4, 5)
    left_out[...] = in_rows[0].astype(f32)
    left_state_out[...] = in_states[1, 0:1, :]
    next(reducing)

    def relation_update(c):
        half = columns(c)
        grad = whole[c].reshape(512, SHARE)[:D].astype(f32)
        state = relation_state[:, half] + grad * grad
        relation_state_out[:, half] = state
        relations_out[:, half] = relations[:, half] - RELATION_RATE * grad / jnp.sqrt(state)

    relation_update(here.core)
    missed[...] = whole[here.core].reshape(512, SHARE)[D : D + 16].astype(f32)[0:1, 0:1].astype(i32)
    moves.take(6, 7)
    right_out[...] = in_rows[1].astype(f32)
    right_state_out[...] = in_states[2, 0:1, :]
    next(reducing, None)
    relation_update(1 - here.core)
    for mail in (id_mail, id2_mail, moves):
        mail.close()


def train(*args):
    table = jax.ShapeDtypeStruct((D, NREL), f32)
    block = jax.ShapeDtypeStruct((D, SHARE), f32)
    row = jax.ShapeDtypeStruct((1, SHARE), f32)
    vmem = pltpu.VMEM
    low = vmem((D, SHARE), bf16)
    hots = [vmem((SHARE, ROOM), bf16), vmem((NREL, ROOM), bf16), vmem((ROOM, SHARE), i32)]
    return pl.pallas_call(
        train_kernel,
        out_shape=(block, row, block, row, table, table, jax.ShapeDtypeStruct((1, 1), i32)),
        in_specs=[pl.BlockSpec(memory_space=pl.ANY)] * 11,
        out_specs=(VMEM,) * 7,
        scratch_shapes=[
            *(vmem(x.shape, x.dtype) for x in args), DMA((11,)),
            vmem((16, LANES), f32),
            vmem((MEMBERS, 16, LANES), bf16), vmem((MEMBERS, 16, LANES), bf16),
            vmem((2, ROWS), i32), vmem((2, 8, SHARE), i32),
            vmem((D, 2 * NREL), bf16),
            vmem((D, ROWS), bf16), vmem((D, ROWS), bf16),
            vmem((8, ROWS), f32), vmem((8, ROWS), f32),
            *hots, *hots,
            vmem((D, ROOM), f32), vmem((D, ROOM), f32),
            vmem((D, ROOM), bf16), vmem((ROOM, D), bf16), vmem((ROOM, ROWS), bf16),
            vmem((MEMBERS, D, SHARE), bf16), vmem((MEMBERS, D, SHARE), bf16),
            vmem((D, SHARE), f32), vmem((2, D, SHARE), f32),
            vmem((D, SHARE), f32), vmem((1, SHARE), f32),
            low, low, low, low, vmem((2, D, SHARE), bf16), vmem((2, D, SHARE), bf16),
            vmem((3, 8, SHARE), f32), vmem((3, 8, SHARE), f32),
            DMA((7,)), DMA((7,)), DMA((7,)), DMA((7,)), DMA((8,)), DMA((8,)),
            DMA((14,)), DMA((14,)), DMA((14,)), DMA((14,)),
            *fold_scratch(), *fold_scratch(), *reduce_scratch(),
        ],
        compiler_params=pltpu.CompilerParams(
            collective_id=1, has_side_effects=True, vmem_limit_bytes=56 * 2**20
        ),
        name="train_two_rounds",
    )(*args)


def settle_kernel(*refs):
    for given, out in zip(refs[:6], refs[6:]):
        out[...] = given[...]


def settle(done):
    left, left_sums, right, right_sums, table, table_state = done
    flat = (left.T, left_sums.reshape(1, SHARE), right.T, right_sums.reshape(1, SHARE), table.T, table_state.T)
    left, left_sums, right, right_sums, table, table_state = pl.pallas_call(
        settle_kernel,
        out_shape=tuple(jax.ShapeDtypeStruct(x.shape, x.dtype) for x in flat),
        in_specs=[VMEM] * 6,
        out_specs=(VMEM,) * 6,
        name="settle",
    )(*flat)
    return (
        left.T, left_sums.reshape(SHARE), right.T, right_sums.reshape(SHARE), table.T, table_state.T,
    )


def body(
    left_block, left_state, right_block, right_state, relations, relation_state,
    source_ids, relation_ids, target_ids, sample_ids, bucket_counts,
):
    left, left_sums, right, right_sums, table, table_state, missed = train(
        left_block.T, left_state.reshape(1, SHARE), right_block.T, right_state.reshape(1, SHARE),
        relations.T, relation_state.T,
        source_ids, relation_ids, target_ids, sample_ids, bucket_counts.T,
    )
    fast = (
        left.T, left_sums.reshape(SHARE), right.T, right_sums.reshape(SHARE), table.T, table_state.T,
    )
    done = lax.cond(
        missed[0, 0] > 0,
        lambda *args: any_spread(*args[6:]),
        lambda *args: args[:6],
        *fast,
        left_block, left_state, right_block, right_state, relations, relation_state,
        source_ids, relation_ids, target_ids, sample_ids, bucket_counts,
    )
    return settle(done)


def solution(mesh):
    block, row = P(("pair", "edge"), None), P(("pair", "edge"))
    ids, group = P(None, ("pair", "edge")), P(None, "pair")
    return jax.shard_map(
        body,
        mesh=mesh,
        in_specs=(block, row, block, row, P(), P(), ids, ids, ids, group, group),
        out_specs=(block, row, block, row, P(), P()),
        check_vma=False,
    )
```
